32 devices in a mesh: lon: 8 (over y, x, core), lat: 4 (over z).
Axes of the slice: x: 2, y: 2, z: 4, core: 2. Of those that a mesh axis runs over, the one named last changes fastest.
Arguments:
- velocity: float32 [2, 256, 2048], P(None, 'lat', 'lon'), may hold values from -4 to 4
- stress: float32 [3, 256, 2048], P(None, 'lat', 'lon'), may hold values from -4 to 4
- thickness: float32 [6, 256, 2048], P(None, 'lat', 'lon'), may hold values from 0.1 to 5
- concentration: float32 [6, 256, 2048], P(None, 'lat', 'lon'), may hold values from 0.02 to 0.16
- land_mask: int32 [256, 2048], P('lat', 'lon'), may hold values 0 or 1
- covered: int32 [4, 16], P('lat'), may hold values 0 or 1
- ocean_current: bfloat16 [2, 2, 256, 2048], P(None, None, 'lat', 'lon'), may hold values from -6 to 6
- wind_stress: bfloat16 [2, 2, 256, 2048], P(None, None, 'lat', 'lon'), may hold values from -6 to 6
- regrid_weights: bfloat16 [256, 128], P('lat'), may hold values from -0.5 to 0.5
- tile_offset: int32 [256], P('lat'), may hold values from -1 to 1, as said below
Outputs:
- velocity_out: float32 [2, 256, 2048], P(None, 'lat', 'lon')
- stress_out: float32 [3, 256, 2048], P(None, 'lat', 'lon')
- thickness_out: float32 [6, 256, 2048], P(None, 'lat', 'lon')
The draws below stay inside these ranges and needn't reach their ends.
Inputs may be any that keep to these rules, and one draw needn't show every extreme that they name: `tile_offset`: never 0; rows of the first tile have +1 and rows of the last tile have -1, so every row reads a tile of the grid.
All inputs are finite; a program needn't handle non-finite values. No bound on the sum of `land_mask` or of `covered` on one device may be relied on, other than what follows from the above.
Results may differ from the reference program's by a relative error of at most 0.0015.
Values may be sent and summed in bfloat16 or wider, within the bound.
No kernel may reach another device: no remote copies, remote signals or barrier semaphores. Data moves between devices by JAX's collectives and lax.ppermute only.
A program may use at most 64 MiB of HBM per device.

```python
import math
import jax
import jax.numpy as jnp
from jax import lax

NCAT = 6
CY = 64
BLK = 128
SUB = 4
WIN = 2
NY = 256
NX = 2048
NT = 4
NBX = 16


def draw_tile_offset(key, part):
    number = jnp.arange(NY)
    picks = 2 * jax.random.randint(key, (NY,), 0, 2) - 1
    return jnp.where(number < CY, 1, jnp.where(number >= NY - CY, -1, picks)).astype(jnp.int32)


def place_ends(result, stream_key, least, high):
    spot = [jax.random.randint(jax.random.fold_in(stream_key, axis), (), 0, length) for axis, length in enumerate(result.shape)]
    main_axis = result.shape.index(max(result.shape))
    beside = spot[:main_axis] + [(spot[main_axis] + 1) % result.shape[main_axis]] + spot[main_axis + 1:]
    return result.at[tuple(spot)].set(least).at[tuple(beside)].set(high)


def block_levels(stream_key, dims, split, least, high):
    factor_of, own = 1.0, jax.random.fold_in(stream_key, 6)
    for position, parts in split:
        draws = jnp.exp(jax.random.uniform(jax.random.fold_in(own, position), (parts,), jnp.float32, least / len(split), high / len(split)))
        factor_of = factor_of * jnp.repeat(draws, dims[position] // parts).reshape([-1 if axis == position else 1 for axis in range(len(dims))])
    return factor_of


def noise(key, shape, deviation, limit, pieces=(), dtype=jnp.bfloat16):
    result = deviation * jax.random.normal(key, shape, jnp.float32)
    if pieces:
        result = result * block_levels(key, shape, pieces, -0.22, 0.18)
    return jnp.clip(result, -limit, limit).astype(dtype)


def setup_inputs(seed: int = 0) -> dict:
    key_list = jax.random.split(jax.random.key(seed), 11)
    return {
        "velocity": noise(key_list[0], (2, NY, NX), 0.5, 4.0, ((1, 4), (2, 8)), jnp.float32),
        "stress": noise(key_list[1], (3, NY, NX), 0.5, 4.0, ((1, 4), (2, 8)), jnp.float32),
        "thickness": jnp.clip(jnp.exp(math.log(5.0) - 3.912023 * jax.random.uniform(key_list[2], (NCAT, NY, NX), jnp.float32) ** block_levels(key_list[2], (NCAT, NY, NX), ((1, 4), (2, 8)), -0.2, 0.2)), 0.1, 5.0),
        "concentration": jnp.clip(0.02 + 0.14 * jax.random.uniform(key_list[3], (NCAT, NY, NX), jnp.float32) ** block_levels(key_list[3], (NCAT, NY, NX), ((1, 4), (2, 8)), -0.2, 0.2), 0.02, 0.16),
        "land_mask": place_ends((jax.random.randint(key_list[4], (NY, NX), 0, 8) < 7).astype(jnp.int32), jax.random.fold_in(key_list[4], 1), 0, 1),
        "covered": place_ends((jax.random.randint(key_list[5], (NT, NBX), 0, 2) < 1).astype(jnp.int32), jax.random.fold_in(key_list[5], 1), 0, 1),
        "ocean_current": noise(key_list[6], (WIN, 2, NY, NX), 1.0, 6.0, ((2, 4), (3, 8))),
        "wind_stress": noise(key_list[7], (WIN, 2, NY, NX), 1.0, 6.0, ((2, 4), (3, 8))),
        "regrid_weights": noise(key_list[8], (NY, 2 * CY), (2 * CY) ** -0.5, 0.5, ((0, 4),)),
        "tile_offset": draw_tile_offset(jax.random.fold_in(key_list[10], 71), 0),
    }


relax_rate = 0.5
strain_offset = 0.5
time_step = 0.5
water_drag = 1.0
growth_rate = 0.3
mixing_rate = 0.3

def toward_east(field):
    return jnp.roll(field, -1, axis=-1)

def toward_west(field):
    return jnp.roll(field, 1, axis=-1)

def toward_north(field):
    zero_row = jnp.zeros_like(field[..., :1, :])
    return jnp.concatenate([field[..., 1:, :], zero_row], axis=-2)

def toward_south(field):
    zero_row = jnp.zeros_like(field[..., :1, :])
    return jnp.concatenate([zero_row, field[..., :-1, :]], axis=-2)

def growth(thick_now, conc_now):
    ice_area = lax.optimization_barrier(jnp.sum(conc_now, axis=0))
    mean_thick = lax.optimization_barrier(jnp.sum(conc_now * thick_now, axis=0)) / ice_area
    return thick_now + growth_rate / (0.5 + thick_now) + mixing_rate * (mean_thick - thick_now)

def forcing(thick_now, conc_now):
    volume = lax.optimization_barrier(jnp.sum(conc_now * thick_now, axis=0))
    ice_area = lax.optimization_barrier(jnp.sum(conc_now, axis=0))
    strength = volume * jnp.exp(-2.0 * (1.0 - ice_area))
    return (strength, volume + 0.5)

def new_stress(east_u, west_u, north_u, south_u, east_v, west_v, north_v, south_v, stresses, strength, open_mask):
    stretch_x = (east_u - west_u) / 2.0
    stretch_y = (north_v - south_v) / 2.0
    shear_half = (north_u - south_u + (east_v - west_v)) / 4.0
    divergence = stretch_x + stretch_y
    tension = stretch_x - stretch_y
    shearing = 2.0 * shear_half
    deformation = jnp.sqrt(divergence * divergence + (tension * tension + shearing * shearing) / 4.0 + strain_offset * strain_offset)
    bulk_stress = (stresses[0] + relax_rate * strength * (divergence / deformation - 1.0)) / (1.0 + relax_rate) * open_mask
    tension_stress = (stresses[1] + relax_rate * strength * tension / (4.0 * deformation)) / (1.0 + relax_rate) * open_mask
    shear_stress = (stresses[2] + relax_rate * strength * shearing / (8.0 * deformation)) / (1.0 + relax_rate) * open_mask
    return jnp.stack([bulk_stress, tension_stress, shear_stress])

def new_velocity(sxx_east, sxx_west, syy_north, syy_south, sxy_east, sxy_west, sxy_north, sxy_south, velocity_now, ice_mass, current, wind_now, open_mask):
    force_x = (sxx_east - sxx_west) / 2.0 + (sxy_north - sxy_south) / 2.0
    force_y = (sxy_east - sxy_west) / 2.0 + (syy_north - syy_south) / 2.0
    damping = 1.0 + time_step * water_drag / ice_mass
    u = (velocity_now[0] + time_step * (force_x + wind_now[0] + water_drag * current[0]) / ice_mass) / damping * open_mask
    v = (velocity_now[1] + time_step * (force_y + wind_now[1] + water_drag * current[1]) / ice_mass) / damping * open_mask
    return jnp.stack([u, v])

def reference(velocity, stress, thickness, concentration, land_mask, covered, ocean_current, wind_stress, regrid_weights, tile_offset):
    open_mask = land_mask.astype(jnp.float32)
    covered_cells = jnp.repeat(jnp.repeat(covered, CY, axis=0), BLK, axis=1) > 0
    ocean_tiles = ocean_current.astype(jnp.float32).reshape(WIN, 2, NT, CY, NX)
    numbers = jnp.arange(NT).astype(jnp.int32)
    upper_index = jnp.clip(numbers + 1, 0, NT - 1).astype(jnp.int32)
    lower_index = jnp.clip(numbers - 1, 0, NT - 1).astype(jnp.int32)
    upper_tiles = jnp.take(ocean_tiles, upper_index, axis=2)
    lower_tiles = jnp.take(ocean_tiles, lower_index, axis=2)
    weights = regrid_weights.astype(jnp.float32).reshape(NT, CY, 2 * CY)
    currents = jnp.einsum('tij,wctjx->wctix', weights[:, :, :CY], ocean_tiles, precision=lax.Precision.HIGHEST)
    from_upper = jnp.einsum('tij,wctjx->wctix', weights[:, :, CY:], upper_tiles, precision=lax.Precision.HIGHEST)
    from_lower = jnp.einsum('tij,wctjx->wctix', weights[:, :, CY:], lower_tiles, precision=lax.Precision.HIGHEST)
    upward = (tile_offset.reshape(NT, CY) > 0)[None, None, :, :, None]
    currents = currents + jnp.where(upward, from_upper, from_lower)
    currents = currents.reshape(WIN, 2, NY, NX)
    thick_now = thickness
    velocity_now = velocity
    stresses = stress
    for window in range(WIN):
        thick_now = jnp.where(covered_cells, growth(thick_now, concentration), thick_now)
        strength, ice_mass = forcing(thick_now, concentration)
        wind_now = wind_stress[window].astype(jnp.float32)
        current = currents[window]
        for substep in range(SUB):
            u = velocity_now[0]
            v = velocity_now[1]
            stresses = new_stress(toward_east(u), toward_west(u), toward_north(u), toward_south(u), toward_east(v), toward_west(v), toward_north(v), toward_south(v), stresses, strength, open_mask)
            sigma_xx = (stresses[0] + stresses[1]) / 2.0
            sigma_yy = (stresses[0] - stresses[1]) / 2.0
            sigma_xy = stresses[2]
            velocity_now = new_velocity(toward_east(sigma_xx), toward_west(sigma_xx), toward_north(sigma_yy), toward_south(sigma_yy), toward_east(sigma_xy), toward_west(sigma_xy), toward_north(sigma_xy), toward_south(sigma_xy), velocity_now, ice_mass, current, wind_now, open_mask)
    return (velocity_now, stresses, thick_now)
```

```python
import jax
import jax.numpy as jnp
from jax import lax
from jax.experimental import pallas as pl
from jax.experimental.pallas import tpu as pltpu
from jax.sharding import PartitionSpec as P

BLK = 128
SUB = 4
LANES = 128
PAD = 8
STATE = 5
COEF = 4
VMEM_LIMIT = 16 * 1024 * 1024

growth_rate = 0.3
mixing_rate = 0.3


def total(terms):
    result = terms[0]
    for term in terms[1:]:
        result = result + term
    return result


def growth_kernel(covered_ref, thick_ref, conc_ref, mask_ref, thick_out_ref, coef_ref):
    cats, rows, cols = thick_ref.shape
    blocks = cols // BLK
    first = lax.axis_index("lon") * blocks
    step = 16
    for block in range(blocks):
        live = covered_ref[0, first + block] > 0
        lanes = slice(block * BLK, (block + 1) * BLK)
        for row in range(0, rows, step):
            at = slice(row, row + step)
            conc = [conc_ref[c, at, lanes] for c in range(cats)]
            thick = [thick_ref[c, at, lanes] for c in range(cats)]
            mask = mask_ref[at, lanes].astype(jnp.float32)
            area = total(conc)
            inverse = 1.0 / area
            factor = jnp.exp(-2.0 * (1.0 - area)) * (mask * (1.0 / 3.0))
            half = 0.5 * mask
            volume = total([c * h for c, h in zip(conc, thick)])
            for window in range(coef_ref.shape[0] // 2):
                mean = volume * inverse
                grown = [h + growth_rate / (0.5 + h) + mixing_rate * (mean - h) for h in thick]
                thick = [jnp.where(live, g, h) for g, h in zip(grown, thick)]
                volume = total([c * h for c, h in zip(conc, thick)])
                coef_ref[2 * window, at, lanes] = volume * factor
                coef_ref[2 * window + 1, at, lanes] = half / (volume + 1.0)
            for c in range(cats):
                thick_out_ref[c, at, lanes] = thick[c]


def slots(depth):
    return LANES // depth


def message_plan(margin, windows):
    plan = [(f, margin) for f in range(STATE)]
    for window in range(windows):
        plan += [(STATE + COEF * window + k, margin - 2 * SUB * window) for k in range(COEF)]
    return plan


def pack_kernel(
    offset_ref,
    weights_ref,
    own_ref,
    lower_ref,
    upper_ref,
    wind_ref,
    coef_ref,
    velocity_ref,
    stress_ref,
    mask_ref,
    fields_ref,
    east_ref,
    west_ref,
    north_ref,
    south_ref,
):
    windows, _, rows, cols = own_ref.shape
    margin = 2 * SUB * windows
    up = offset_ref[...] > 0
    square = (rows, rows)
    diagonal = lax.broadcasted_iota(jnp.int32, square, 0) == lax.broadcasted_iota(
        jnp.int32, square, 1
    )
    upward = jnp.where(diagonal & up, 1.0, 0.0).astype(jnp.bfloat16)
    downward = jnp.where(diagonal & jnp.logical_not(up), 1.0, 0.0).astype(jnp.bfloat16)
    own_weights = weights_ref[:, :rows]
    side = weights_ref[:, rows:]

    def dot(a, b):
        return jnp.dot(a, b, preferred_element_type=jnp.float32)

    up_weights = dot(upward, side).astype(jnp.bfloat16)
    down_weights = dot(downward, side).astype(jnp.bfloat16)
    mask = mask_ref[...].astype(jnp.float32)
    fields_ref[0] = velocity_ref[0]
    fields_ref[1] = velocity_ref[1]
    fields_ref[2] = (stress_ref[0] + stress_ref[1]) * mask
    fields_ref[3] = (stress_ref[0] - stress_ref[1]) * mask
    fields_ref[4] = (stress_ref[2] + stress_ref[2]) * mask
    for w in range(windows):
        base = STATE + COEF * w
        fields_ref[base] = coef_ref[2 * w]
        b = coef_ref[2 * w + 1]
        fields_ref[base + 1] = b
        for k in range(2):
            current = (
                dot(own_weights, own_ref[w, k])
                + dot(up_weights, upper_ref[w, k])
                + dot(down_weights, lower_ref[w, k])
            )
            fields_ref[base + 2 + k] = b * (wind_ref[w, k].astype(jnp.float32) + current)

    count = fields_ref.shape[0]
    per = slots(margin)
    lane = lax.broadcasted_iota(jnp.int32, (rows, LANES), 1) // margin
    for group in range(-(-count // per)):
        eastward = jnp.zeros((rows, LANES), jnp.float32)
        westward = jnp.zeros((rows, LANES), jnp.float32)
        for slot in range(min(per, count - group * per)):
            field = group * per + slot
            last = fields_ref[field, :, cols - LANES :]
            leading = fields_ref[field, :, :LANES]
            here = lane == slot
            shift = slot * margin
            last = pltpu.roll(last, (shift + margin) % LANES, 1)
            leading = pltpu.roll(leading, shift, 1) if shift else leading
            eastward = jnp.where(here, last, eastward)
            westward = jnp.where(here, leading, westward)
        lanes = slice(group * LANES, (group + 1) * LANES)
        east_ref[:, lanes] = eastward.astype(jnp.bfloat16)
        west_ref[:, lanes] = westward.astype(jnp.bfloat16)

    row, held_north, held_south, held = 0, [], [], 0
    for field, depth in message_plan(margin, windows):
        held_north.append(fields_ref[field, rows - depth :, :])
        held_south.append(fields_ref[field, :depth, :])
        held += depth
        if held % 16 == 0:
            join = (lambda x: x[0] if len(x) == 1 else jnp.concatenate(x, axis=0))
            north_ref[row : row + held] = join(held_north).astype(jnp.bfloat16)
            south_ref[row : row + held] = join(held_south).astype(jnp.bfloat16)
            row, held_north, held_south, held = row + held, [], [], 0
    tail = north_ref.shape[0] - row
    north_ref[row:] = jnp.zeros((tail, cols), jnp.bfloat16)
    south_ref[row:] = jnp.zeros((tail, cols), jnp.bfloat16)


def dynamics_kernel(
    fields_ref,
    east_ref,
    west_ref,
    north_ref,
    south_ref,
    velocity_ref,
    stress_ref,
    state,
    strength,
    keep,
    push,
    force,
):
    count, rows, cols = fields_ref.shape
    windows = strength.shape[0]
    margin = 2 * SUB * windows
    own_tiles = cols // LANES
    tiles = own_tiles + 1
    per = slots(margin)
    top = PAD + margin
    bottom = top + rows
    lane = lax.broadcasted_iota(jnp.int32, (8, LANES), 1)

    def place(field, tile, row, value):
        at = slice(row, row + value.shape[0])
        if field < STATE:
            state[field, tile, at, :] = value
            return
        window, kind = divmod(field - STATE, COEF)
        if kind == 0:
            strength[window, tile, at, :] = value
        elif kind == 1:
            push[window, tile, at, :] = value
            keep[window, tile, at, :] = jnp.where(value > 0.0, 1.0 - value, 0.0)
        else:
            force[window, kind - 2, tile, at, :] = value

    zero = jnp.zeros((PAD, LANES), jnp.float32)
    for tile in range(tiles):
        for field in range(STATE):
            state[field, tile, 0:PAD, :] = zero
            state[field, tile, bottom + margin : bottom + margin + PAD, :] = zero

    def side_tile(field, east, west, row, depth, skip):
        group, slot = divmod(field, per)
        lanes = slice(group * LANES, (group + 1) * LANES)
        from_east = east[:, lanes].astype(jnp.float32)
        from_west = west[:, lanes].astype(jnp.float32)
        shift = slot * margin
        if shift:
            from_east = pltpu.roll(from_east, LANES - shift, 1)
        back = (LANES - margin - shift) % LANES
        if back:
            from_west = pltpu.roll(from_west, back, 1)
        wide = lax.broadcasted_iota(jnp.int32, from_east.shape, 1)
        value = jnp.where(
            wide < margin, from_east, jnp.where(wide >= LANES - margin, from_west, 0.0)
        )
        place(field, own_tiles, row, value[skip : skip + depth])

    plan = message_plan(margin, windows)
    corner = sum(depth for _, depth in plan)
    for field in range(count):
        for tile in range(own_tiles):
            lanes = slice(tile * LANES, (tile + 1) * LANES)
            place(field, tile, top, fields_ref[field, :, lanes])
        side_tile(field, east_ref[...], west_ref[...], top, rows, 0)
    for ref, is_north in ((north_ref, True), (south_ref, False)):
        row = 0
        east = ref[corner : corner + margin]
        west = ref[corner + margin : corner + 2 * margin]
        for field, depth in plan:
            begin = row // 16 * 16
            value = ref[begin : begin + 16].astype(jnp.float32)
            value = value[row - begin : row - begin + depth]
            to = bottom if is_north else top - depth
            for tile in range(own_tiles):
                lanes = slice(tile * LANES, (tile + 1) * LANES)
                place(field, tile, to, value[:, lanes])
            side_tile(field, east, west, to, depth, 0 if is_north else margin - depth)
            row += depth

    first_lane = lane == 0
    last_lane = lane == LANES - 1

    def across(values):
        ahead = [pltpu.roll(x, LANES - 1, 1) for x in values]
        behind = [pltpu.roll(x, 1, 1) for x in values]
        return [
            jnp.where(last_lane, ahead[(j + 1) % tiles], ahead[j])
            - jnp.where(first_lane, behind[j - 1], behind[j])
            for j in range(tiles)
        ]

    def along(field, tile, row):
        return state[field, tile, row + 1 : row + 9, :] - state[field, tile, row - 1 : row + 7, :]

    every = range(tiles)
    for window in range(windows):
        spare = 2 * SUB * window
        row_list = range(top - margin + spare, bottom + margin - spare, 8)

        def subcycle(_, carry):
            for row in row_list:
                at = slice(row, row + 8)
                u_x = across([state[0, j, at, :] for j in every])
                v_x = across([state[1, j, at, :] for j in every])
                for j in every:
                    u_y = along(0, j, row)
                    v_y = along(1, j, row)
                    shear = u_y + v_x[j]
                    spread = u_x[j] + v_y
                    tension = u_x[j] - v_y
                    tension4 = tension * 0.25
                    shear4 = shear * 0.25
                    squares = spread * spread + tension * tension4 + (shear * shear4 + 1.0)
                    k = strength[window, j, at, :]
                    kr = k * lax.rsqrt(squares)
                    state[2, j, at, :] = state[2, j, at, :] * (2.0 / 3.0) + (
                        kr * (spread + tension4) - k
                    )
                    state[3, j, at, :] = state[3, j, at, :] * (2.0 / 3.0) + (
                        kr * (spread - tension4) - k
                    )
                    state[4, j, at, :] = state[4, j, at, :] * (2.0 / 3.0) + kr * shear4
            for row in row_list:
                at = slice(row, row + 8)
                p_x = across([state[2, j, at, :] for j in every])
                t_x = across([state[4, j, at, :] for j in every])
                for j in every:
                    b = push[window, j, at, :] * 0.25
                    a = keep[window, j, at, :]
                    state[0, j, at, :] = (
                        a * state[0, j, at, :]
                        + b * (p_x[j] + along(4, j, row))
                        + force[window, 0, j, at, :]
                    )
                    state[1, j, at, :] = (
                        a * state[1, j, at, :]
                        + b * (t_x[j] + along(3, j, row))
                        + force[window, 1, j, at, :]
                    )
            return carry

        lax.fori_loop(0, SUB, subcycle, 0)

    for tile in range(own_tiles):
        lanes = slice(tile * LANES, (tile + 1) * LANES)
        for row in range(0, rows, 8):
            at = slice(row, row + 8)
            to = slice(top + row, top + row + 8)
            velocity_ref[0, at, lanes] = state[0, tile, to, :]
            velocity_ref[1, at, lanes] = state[1, tile, to, :]
            p = state[2, tile, to, :]
            q = state[3, tile, to, :]
            stress_ref[0, at, lanes] = (p + q) * 0.5
            stress_ref[1, at, lanes] = (p - q) * 0.5
            stress_ref[2, at, lanes] = state[4, tile, to, :] * 0.5


def params():
    return pltpu.CompilerParams(vmem_limit_bytes=VMEM_LIMIT)


def shift_pairs(axis, step, wrap):
    n = lax.axis_size(axis)
    return [(i, (i + step) % n) for i in range(n) if wrap or 0 <= i + step < n]


def shape(dims, dtype=jnp.float32):
    return jax.ShapeDtypeStruct(dims, dtype)


def local(
    velocity,
    stress,
    thickness,
    concentration,
    land_mask,
    covered,
    ocean_current,
    wind_stress,
    regrid_weights,
    tile_offset,
):
    _, rows, cols = velocity.shape
    windows = wind_stress.shape[0]
    margin = 2 * SUB * windows
    count = STATE + COEF * windows
    tiles = cols // LANES + 1

    lower = lax.ppermute(ocean_current, "lat", shift_pairs("lat", 1, False))
    upper = lax.ppermute(ocean_current, "lat", shift_pairs("lat", -1, False))

    whole = pl.BlockSpec(memory_space=pltpu.VMEM)
    thick_out, coef = pl.pallas_call(
        growth_kernel,
        out_shape=(shape(thickness.shape), shape((2 * windows, rows, cols))),
        in_specs=[pl.BlockSpec(memory_space=pltpu.SMEM)] + [whole] * 3,
        out_specs=(whole, whole),
        compiler_params=params(),
        cost_estimate=pl.CostEstimate(
            flops=100 * thickness.size, bytes_accessed=12 * thickness.size, transcendentals=0
        ),
        name="growth",
    )(covered, thickness, concentration, land_mask)

    plan = message_plan(margin, windows)
    body = sum(depth for _, depth in plan)
    packed = -(-count // slots(margin)) * LANES
    bf16 = jnp.bfloat16
    fields, eastward, westward, northward, southward = pl.pallas_call(
        pack_kernel,
        out_shape=(
            shape((count, rows, cols)),
            shape((rows, packed), bf16),
            shape((rows, packed), bf16),
            shape((body + 2 * margin, cols), bf16),
            shape((body + 2 * margin, cols), bf16),
        ),
        in_specs=[whole] * 10,
        out_specs=(whole,) * 5,
        compiler_params=params(),
        name="pack",
    )(
        tile_offset.reshape(1, rows),
        regrid_weights,
        ocean_current,
        lower,
        upper,
        wind_stress,
        coef,
        velocity,
        stress,
        land_mask,
    )

    from_west = lax.ppermute(eastward, "lon", shift_pairs("lon", 1, True))
    from_east = lax.ppermute(westward, "lon", shift_pairs("lon", -1, True))
    for number, side in enumerate((from_east, from_west)):
        at = body + number * margin
        northward = northward.at[at : at + margin, :packed].set(side[rows - margin :])
        southward = southward.at[at : at + margin, :packed].set(side[:margin])
    from_south = lax.ppermute(northward, "lat", shift_pairs("lat", 1, False))
    from_north = lax.ppermute(southward, "lat", shift_pairs("lat", -1, False))

    height = rows + 2 * margin + 2 * PAD

    def scratch(*lead):
        return pltpu.VMEM((*lead, tiles, height, LANES), jnp.float32)

    velocity_out, stress_out = pl.pallas_call(
        dynamics_kernel,
        out_shape=(shape(velocity.shape), shape(stress.shape)),
        in_specs=[whole] * 5,
        out_specs=(whole, whole),
        scratch_shapes=[
            scratch(STATE),
            scratch(windows),
            scratch(windows),
            scratch(windows),
            scratch(windows, 2),
        ],
        compiler_params=params(),
        name="dynamics",
    )(fields, from_east, from_west, from_north, from_south)
    return (velocity_out, stress_out, thick_out)


def solution(mesh):
    return jax.shard_map(
        local,
        mesh=mesh,
        in_specs=(
            P(None, "lat", "lon"),
            P(None, "lat", "lon"),
            P(None, "lat", "lon"),
            P(None, "lat", "lon"),
            P("lat", "lon"),
            P("lat", None),
            P(None, None, "lat", "lon"),
            P(None, None, "lat", "lon"),
            P("lat", None),
            P("lat"),
        ),
        out_specs=(P(None, "lat", "lon"), P(None, "lat", "lon"), P(None, "lat", "lon")),
        check_vma=False,
    )
```

```python
import functools

import jax
import jax.numpy as jnp
from jax import lax
from jax.experimental import pallas as pl
from jax.experimental.pallas import tpu as pltpu
from jax.sharding import PartitionSpec as P

BLK = 128
SUB = 4
LANES = 128
GROUP = 16
PAD = 8
STATE = 5
VMEM_LIMIT = 16 * 1024 * 1024

growth_rate = 0.3
mixing_rate = 0.3


def total(terms):
    result = terms[0]
    for term in terms[1:]:
        result = result + term
    return result


def field_depths(margin, windows):
    depths = [margin] * STATE
    for copies in (2, 2):
        for window in range(windows):
            depths += [margin - 2 * SUB * window] * copies
    return depths


def message_groups(fields, depths):
    groups, held = [], []
    for field in fields:
        held.append(field)
        if sum(depths[f] for f in held) % GROUP == 0:
            groups.append(held)
            held = []
    return groups + ([held] if held else [])


def even(axis):
    return lax.axis_index(axis) % 2 == 0


def pack_rows(message_ref, row, groups, depths, value_of, northward, rows):
    for group in groups:
        parts = []
        for field in group:
            start = jnp.where(northward, rows - depths[field], 0)
            parts.append(value_of(field, pl.ds(pl.multiple_of(start, 8), depths[field])))
        value = parts[0] if len(parts) == 1 else jnp.concatenate(parts, axis=0)
        message_ref[row : row + value.shape[0]] = value.astype(jnp.bfloat16)
        row += value.shape[0]
    return row


def local_kernel(
    margin,
    covered_hbm,
    offset_hbm,
    weights_hbm,
    thick_hbm,
    conc_hbm,
    mask_hbm,
    velocity_hbm,
    stress_hbm,
    ocean_hbm,
    wind_hbm,
    thick_out_hbm,
    fields_ref,
    current_ref,
    side_ref,
    lon_x_ref,
    lon_y_ref,
    lat_x_ref,
    lat_y_ref,
    covered,
    offset,
    weights,
    thick,
    conc,
    mask_in,
    velocity,
    stress,
    ocean,
    wind,
    in_sems,
    thick_sems,
    conc_sems,
    out_sems,
):
    cats, rows, cols = thick.shape
    windows = wind.shape[0]
    step = GROUP
    chunks = rows // step

    def rows_of(chunk):
        return pl.ds(chunk * step, step)

    small = [
        pltpu.make_async_copy(source, target, in_sems.at[i])
        for i, (source, target) in enumerate(
            (
                (covered_hbm, covered),
                (mask_hbm, mask_in),
                (velocity_hbm, velocity),
                (stress_hbm, stress),
                (ocean_hbm, ocean),
                (wind_hbm, wind),
                (weights_hbm, weights),
                (offset_hbm, offset),
            )
        )
    ]
    pairs = [
        [
            pltpu.make_async_copy(hbm.at[:, rows_of(c)], vmem.at[:, rows_of(c)], sems.at[c])
            for hbm, vmem, sems in ((thick_hbm, thick, thick_sems), (conc_hbm, conc, conc_sems))
        ]
        for c in range(chunks)
    ]
    writes = [
        pltpu.make_async_copy(thick.at[:, rows_of(c)], thick_out_hbm.at[:, rows_of(c)], out_sems.at[c])
        for c in range(chunks)
    ]
    for copy in small[:2] + [copy for pair in pairs for copy in pair] + small[2:]:
        copy.start()

    blocks = cols // BLK
    first = lax.axis_index("lon") * blocks
    small[0].wait()
    live = [covered[0, first + block] > 0 for block in range(blocks)]
    small[1].wait()
    for c in range(chunks):
        at = slice(c * step, (c + 1) * step)
        for copy in pairs[c]:
            copy.wait()
        for block in range(blocks):
            lanes = slice(block * BLK, (block + 1) * BLK)
            part = [conc[k, at, lanes] for k in range(cats)]
            height = [thick[k, at, lanes] for k in range(cats)]
            mask = mask_in[at, lanes].astype(jnp.float32)
            area = total(part)
            inverse = 1.0 / area
            factor = jnp.exp(-2.0 * (1.0 - area)) * (mask * (1.0 / 3.0))
            half = 0.5 * mask
            volume = total([a * h for a, h in zip(part, height)])
            for window in range(windows):
                mean = volume * inverse
                grown = [h + growth_rate / (0.5 + h) + mixing_rate * (mean - h) for h in height]
                height = [jnp.where(live[block], g, h) for g, h in zip(grown, height)]
                volume = total([a * h for a, h in zip(part, height)])
                fields_ref[STATE + 2 * window, at, lanes] = volume * factor
                fields_ref[STATE + 2 * window + 1, at, lanes] = half / (volume + 1.0)
            for k in range(cats):
                thick[k, at, lanes] = height[k]
        writes[c].start()

    small[2].wait()
    small[3].wait()
    for row in range(0, rows, step):
        at = slice(row, row + step)
        mask = mask_in[at].astype(jnp.float32)
        fields_ref[0, at] = velocity[0, at]
        fields_ref[1, at] = velocity[1, at]
        fields_ref[2, at] = (stress[0, at] + stress[1, at]) * mask
        fields_ref[3, at] = (stress[0, at] - stress[1, at]) * mask
        fields_ref[4, at] = (stress[2, at] + stress[2, at]) * mask

    count = fields_ref.shape[0]
    per = LANES // margin
    slot_of_lane = lax.broadcasted_iota(jnp.int32, (rows, LANES), 1) // margin
    eastward = even("lon")
    for group in range(lon_x_ref.shape[1] // LANES):
        east = jnp.zeros((rows, LANES), jnp.float32)
        west = jnp.zeros((rows, LANES), jnp.float32)
        for slot in range(min(per, count - group * per)):
            field = group * per + slot
            east, west = add_slot(
                east, west, fields_ref.at[field], slot_of_lane == slot, slot * margin, margin
            )
        store_sides(lon_x_ref, lon_y_ref, group, east, west, eastward)
    depths = field_depths(margin, windows)
    groups = message_groups(range(count), depths)
    northward = even("lat")

    def value_of(field, at):
        return fields_ref[field, at, :]

    pack_rows(lat_x_ref, 0, groups, depths, value_of, northward, rows)
    pack_rows(lat_y_ref, 0, groups, depths, value_of, jnp.logical_not(northward), rows)

    for copy in small[4:]:
        copy.wait()
    own_weights = weights[:, :rows]
    for w in range(windows):
        for k in range(2):
            current_ref[w, k] = wind[w, k].astype(jnp.float32) + jnp.dot(
                own_weights, ocean[w, k], preferred_element_type=jnp.float32
            )
    square = (rows, rows)
    diagonal = lax.broadcasted_iota(jnp.int32, square, 0) == lax.broadcasted_iota(
        jnp.int32, square, 1
    )
    up = offset[...] > 0
    for number, north in enumerate((northward, jnp.logical_not(northward))):
        wanted = jnp.where(north, up.astype(jnp.int32), 1 - up.astype(jnp.int32)) > 0
        pick = jnp.where(diagonal & wanted, 1.0, 0.0).astype(jnp.bfloat16)
        side_ref[:, number * rows : (number + 1) * rows] = jnp.dot(
            pick, weights[:, rows:], preferred_element_type=jnp.float32
        ).astype(jnp.bfloat16)

    for copy in writes:
        copy.wait()


def add_slot(east, west, field_ref, here, shift, margin):
    cols = field_ref.shape[1]
    last = pltpu.roll(field_ref[:, cols - LANES :], (shift + margin) % LANES, 1)
    leading = field_ref[:, :LANES]
    if shift:
        leading = pltpu.roll(leading, shift, 1)
    return jnp.where(here, last, east), jnp.where(here, leading, west)


def store_sides(x_ref, y_ref, group, east, west, eastward):
    lanes = slice(group * LANES, (group + 1) * LANES)
    x_ref[:, lanes] = jnp.where(eastward, east, west).astype(jnp.bfloat16)
    y_ref[:, lanes] = jnp.where(eastward, west, east).astype(jnp.bfloat16)


def force_kernel(
    margin,
    early,
    side_ref,
    tile_x_ref,
    tile_y_ref,
    current_ref,
    fields_ref,
    lon_x_in,
    lon_y_in,
    lat_x_in,
    lat_y_in,
    force_ref,
    lon_x_ref,
    lon_y_ref,
    lat_x_ref,
    lat_y_ref,
):
    windows, _, rows, cols = current_ref.shape
    side_x = side_ref[:, :rows]
    side_y = side_ref[:, rows:]

    def dot(a, b):
        return jnp.dot(a, b, preferred_element_type=jnp.float32)

    for w in range(windows):
        b = fields_ref[STATE + 2 * w + 1]
        for k in range(2):
            current = dot(side_x, tile_x_ref[w, k]) + dot(side_y, tile_y_ref[w, k])
            force_ref[2 * w + k] = b * (current_ref[w, k] + current)

    per = LANES // margin
    count = early + force_ref.shape[0]
    slot_of_lane = lax.broadcasted_iota(jnp.int32, (rows, LANES), 1) // margin
    eastward = even("lon")
    for group in range(lon_x_ref.shape[1] // LANES):
        lanes = slice(group * LANES, (group + 1) * LANES)
        x = lon_x_in[:, lanes].astype(jnp.float32)
        y = lon_y_in[:, lanes].astype(jnp.float32)
        east, west = jnp.where(eastward, x, y), jnp.where(eastward, y, x)
        for field in range(max(early, group * per), min(count, (group + 1) * per)):
            slot = field - group * per
            east, west = add_slot(
                east, west, force_ref.at[field - early], slot_of_lane == slot, slot * margin, margin
            )
        store_sides(lon_x_ref, lon_y_ref, group, east, west, eastward)

    depths = field_depths(margin, windows)
    groups = message_groups(range(early, count), depths)
    northward = even("lat")

    def value_of(field, at):
        return force_ref[field - early, at, :]

    for old_ref, ref, north in (
        (lat_x_in, lat_x_ref, northward),
        (lat_y_in, lat_y_ref, jnp.logical_not(northward)),
    ):
        row = old_ref.shape[0]
        ref[:row] = old_ref[...]
        row = pack_rows(ref, row, groups, depths, value_of, north, rows)
        ref[row:] = jnp.zeros((ref.shape[0] - row, cols), jnp.bfloat16)


def dynamics_kernel(
    margin,
    lat_count,
    fields_ref,
    force_ref,
    lon_x_ref,
    lon_y_ref,
    lat_x_ref,
    lat_y_ref,
    velocity_ref,
    stress_ref,
    state,
    strength,
    keep,
    push,
    force,
):
    early, rows, cols = fields_ref.shape
    windows = strength.shape[0]
    count = early + force_ref.shape[0]
    own_tiles = cols // LANES
    tiles = own_tiles + 1
    per = LANES // margin
    top = PAD + margin
    bottom = top + rows
    lane = lax.broadcasted_iota(jnp.int32, (8, LANES), 1)

    def place(field, tile, row, value):
        at = pl.ds(row, value.shape[0])
        if field < STATE:
            state[field, tile, at, :] = value
        elif field >= early:
            window, kind = divmod(field - early, 2)
            force[window, kind, tile, at, :] = value
        else:
            window, kind = divmod(field - STATE, 2)
            if kind == 0:
                strength[window, tile, at, :] = value
            else:
                push[window, tile, at, :] = value
                keep[window, tile, at, :] = jnp.where(value > 0.0, 1.0 - value, 0.0)

    zero = jnp.zeros((PAD, LANES), jnp.float32)
    for tile in range(tiles):
        for field in range(STATE):
            state[field, tile, 0:PAD, :] = zero
            state[field, tile, bottom + margin : bottom + margin + PAD, :] = zero

    def side_tiles(x, y, row):
        wide = lax.broadcasted_iota(jnp.int32, (x.shape[0], LANES), 1)
        from_x_is_east = even("lon")
        for group in range(x.shape[1] // LANES):
            lanes = slice(group * LANES, (group + 1) * LANES)
            x_now, y_now = x[:, lanes], y[:, lanes]
            east = jnp.where(from_x_is_east, x_now, y_now)
            west = jnp.where(from_x_is_east, y_now, x_now)
            for slot in range(min(per, count - group * per)):
                shift = slot * margin
                back = (LANES - margin - shift) % LANES
                e = pltpu.roll(east, LANES - shift, 1) if shift else east
                w = pltpu.roll(west, back, 1) if back else west
                value = jnp.where(wide < margin, e, jnp.where(wide >= LANES - margin, w, 0.0))
                place(group * per + slot, own_tiles, row, value)

    for field in range(count):
        for tile in range(own_tiles):
            lanes = slice(tile * LANES, (tile + 1) * LANES)
            own = fields_ref[field, :, lanes] if field < early else force_ref[field - early, :, lanes]
            place(field, tile, top, own)
    side_tiles(lon_x_ref[...].astype(jnp.float32), lon_y_ref[...].astype(jnp.float32), top)

    depths = field_depths(margin, windows)
    groups = message_groups(range(early), depths) + message_groups(range(early, count), depths)
    me = lax.axis_index("lat")
    for ref, north in ((lat_x_ref, even("lat")), (lat_y_ref, jnp.logical_not(even("lat")))):
        exists = jnp.where(north, me < lat_count - 1, me > 0)

        def read(at):
            return jnp.where(exists, ref[at].astype(jnp.float32), 0.0)

        row = 0
        for group in groups:
            height = sum(depths[f] for f in group)
            value = read(slice(row, row + height))
            begin = 0
            for field in group:
                depth = depths[field]
                to = pl.multiple_of(jnp.where(north, bottom, top - depth), 8)
                for tile in range(own_tiles):
                    lanes = slice(tile * LANES, (tile + 1) * LANES)
                    place(field, tile, to, value[begin : begin + depth, lanes])
                begin += depth
            row += height
        to = pl.multiple_of(jnp.where(north, bottom, top - margin), 8)
        packed = lon_x_ref.shape[1]
        side_tiles(
            read(slice(row, row + margin))[:, :packed],
            read(slice(row + margin, row + 2 * margin))[:, :packed],
            to,
        )

    first_lane = lane == 0
    last_lane = lane == LANES - 1

    def across(values):
        ahead = [pltpu.roll(x, LANES - 1, 1) for x in values]
        behind = [pltpu.roll(x, 1, 1) for x in values]
        return [
            jnp.where(last_lane, ahead[(j + 1) % tiles], ahead[j])
            - jnp.where(first_lane, behind[j - 1], behind[j])
            for j in range(tiles)
        ]

    def along(field, tile, row):
        return state[field, tile, row + 1 : row + 9, :] - state[field, tile, row - 1 : row + 7, :]

    every = range(tiles)
    for window in range(windows):
        spare = 2 * SUB * window
        row_list = range(top - margin + spare, bottom + margin - spare, 8)

        def subcycle(_, carry):
            for row in row_list:
                at = slice(row, row + 8)
                u_x = across([state[0, j, at, :] for j in every])
                v_x = across([state[1, j, at, :] for j in every])
                for j in every:
                    u_y = along(0, j, row)
                    v_y = along(1, j, row)
                    shear = u_y + v_x[j]
                    spread = u_x[j] + v_y
                    tension = u_x[j] - v_y
                    tension4 = tension * 0.25
                    shear4 = shear * 0.25
                    squares = spread * spread + tension * tension4 + (shear * shear4 + 1.0)
                    k = strength[window, j, at, :]
                    kr = k * lax.rsqrt(squares)
                    state[2, j, at, :] = state[2, j, at, :] * (2.0 / 3.0) + (
                        kr * (spread + tension4) - k
                    )
                    state[3, j, at, :] = state[3, j, at, :] * (2.0 / 3.0) + (
                        kr * (spread - tension4) - k
                    )
                    state[4, j, at, :] = state[4, j, at, :] * (2.0 / 3.0) + kr * shear4
            for row in row_list:
                at = slice(row, row + 8)
                p_x = across([state[2, j, at, :] for j in every])
                t_x = across([state[4, j, at, :] for j in every])
                for j in every:
                    b = push[window, j, at, :] * 0.25
                    a = keep[window, j, at, :]
                    state[0, j, at, :] = (
                        a * state[0, j, at, :]
                        + b * (p_x[j] + along(4, j, row))
                        + force[window, 0, j, at, :]
                    )
                    state[1, j, at, :] = (
                        a * state[1, j, at, :]
                        + b * (t_x[j] + along(3, j, row))
                        + force[window, 1, j, at, :]
                    )
            return carry

        lax.fori_loop(0, SUB, subcycle, 0)

    for tile in range(own_tiles):
        lanes = slice(tile * LANES, (tile + 1) * LANES)
        for row in range(0, rows, 8):
            at = slice(row, row + 8)
            to = slice(top + row, top + row + 8)
            velocity_ref[0, at, lanes] = state[0, tile, to, :]
            velocity_ref[1, at, lanes] = state[1, tile, to, :]
            p = state[2, tile, to, :]
            q = state[3, tile, to, :]
            stress_ref[0, at, lanes] = (p + q) * 0.5
            stress_ref[1, at, lanes] = (p - q) * 0.5
            stress_ref[2, at, lanes] = state[4, tile, to, :] * 0.5


def params():
    return pltpu.CompilerParams(vmem_limit_bytes=VMEM_LIMIT)


def swaps(axis, first, ring):
    n = lax.axis_size(axis)
    if ring and n % 2:
        raise ValueError("odd ring")
    partner = list(range(n))
    for i in range(first, n if ring else n - 1, 2):
        j = (i + 1) % n
        partner[i], partner[j] = j, i
    return list(enumerate(partner))


def exchange(x, y, axis, ring):
    return (
        lax.ppermute(x, axis, swaps(axis, 0, ring)),
        lax.ppermute(y, axis, swaps(axis, 1, ring)),
    )


def shape(dims, dtype=jnp.float32):
    return jax.ShapeDtypeStruct(dims, dtype)


def local(
    velocity,
    stress,
    thickness,
    concentration,
    land_mask,
    covered,
    ocean_current,
    wind_stress,
    regrid_weights,
    tile_offset,
):
    _, rows, cols = velocity.shape
    windows = wind_stress.shape[0]
    margin = 2 * SUB * windows
    early = STATE + 2 * windows
    count = early + 2 * windows
    tiles = cols // LANES + 1
    packed = -(-count // (LANES // margin)) * LANES
    depths = field_depths(margin, windows)
    early_rows = sum(depths[:early])
    message_rows = sum(depths)
    bf16 = jnp.bfloat16

    tile_x, tile_y = exchange(ocean_current, ocean_current, "lat", False)

    whole = pl.BlockSpec(memory_space=pltpu.VMEM)
    anywhere = pl.BlockSpec(memory_space=pl.ANY)
    chunks = rows // GROUP
    thick_out, fields, current, side, lon_x, lon_y, lat_x, lat_y = pl.pallas_call(
        functools.partial(local_kernel, margin),
        out_shape=(
            shape(thickness.shape),
            shape((early, rows, cols)),
            shape(wind_stress.shape),
            shape((rows, 2 * rows), bf16),
            shape((rows, packed), bf16),
            shape((rows, packed), bf16),
            shape((early_rows, cols), bf16),
            shape((early_rows, cols), bf16),
        ),
        in_specs=[anywhere] * 10,
        out_specs=(anywhere,) + (whole,) * 7,
        scratch_shapes=[
            pltpu.SMEM(covered.shape, jnp.int32),
            pltpu.VMEM((1, rows), jnp.int32),
            pltpu.VMEM(regrid_weights.shape, bf16),
            pltpu.VMEM(thickness.shape, jnp.float32),
            pltpu.VMEM(thickness.shape, jnp.float32),
            pltpu.VMEM(land_mask.shape, jnp.int32),
            pltpu.VMEM(velocity.shape, jnp.float32),
            pltpu.VMEM(stress.shape, jnp.float32),
            pltpu.VMEM(ocean_current.shape, bf16),
            pltpu.VMEM(wind_stress.shape, bf16),
            pltpu.SemaphoreType.DMA((8,)),
            pltpu.SemaphoreType.DMA((chunks,)),
            pltpu.SemaphoreType.DMA((chunks,)),
            pltpu.SemaphoreType.DMA((chunks,)),
        ],
        compiler_params=params(),
        cost_estimate=pl.CostEstimate(
            flops=100 * thickness.size, bytes_accessed=12 * thickness.size, transcendentals=0
        ),
        name="local",
    )(
        covered,
        tile_offset.reshape(1, rows),
        regrid_weights,
        thickness,
        concentration,
        land_mask,
        velocity,
        stress,
        ocean_current,
        wind_stress,
    )

    force, lon_x, lon_y, lat_x, lat_y = pl.pallas_call(
        functools.partial(force_kernel, margin, early),
        out_shape=(
            shape((2 * windows, rows, cols)),
            shape((rows, packed), bf16),
            shape((rows, packed), bf16),
            shape((message_rows + 2 * margin, cols), bf16),
            shape((message_rows + 2 * margin, cols), bf16),
        ),
        in_specs=[whole] * 9,
        out_specs=(whole,) * 5,
        compiler_params=params(),
        name="force",
    )(side, tile_x, tile_y, current, fields, lon_x, lon_y, lat_x, lat_y)

    lon_x, lon_y = exchange(lon_x, lon_y, "lon", True)
    north_end = rows - margin
    start_x = jnp.where(even("lat"), north_end, 0)
    for number, part in enumerate((lon_x, lon_y)):
        at = message_rows + number * margin
        corner_x = lax.dynamic_slice_in_dim(part, start_x, margin, 0)
        corner_y = lax.dynamic_slice_in_dim(part, north_end - start_x, margin, 0)
        lat_x = lat_x.at[at : at + margin, :packed].set(corner_x)
        lat_y = lat_y.at[at : at + margin, :packed].set(corner_y)
    lat_x, lat_y = exchange(lat_x, lat_y, "lat", False)

    height = rows + 2 * margin + 2 * PAD

    def scratch(*lead):
        return pltpu.VMEM((*lead, tiles, height, LANES), jnp.float32)

    velocity_out, stress_out = pl.pallas_call(
        functools.partial(dynamics_kernel, margin, lax.axis_size("lat")),
        out_shape=(shape(velocity.shape), shape(stress.shape)),
        in_specs=[whole] * 6,
        out_specs=(whole, whole),
        scratch_shapes=[
            scratch(STATE),
            scratch(windows),
            scratch(windows),
            scratch(windows),
            scratch(windows, 2),
        ],
        compiler_params=params(),
        name="dynamics",
    )(fields, force, lon_x, lon_y, lat_x, lat_y)
    return (velocity_out, stress_out, thick_out)


def solution(mesh):
    return jax.shard_map(
        local,
        mesh=mesh,
        in_specs=(
            P(None, "lat", "lon"),
            P(None, "lat", "lon"),
            P(None, "lat", "lon"),
            P(None, "lat", "lon"),
            P("lat", "lon"),
            P("lat", None),
            P(None, None, "lat", "lon"),
            P(None, None, "lat", "lon"),
            P("lat", None),
            P("lat"),
        ),
        out_specs=(P(None, "lat", "lon"), P(None, "lat", "lon"), P(None, "lat", "lon")),
        check_vma=False,
    )
```

```python
import functools

import jax
import jax.numpy as jnp
from jax import lax
from jax.experimental import pallas as pl
from jax.experimental.pallas import tpu as pltpu
from jax.sharding import PartitionSpec as P

BLK = 128
SUB = 4
LANES = 128
GROUP = 16
PAD = 8
STATE = 5
VMEM_LIMIT = 16 * 1024 * 1024

growth_rate = 0.3
mixing_rate = 0.3


def total(terms):
    result = terms[0]
    for term in terms[1:]:
        result = result + term
    return result


def field_depths(margin, windows):
    depths = [margin] * STATE
    for copies in (2, 2):
        for window in range(windows):
            depths += [margin - 2 * SUB * window] * copies
    return depths


def message_groups(fields, depths):
    groups, held = [], []
    for field in fields:
        held.append(field)
        if sum(depths[f] for f in held) % GROUP == 0:
            groups.append(held)
            held = []
    return groups + ([held] if held else [])


def even(axis):
    return lax.axis_index(axis) % 2 == 0


def pack_rows(message_ref, row, groups, depths, value_of, northward, rows):
    for group in groups:
        parts = []
        for field in group:
            start = jnp.where(northward, rows - depths[field], 0)
            parts.append(value_of(field, pl.ds(pl.multiple_of(start, 8), depths[field])))
        value = parts[0] if len(parts) == 1 else jnp.concatenate(parts, axis=0)
        message_ref[row : row + value.shape[0]] = value.astype(jnp.bfloat16)
        row += value.shape[0]
    return row


def local_kernel(
    margin,
    covered_hbm,
    offset_hbm,
    weights_hbm,
    thick_hbm,
    conc_hbm,
    mask_hbm,
    velocity_hbm,
    stress_hbm,
    ocean_hbm,
    wind_hbm,
    thick_out_hbm,
    fields_ref,
    current_ref,
    side_ref,
    lon_x_ref,
    lon_y_ref,
    lat_x_ref,
    lat_y_ref,
    covered,
    offset,
    weights,
    thick,
    conc,
    mask_in,
    velocity,
    stress,
    ocean,
    wind,
    in_sems,
    thick_sems,
    conc_sems,
    out_sems,
):
    cats, rows, cols = thick.shape
    windows = wind.shape[0]
    step = GROUP
    chunks = rows // step

    def rows_of(chunk):
        return pl.ds(chunk * step, step)

    small = [
        pltpu.make_async_copy(source, target, in_sems.at[i])
        for i, (source, target) in enumerate(
            (
                (covered_hbm, covered),
                (mask_hbm, mask_in),
                (velocity_hbm, velocity),
                (stress_hbm, stress),
                (ocean_hbm, ocean),
                (wind_hbm, wind),
                (weights_hbm, weights),
                (offset_hbm, offset),
            )
        )
    ]
    pairs = [
        [
            pltpu.make_async_copy(hbm.at[:, rows_of(c)], vmem.at[:, rows_of(c)], sems.at[c])
            for hbm, vmem, sems in ((thick_hbm, thick, thick_sems), (conc_hbm, conc, conc_sems))
        ]
        for c in range(chunks)
    ]
    writes = [
        pltpu.make_async_copy(thick.at[:, rows_of(c)], thick_out_hbm.at[:, rows_of(c)], out_sems.at[c])
        for c in range(chunks)
    ]
    for copy in small[:2] + [copy for pair in pairs for copy in pair] + small[2:]:
        copy.start()

    blocks = cols // BLK
    first = lax.axis_index("lon") * blocks
    small[0].wait()
    live = [covered[0, first + block] > 0 for block in range(blocks)]
    small[1].wait()
    for c in range(chunks):
        at = slice(c * step, (c + 1) * step)
        for copy in pairs[c]:
            copy.wait()
        for block in range(blocks):
            lanes = slice(block * BLK, (block + 1) * BLK)
            part = [conc[k, at, lanes] for k in range(cats)]
            height = [thick[k, at, lanes] for k in range(cats)]
            mask = mask_in[at, lanes].astype(jnp.float32)
            area = total(part)
            inverse = 1.0 / area
            factor = jnp.exp(-2.0 * (1.0 - area)) * (mask * (1.0 / 3.0))
            half = 0.5 * mask
            volume = total([a * h for a, h in zip(part, height)])
            for window in range(windows):
                mean = volume * inverse
                grown = [h + growth_rate / (0.5 + h) + mixing_rate * (mean - h) for h in height]
                height = [jnp.where(live[block], g, h) for g, h in zip(grown, height)]
                volume = total([a * h for a, h in zip(part, height)])
                fields_ref[STATE + 2 * window, at, lanes] = volume * factor
                fields_ref[STATE + 2 * window + 1, at, lanes] = half / (volume + 1.0)
            for k in range(cats):
                thick[k, at, lanes] = height[k]
        writes[c].start()

    small[2].wait()
    small[3].wait()
    for row in range(0, rows, step):
        at = slice(row, row + step)
        mask = mask_in[at].astype(jnp.float32)
        fields_ref[0, at] = velocity[0, at]
        fields_ref[1, at] = velocity[1, at]
        fields_ref[2, at] = (stress[0, at] + stress[1, at]) * mask
        fields_ref[3, at] = (stress[0, at] - stress[1, at]) * mask
        fields_ref[4, at] = (stress[2, at] + stress[2, at]) * mask

    count = fields_ref.shape[0]
    per = LANES // margin
    slot_of_lane = lax.broadcasted_iota(jnp.int32, (rows, LANES), 1) // margin
    eastward = even("lon")
    for group in range(lon_x_ref.shape[1] // LANES):
        east = jnp.zeros((rows, LANES), jnp.float32)
        west = jnp.zeros((rows, LANES), jnp.float32)
        for slot in range(min(per, count - group * per)):
            field = group * per + slot
            east, west = add_slot(
                east, west, fields_ref.at[field], slot_of_lane == slot, slot * margin, margin
            )
        store_sides(lon_x_ref, lon_y_ref, group, east, west, eastward)
    depths = field_depths(margin, windows)
    groups = message_groups(range(count), depths)
    northward = even("lat")

    def value_of(field, at):
        return fields_ref[field, at, :]

    pack_rows(lat_x_ref, 0, groups, depths, value_of, northward, rows)
    pack_rows(lat_y_ref, 0, groups, depths, value_of, jnp.logical_not(northward), rows)

    for copy in small[4:]:
        copy.wait()
    own_weights = weights[:, :rows]
    for w in range(windows):
        for k in range(2):
            current_ref[w, k] = wind[w, k].astype(jnp.float32) + jnp.dot(
                own_weights, ocean[w, k], preferred_element_type=jnp.float32
            )
    square = (rows, rows)
    diagonal = lax.broadcasted_iota(jnp.int32, square, 0) == lax.broadcasted_iota(
        jnp.int32, square, 1
    )
    up = offset[...] > 0
    for number, north in enumerate((northward, jnp.logical_not(northward))):
        wanted = jnp.where(north, up.astype(jnp.int32), 1 - up.astype(jnp.int32)) > 0
        pick = jnp.where(diagonal & wanted, 1.0, 0.0).astype(jnp.bfloat16)
        side_ref[:, number * rows : (number + 1) * rows] = jnp.dot(
            pick, weights[:, rows:], preferred_element_type=jnp.float32
        ).astype(jnp.bfloat16)

    for copy in writes:
        copy.wait()


def add_slot(east, west, field_ref, here, shift, margin):
    cols = field_ref.shape[1]
    last = pltpu.roll(field_ref[:, cols - LANES :], (shift + margin) % LANES, 1)
    leading = field_ref[:, :LANES]
    if shift:
        leading = pltpu.roll(leading, shift, 1)
    return jnp.where(here, last, east), jnp.where(here, leading, west)


def store_sides(x_ref, y_ref, group, east, west, eastward):
    lanes = slice(group * LANES, (group + 1) * LANES)
    x_ref[:, lanes] = jnp.where(eastward, east, west).astype(jnp.bfloat16)
    y_ref[:, lanes] = jnp.where(eastward, west, east).astype(jnp.bfloat16)


def force_kernel(
    margin,
    early,
    side_ref,
    tile_x_ref,
    tile_y_ref,
    current_ref,
    fields_ref,
    lon_x_in,
    lon_y_in,
    lat_x_in,
    lat_y_in,
    force_ref,
    lon_x_ref,
    lon_y_ref,
    lat_x_ref,
    lat_y_ref,
):
    windows, _, rows, cols = current_ref.shape
    side_x = side_ref[:, :rows]
    side_y = side_ref[:, rows:]

    def dot(a, b):
        return jnp.dot(a, b, preferred_element_type=jnp.float32)

    for w in range(windows):
        b = fields_ref[STATE + 2 * w + 1]
        for k in range(2):
            current = dot(side_x, tile_x_ref[w, k]) + dot(side_y, tile_y_ref[w, k])
            force_ref[2 * w + k] = b * (current_ref[w, k] + current)

    per = LANES // margin
    count = early + force_ref.shape[0]
    slot_of_lane = lax.broadcasted_iota(jnp.int32, (rows, LANES), 1) // margin
    eastward = even("lon")
    for group in range(lon_x_ref.shape[1] // LANES):
        lanes = slice(group * LANES, (group + 1) * LANES)
        x = lon_x_in[:, lanes].astype(jnp.float32)
        y = lon_y_in[:, lanes].astype(jnp.float32)
        east, west = jnp.where(eastward, x, y), jnp.where(eastward, y, x)
        for field in range(max(early, group * per), min(count, (group + 1) * per)):
            slot = field - group * per
            east, west = add_slot(
                east, west, force_ref.at[field - early], slot_of_lane == slot, slot * margin, margin
            )
        store_sides(lon_x_ref, lon_y_ref, group, east, west, eastward)

    depths = field_depths(margin, windows)
    groups = message_groups(range(early, count), depths)
    northward = even("lat")

    def value_of(field, at):
        return force_ref[field - early, at, :]

    for old_ref, ref, north in (
        (lat_x_in, lat_x_ref, northward),
        (lat_y_in, lat_y_ref, jnp.logical_not(northward)),
    ):
        row = old_ref.shape[0]
        ref[:row] = old_ref[...]
        row = pack_rows(ref, row, groups, depths, value_of, north, rows)
        ref[row:] = jnp.zeros((ref.shape[0] - row, cols), jnp.bfloat16)


def dynamics_kernel(
    margin,
    lat_count,
    fields_ref,
    force_ref,
    lon_x_ref,
    lon_y_ref,
    lat_x_ref,
    lat_y_ref,
    velocity_ref,
    stress_ref,
    state,
    strength,
    keep,
    push,
    force,
):
    early, rows, cols = fields_ref.shape
    windows = strength.shape[0]
    count = early + force_ref.shape[0]
    own_tiles = cols // LANES
    tiles = own_tiles + 1
    per = LANES // margin
    top = PAD + margin
    bottom = top + rows
    lane = lax.broadcasted_iota(jnp.int32, (8, LANES), 1)

    def place(field, tile, row, value):
        at = pl.ds(row, value.shape[0])
        if field < STATE:
            state[field, tile, at, :] = value
        elif field >= early:
            window, kind = divmod(field - early, 2)
            force[window, kind, tile, at, :] = value
        else:
            window, kind = divmod(field - STATE, 2)
            if kind == 0:
                strength[window, tile, at, :] = value
            else:
                push[window, tile, at, :] = value
                keep[window, tile, at, :] = jnp.where(value > 0.0, 1.0 - value, 0.0)

    zero = jnp.zeros((PAD, LANES), jnp.float32)
    for tile in range(tiles):
        for field in range(STATE):
            state[field, tile, 0:PAD, :] = zero
            state[field, tile, bottom + margin : bottom + margin + PAD, :] = zero

    def side_tiles(x, y, row):
        wide = lax.broadcasted_iota(jnp.int32, (x.shape[0], LANES), 1)
        from_x_is_east = even("lon")
        for group in range(x.shape[1] // LANES):
            lanes = slice(group * LANES, (group + 1) * LANES)
            x_now, y_now = x[:, lanes], y[:, lanes]
            east = jnp.where(from_x_is_east, x_now, y_now)
            west = jnp.where(from_x_is_east, y_now, x_now)
            for slot in range(min(per, count - group * per)):
                shift = slot * margin
                back = (LANES - margin - shift) % LANES
                e = pltpu.roll(east, LANES - shift, 1) if shift else east
                w = pltpu.roll(west, back, 1) if back else west
                value = jnp.where(wide < margin, e, jnp.where(wide >= LANES - margin, w, 0.0))
                place(group * per + slot, own_tiles, row, value)

    for field in range(count):
        for tile in range(own_tiles):
            lanes = slice(tile * LANES, (tile + 1) * LANES)
            own = fields_ref[field, :, lanes] if field < early else force_ref[field - early, :, lanes]
            place(field, tile, top, own)
    side_tiles(lon_x_ref[...].astype(jnp.float32), lon_y_ref[...].astype(jnp.float32), top)

    depths = field_depths(margin, windows)
    groups = message_groups(range(early), depths) + message_groups(range(early, count), depths)
    me = lax.axis_index("lat")
    for ref, north in ((lat_x_ref, even("lat")), (lat_y_ref, jnp.logical_not(even("lat")))):
        exists = jnp.where(north, me < lat_count - 1, me > 0)

        def read(at):
            return jnp.where(exists, ref[at].astype(jnp.float32), 0.0)

        row = 0
        for group in groups:
            height = sum(depths[f] for f in group)
            value = read(slice(row, row + height))
            begin = 0
            for field in group:
                depth = depths[field]
                to = pl.multiple_of(jnp.where(north, bottom, top - depth), 8)
                for tile in range(own_tiles):
                    lanes = slice(tile * LANES, (tile + 1) * LANES)
                    place(field, tile, to, value[begin : begin + depth, lanes])
                begin += depth
            row += height
        to = pl.multiple_of(jnp.where(north, bottom, top - margin), 8)
        packed = lon_x_ref.shape[1]
        side_tiles(
            read(slice(row, row + margin))[:, :packed],
            read(slice(row + margin, row + 2 * margin))[:, :packed],
            to,
        )

    first_lane = lane == 0
    last_lane = lane == LANES - 1

    def across(values):
        ahead = [pltpu.roll(x, LANES - 1, 1) for x in values]
        behind = [pltpu.roll(x, 1, 1) for x in values]
        return [
            jnp.where(last_lane, ahead[(j + 1) % tiles], ahead[j])
            - jnp.where(first_lane, behind[j - 1], behind[j])
            for j in range(tiles)
        ]

    def along(field, tile, row):
        return state[field, tile, row + 1 : row + 9, :] - state[field, tile, row - 1 : row + 7, :]

    every = range(tiles)
    for window in range(windows):
        spare = 2 * SUB * window
        row_list = range(top - margin + spare, bottom + margin - spare, 8)

        def subcycle(_, carry):
            for row in row_list:
                at = slice(row, row + 8)
                u_x = across([state[0, j, at, :] for j in every])
                v_x = across([state[1, j, at, :] for j in every])
                for j in every:
                    u_y = along(0, j, row)
                    v_y = along(1, j, row)
                    shear = u_y + v_x[j]
                    spread = u_x[j] + v_y
                    tension = u_x[j] - v_y
                    tension4 = tension * 0.25
                    shear4 = shear * 0.25
                    squares = spread * spread + tension * tension4 + (shear * shear4 + 1.0)
                    k = strength[window, j, at, :]
                    kr = k * lax.rsqrt(squares)
                    state[2, j, at, :] = state[2, j, at, :] * (2.0 / 3.0) + (
                        kr * (spread + tension4) - k
                    )
                    state[3, j, at, :] = state[3, j, at, :] * (2.0 / 3.0) + (
                        kr * (spread - tension4) - k
                    )
                    state[4, j, at, :] = state[4, j, at, :] * (2.0 / 3.0) + kr * shear4
            for row in row_list:
                at = slice(row, row + 8)
                p_x = across([state[2, j, at, :] for j in every])
                t_x = across([state[4, j, at, :] for j in every])
                for j in every:
                    b = push[window, j, at, :] * 0.25
                    a = keep[window, j, at, :]
                    state[0, j, at, :] = (
                        a * state[0, j, at, :]
                        + b * (p_x[j] + along(4, j, row))
                        + force[window, 0, j, at, :]
                    )
                    state[1, j, at, :] = (
                        a * state[1, j, at, :]
                        + b * (t_x[j] + along(3, j, row))
                        + force[window, 1, j, at, :]
                    )
            return carry

        lax.fori_loop(0, SUB, subcycle, 0)

    for tile in range(own_tiles):
        lanes = slice(tile * LANES, (tile + 1) * LANES)
        for row in range(0, rows, 8):
            at = slice(row, row + 8)
            to = slice(top + row, top + row + 8)
            velocity_ref[0, at, lanes] = state[0, tile, to, :]
            velocity_ref[1, at, lanes] = state[1, tile, to, :]
            p = state[2, tile, to, :]
            q = state[3, tile, to, :]
            stress_ref[0, at, lanes] = (p + q) * 0.5
            stress_ref[1, at, lanes] = (p - q) * 0.5
            stress_ref[2, at, lanes] = state[4, tile, to, :] * 0.5


def params():
    return pltpu.CompilerParams(vmem_limit_bytes=VMEM_LIMIT)


def lon_swaps(first):
    n = lax.axis_size("lon")
    if n % 2:
        raise ValueError("odd ring")
    pairs = [(i, (i + 1) % n) for i in range(first, n, 2)]
    return pairs + [(j, i) for i, j in pairs]


def lat_swaps(first):
    m, n = lax.axis_size("lat"), lax.axis_size("lon")
    partner = {}
    for i in range(m):
        north = i + 1 if (i - first) % 2 == 0 else i - 1
        for k in range(n):
            to = (north, k) if 0 <= north < m else (i, k ^ 1)
            partner[k * m + i] = to[1] * m + to[0]
    return list(partner.items())


def lon_exchange(x, y):
    return lax.ppermute(x, "lon", lon_swaps(0)), lax.ppermute(y, "lon", lon_swaps(1))


def lat_exchange(x, y):
    axes = ("lon", "lat")
    return lax.ppermute(x, axes, lat_swaps(0)), lax.ppermute(y, axes, lat_swaps(1))


def shape(dims, dtype=jnp.float32):
    return jax.ShapeDtypeStruct(dims, dtype)


def local(
    velocity,
    stress,
    thickness,
    concentration,
    land_mask,
    covered,
    ocean_current,
    wind_stress,
    regrid_weights,
    tile_offset,
):
    _, rows, cols = velocity.shape
    windows = wind_stress.shape[0]
    margin = 2 * SUB * windows
    early = STATE + 2 * windows
    count = early + 2 * windows
    tiles = cols // LANES + 1
    packed = -(-count // (LANES // margin)) * LANES
    depths = field_depths(margin, windows)
    early_rows = sum(depths[:early])
    message_rows = sum(depths)
    bf16 = jnp.bfloat16

    tile_x, tile_y = lat_exchange(ocean_current, ocean_current)

    whole = pl.BlockSpec(memory_space=pltpu.VMEM)
    anywhere = pl.BlockSpec(memory_space=pl.ANY)
    chunks = rows // GROUP
    thick_out, fields, current, side, lon_x, lon_y, lat_x, lat_y = pl.pallas_call(
        functools.partial(local_kernel, margin),
        out_shape=(
            shape(thickness.shape),
            shape((early, rows, cols)),
            shape(wind_stress.shape),
            shape((rows, 2 * rows), bf16),
            shape((rows, packed), bf16),
            shape((rows, packed), bf16),
            shape((early_rows, cols), bf16),
            shape((early_rows, cols), bf16),
        ),
        in_specs=[anywhere] * 10,
        out_specs=(anywhere,) + (whole,) * 7,
        scratch_shapes=[
            pltpu.SMEM(covered.shape, jnp.int32),
            pltpu.VMEM((1, rows), jnp.int32),
            pltpu.VMEM(regrid_weights.shape, bf16),
            pltpu.VMEM(thickness.shape, jnp.float32),
            pltpu.VMEM(thickness.shape, jnp.float32),
            pltpu.VMEM(land_mask.shape, jnp.int32),
            pltpu.VMEM(velocity.shape, jnp.float32),
            pltpu.VMEM(stress.shape, jnp.float32),
            pltpu.VMEM(ocean_current.shape, bf16),
            pltpu.VMEM(wind_stress.shape, bf16),
            pltpu.SemaphoreType.DMA((8,)),
            pltpu.SemaphoreType.DMA((chunks,)),
            pltpu.SemaphoreType.DMA((chunks,)),
            pltpu.SemaphoreType.DMA((chunks,)),
        ],
        compiler_params=params(),
        cost_estimate=pl.CostEstimate(
            flops=100 * thickness.size, bytes_accessed=12 * thickness.size, transcendentals=0
        ),
        name="local",
    )(
        *(
            pltpu.with_memory_space_constraint(x, pltpu.HBM)
            for x in (
                covered,
                tile_offset.reshape(1, rows),
                regrid_weights,
                thickness,
                concentration,
                land_mask,
                velocity,
                stress,
                ocean_current,
                wind_stress,
            )
        )
    )

    force, lon_x, lon_y, lat_x, lat_y = pl.pallas_call(
        functools.partial(force_kernel, margin, early),
        out_shape=(
            shape((2 * windows, rows, cols)),
            shape((rows, packed), bf16),
            shape((rows, packed), bf16),
            shape((message_rows + 2 * margin, cols), bf16),
            shape((message_rows + 2 * margin, cols), bf16),
        ),
        in_specs=[whole] * 9,
        out_specs=(whole,) * 5,
        compiler_params=params(),
        name="force",
    )(side, tile_x, tile_y, current, fields, lon_x, lon_y, lat_x, lat_y)

    lon_x, lon_y = lon_exchange(lon_x, lon_y)
    north_end = rows - margin
    start_x = jnp.where(even("lat"), north_end, 0)
    for number, part in enumerate((lon_x, lon_y)):
        at = message_rows + number * margin
        corner_x = lax.dynamic_slice_in_dim(part, start_x, margin, 0)
        corner_y = lax.dynamic_slice_in_dim(part, north_end - start_x, margin, 0)
        lat_x = lat_x.at[at : at + margin, :packed].set(corner_x)
        lat_y = lat_y.at[at : at + margin, :packed].set(corner_y)
    lat_x, lat_y = lat_exchange(lat_x, lat_y)

    height = rows + 2 * margin + 2 * PAD

    def scratch(*lead):
        return pltpu.VMEM((*lead, tiles, height, LANES), jnp.float32)

    velocity_out, stress_out = pl.pallas_call(
        functools.partial(dynamics_kernel, margin, lax.axis_size("lat")),
        out_shape=(shape(velocity.shape), shape(stress.shape)),
        in_specs=[whole] * 6,
        out_specs=(whole, whole),
        scratch_shapes=[
            scratch(STATE),
            scratch(windows),
            scratch(windows),
            scratch(windows),
            scratch(windows, 2),
        ],
        compiler_params=params(),
        name="dynamics",
    )(fields, force, lon_x, lon_y, lat_x, lat_y)
    return (velocity_out, stress_out, thick_out)


def solution(mesh):
    return jax.shard_map(
        local,
        mesh=mesh,
        in_specs=(
            P(None, "lat", "lon"),
            P(None, "lat", "lon"),
            P(None, "lat", "lon"),
            P(None, "lat", "lon"),
            P("lat", "lon"),
            P("lat", None),
            P(None, None, "lat", "lon"),
            P(None, None, "lat", "lon"),
            P("lat", None),
            P("lat"),
        ),
        out_specs=(P(None, "lat", "lon"), P(None, "lat", "lon"), P(None, "lat", "lon")),
        check_vma=False,
    )
```

```python
import functools

import jax
import jax.numpy as jnp
from jax import lax
from jax.experimental import pallas as pl
from jax.experimental.pallas import tpu as pltpu
from jax.sharding import PartitionSpec as P

BLK = 128
SUB = 4
LANES = 128
GROUP = 16
STATE = 5
VMEM_LIMIT = 16 * 1024 * 1024

growth_rate = 0.3
mixing_rate = 0.3


def total(terms):
    result = terms[0]
    for term in terms[1:]:
        result = result + term
    return result


def field_depths(margin, windows):
    depths = [margin] * STATE
    for copies in (2, 2):
        for window in range(windows):
            depths += [margin - 2 * SUB * window] * copies
    return depths


def message_groups(fields, depths):
    groups, held = [], []
    for field in fields:
        held.append(field)
        if sum(depths[f] for f in held) % GROUP == 0:
            groups.append(held)
            held = []
    return groups + ([held] if held else [])


def even(axis):
    return lax.axis_index(axis) % 2 == 0


def pack_rows(message_ref, row, groups, depths, value_of, northward, rows):
    for group in groups:
        parts = []
        for field in group:
            start = jnp.where(northward, rows - depths[field], 0)
            parts.append(value_of(field, pl.ds(pl.multiple_of(start, 8), depths[field])))
        value = parts[0] if len(parts) == 1 else jnp.concatenate(parts, axis=0)
        message_ref[row : row + value.shape[0]] = value.astype(jnp.bfloat16)
        row += value.shape[0]
    return row


def local_kernel(
    margin,
    covered_hbm,
    offset_hbm,
    weights_hbm,
    thick_hbm,
    conc_hbm,
    mask_hbm,
    velocity_hbm,
    stress_hbm,
    ocean_hbm,
    wind_hbm,
    thick_out_hbm,
    fields_ref,
    current_ref,
    side_ref,
    lon_x_ref,
    lon_y_ref,
    lat_x_ref,
    lat_y_ref,
    covered,
    offset,
    weights,
    thick,
    conc,
    mask_in,
    velocity,
    stress,
    ocean,
    wind,
    in_sems,
    thick_sems,
    conc_sems,
    out_sems,
):
    cats, rows, cols = thick.shape
    windows = wind.shape[0]
    step = GROUP
    chunks = rows // step

    def rows_of(chunk):
        return pl.ds(chunk * step, step)

    small = [
        pltpu.make_async_copy(source, target, in_sems.at[i])
        for i, (source, target) in enumerate(
            (
                (covered_hbm, covered),
                (mask_hbm, mask_in),
                (velocity_hbm, velocity),
                (stress_hbm, stress),
                (ocean_hbm, ocean),
                (wind_hbm, wind),
                (weights_hbm, weights),
                (offset_hbm, offset),
            )
        )
    ]
    pairs = [
        [
            pltpu.make_async_copy(hbm.at[:, rows_of(c)], vmem.at[:, rows_of(c)], sems.at[c])
            for hbm, vmem, sems in ((thick_hbm, thick, thick_sems), (conc_hbm, conc, conc_sems))
        ]
        for c in range(chunks)
    ]
    writes = [
        pltpu.make_async_copy(thick.at[:, rows_of(c)], thick_out_hbm.at[:, rows_of(c)], out_sems.at[c])
        for c in range(chunks)
    ]
    for copy in small[:2] + [copy for pair in pairs for copy in pair] + small[2:]:
        copy.start()

    blocks = cols // BLK
    first = lax.axis_index("lon") * blocks
    small[0].wait()
    live = [covered[0, first + block] > 0 for block in range(blocks)]
    small[1].wait()
    for c in range(chunks):
        at = slice(c * step, (c + 1) * step)
        for copy in pairs[c]:
            copy.wait()
        for block in range(blocks):
            lanes = slice(block * BLK, (block + 1) * BLK)
            part = [conc[k, at, lanes] for k in range(cats)]
            height = [thick[k, at, lanes] for k in range(cats)]
            mask = mask_in[at, lanes].astype(jnp.float32)
            area = total(part)
            inverse = 1.0 / area
            factor = jnp.exp(-2.0 * (1.0 - area)) * (mask * (1.0 / 3.0))
            half = 0.5 * mask
            volume = total([a * h for a, h in zip(part, height)])
            for window in range(windows):
                mean = volume * inverse
                grown = [h + growth_rate / (0.5 + h) + mixing_rate * (mean - h) for h in height]
                height = [jnp.where(live[block], g, h) for g, h in zip(grown, height)]
                volume = total([a * h for a, h in zip(part, height)])
                fields_ref[STATE + 2 * window, at, lanes] = volume * factor
                fields_ref[STATE + 2 * window + 1, at, lanes] = half / (volume + 1.0)
            for k in range(cats):
                thick[k, at, lanes] = height[k]
        writes[c].start()

    small[2].wait()
    small[3].wait()
    for row in range(0, rows, step):
        at = slice(row, row + step)
        mask = mask_in[at].astype(jnp.float32)
        fields_ref[0, at] = velocity[0, at]
        fields_ref[1, at] = velocity[1, at]
        fields_ref[2, at] = (stress[0, at] + stress[1, at]) * mask
        fields_ref[3, at] = (stress[0, at] - stress[1, at]) * mask
        fields_ref[4, at] = (stress[2, at] + stress[2, at]) * mask

    count = fields_ref.shape[0]
    per = LANES // margin
    slot_of_lane = lax.broadcasted_iota(jnp.int32, (rows, LANES), 1) // margin
    eastward = even("lon")
    for group in range(lon_x_ref.shape[1] // LANES):
        east = jnp.zeros((rows, LANES), jnp.float32)
        west = jnp.zeros((rows, LANES), jnp.float32)
        for slot in range(min(per, count - group * per)):
            field = group * per + slot
            east, west = add_slot(
                east, west, fields_ref.at[field], slot_of_lane == slot, slot * margin, margin
            )
        store_sides(lon_x_ref, lon_y_ref, group, east, west, eastward)
    depths = field_depths(margin, windows)
    groups = message_groups(range(count), depths)
    northward = even("lat")

    def value_of(field, at):
        return fields_ref[field, at, :]

    pack_rows(lat_x_ref, 0, groups, depths, value_of, northward, rows)
    pack_rows(lat_y_ref, 0, groups, depths, value_of, jnp.logical_not(northward), rows)

    for copy in small[4:]:
        copy.wait()
    own_weights = weights[:, :rows]
    for w in range(windows):
        for k in range(2):
            current_ref[w, k] = wind[w, k].astype(jnp.float32) + jnp.dot(
                own_weights, ocean[w, k], preferred_element_type=jnp.float32
            )
    square = (rows, rows)
    diagonal = lax.broadcasted_iota(jnp.int32, square, 0) == lax.broadcasted_iota(
        jnp.int32, square, 1
    )
    up = offset[...] > 0
    for number, north in enumerate((northward, jnp.logical_not(northward))):
        wanted = jnp.where(north, up.astype(jnp.int32), 1 - up.astype(jnp.int32)) > 0
        pick = jnp.where(diagonal & wanted, 1.0, 0.0).astype(jnp.bfloat16)
        side_ref[:, number * rows : (number + 1) * rows] = jnp.dot(
            pick, weights[:, rows:], preferred_element_type=jnp.float32
        ).astype(jnp.bfloat16)

    for copy in writes:
        copy.wait()


def add_slot(east, west, field_ref, here, shift, margin):
    cols = field_ref.shape[1]
    last = pltpu.roll(field_ref[:, cols - LANES :], (shift + margin) % LANES, 1)
    leading = field_ref[:, :LANES]
    if shift:
        leading = pltpu.roll(leading, shift, 1)
    return jnp.where(here, last, east), jnp.where(here, leading, west)


def store_sides(x_ref, y_ref, group, east, west, eastward):
    lanes = slice(group * LANES, (group + 1) * LANES)
    x_ref[:, lanes] = jnp.where(eastward, east, west).astype(jnp.bfloat16)
    y_ref[:, lanes] = jnp.where(eastward, west, east).astype(jnp.bfloat16)


def force_kernel(
    margin,
    early,
    side_ref,
    tile_x_ref,
    tile_y_ref,
    current_ref,
    fields_ref,
    lon_x_in,
    lon_y_in,
    lat_x_in,
    lat_y_in,
    force_ref,
    lon_x_ref,
    lon_y_ref,
    lat_x_ref,
    lat_y_ref,
):
    windows, _, rows, cols = current_ref.shape
    side_x = side_ref[:, :rows]
    side_y = side_ref[:, rows:]

    def dot(a, b):
        return jnp.dot(a, b, preferred_element_type=jnp.float32)

    for w in range(windows):
        b = fields_ref[STATE + 2 * w + 1]
        for k in range(2):
            current = dot(side_x, tile_x_ref[w, k]) + dot(side_y, tile_y_ref[w, k])
            force_ref[2 * w + k] = b * (current_ref[w, k] + current)

    per = LANES // margin
    count = early + force_ref.shape[0]
    slot_of_lane = lax.broadcasted_iota(jnp.int32, (rows, LANES), 1) // margin
    eastward = even("lon")
    for group in range(lon_x_ref.shape[1] // LANES):
        lanes = slice(group * LANES, (group + 1) * LANES)
        x = lon_x_in[:, lanes].astype(jnp.float32)
        y = lon_y_in[:, lanes].astype(jnp.float32)
        east, west = jnp.where(eastward, x, y), jnp.where(eastward, y, x)
        for field in range(max(early, group * per), min(count, (group + 1) * per)):
            slot = field - group * per
            east, west = add_slot(
                east, west, force_ref.at[field - early], slot_of_lane == slot, slot * margin, margin
            )
        store_sides(lon_x_ref, lon_y_ref, group, east, west, eastward)

    depths = field_depths(margin, windows)
    groups = message_groups(range(early, count), depths)
    northward = even("lat")

    def value_of(field, at):
        return force_ref[field - early, at, :]

    for old_ref, ref, north in (
        (lat_x_in, lat_x_ref, northward),
        (lat_y_in, lat_y_ref, jnp.logical_not(northward)),
    ):
        row = old_ref.shape[0]
        ref[:row] = old_ref[...]
        row = pack_rows(ref, row, groups, depths, value_of, north, rows)
        ref[row:] = jnp.zeros((ref.shape[0] - row, cols), jnp.bfloat16)


def place(refs, early, field, tile, row, value):
    velocity, stress, strength, keep, push, force = refs
    at = pl.ds(row, value.shape[0])
    if field < 2:
        velocity[0, field, tile, at, :] = value
    elif field < STATE:
        stress[0, field - 2, tile, at, :] = value
    elif field >= early:
        window, kind = divmod(field - early, 2)
        force[window, kind, tile, at, :] = value
    else:
        window, kind = divmod(field - STATE, 2)
        if kind == 0:
            strength[window, tile, at, :] = value
        else:
            push[window, tile, at, :] = value * 0.25
            keep[window, tile, at, :] = jnp.where(value > 0.0, 1.0 - value, 0.0)


def place_sides(refs, early, count, margin, x, y, row):
    last = refs[0].shape[2] - 1
    per = LANES // margin
    wide = lax.broadcasted_iota(jnp.int32, (x.shape[0], LANES), 1)
    from_x_is_east = even("lon")
    for group in range(x.shape[1] // LANES):
        lanes = slice(group * LANES, (group + 1) * LANES)
        x_now, y_now = x[:, lanes], y[:, lanes]
        east = jnp.where(from_x_is_east, x_now, y_now)
        west = jnp.where(from_x_is_east, y_now, x_now)
        for slot in range(min(per, count - group * per)):
            shift = slot * margin
            back = (LANES - margin - shift) % LANES
            e = pltpu.roll(east, LANES - shift, 1) if shift else east
            w = pltpu.roll(west, back, 1) if back else west
            value = jnp.where(wide < margin, e, jnp.where(wide >= LANES - margin, w, 0.0))
            place(refs, early, group * per + slot, last, row, value)


def across(values):
    tiles = len(values)
    lane = lax.broadcasted_iota(jnp.int32, values[0].shape, 1)
    ahead = [pltpu.roll(x, LANES - 1, 1) for x in values]
    behind = [pltpu.roll(x, 1, 1) for x in values]
    return [
        jnp.where(lane == LANES - 1, ahead[(j + 1) % tiles], ahead[j])
        - jnp.where(lane == 0, behind[j - 1], behind[j])
        for j in range(tiles)
    ]


def stress_rows(refs, step, window, row):
    velocity, stress, strength, _, _, _ = refs
    every = range(velocity.shape[2])
    at, north, south = pl.ds(row, 8), pl.ds(row + 1, 8), pl.ds(row - 1, 8)
    u_x = across([velocity[step, 0, j, at, :] for j in every])
    v_x = across([velocity[step, 1, j, at, :] for j in every])
    for j in every:
        u_y = velocity[step, 0, j, north, :] - velocity[step, 0, j, south, :]
        v_y = velocity[step, 1, j, north, :] - velocity[step, 1, j, south, :]
        shear = u_y + v_x[j]
        spread = u_x[j] + v_y
        tension = u_x[j] - v_y
        tension4 = tension * 0.25
        shear4 = shear * 0.25
        squares = spread * spread + tension * tension4 + (shear * shear4 + 1.0)
        k = strength[window, j, at, :]
        kr = k * lax.rsqrt(squares)
        old = [stress[step, i, j, at, :] * (2.0 / 3.0) for i in range(3)]
        stress[step + 1, 0, j, at, :] = old[0] + (kr * (spread + tension4) - k)
        stress[step + 1, 1, j, at, :] = old[1] + (kr * (spread - tension4) - k)
        stress[step + 1, 2, j, at, :] = old[2] + kr * shear4


def velocity_rows(refs, step, window, row):
    velocity, stress, _, keep, push, force = refs
    every = range(velocity.shape[2])
    at, north, south = pl.ds(row, 8), pl.ds(row + 1, 8), pl.ds(row - 1, 8)
    now = step + 1
    p_x = across([stress[now, 0, j, at, :] for j in every])
    t_x = across([stress[now, 2, j, at, :] for j in every])
    for j in every:
        q_y = stress[now, 1, j, north, :] - stress[now, 1, j, south, :]
        t_y = stress[now, 2, j, north, :] - stress[now, 2, j, south, :]
        a = keep[window, j, at, :]
        b = push[window, j, at, :]
        velocity[now, 0, j, at, :] = (
            a * velocity[step, 0, j, at, :] + b * (p_x[j] + t_y) + force[window, 0, j, at, :]
        )
        velocity[now, 1, j, at, :] = (
            a * velocity[step, 1, j, at, :] + b * (t_x[j] + q_y) + force[window, 1, j, at, :]
        )


def interior_kernel(margin, fields_ref, force_ref, lon_x_ref, lon_y_ref, *refs):
    early, rows, cols = fields_ref.shape
    count = early + force_ref.shape[0]
    windows = refs[2].shape[0]
    for field in range(count):
        for tile in range(cols // LANES):
            lanes = slice(tile * LANES, (tile + 1) * LANES)
            own = fields_ref[field, :, lanes] if field < early else force_ref[field - early, :, lanes]
            place(refs, early, field, tile, margin, own)
    lon_x, lon_y = lon_x_ref[...].astype(jnp.float32), lon_y_ref[...].astype(jnp.float32)
    place_sides(refs, early, count, margin, lon_x, lon_y, margin)
    for window in range(windows):
        lost = 2 * SUB * window
        row_list = range(margin + lost, margin + rows - lost, 8)

        def subcycle(number, carry):
            step = window * SUB + number
            for row in row_list:
                stress_rows(refs, step, window, row)
            for row in row_list:
                velocity_rows(refs, step, window, row)
            return carry

        lax.fori_loop(0, SUB, subcycle, 0)


def rim_kernel(margin, early, count, lat_count, *args):
    lat_x_ref, lat_y_ref = args[:2]
    refs = args[2:8]
    velocity_ref, stress_ref = args[8:10]
    velocity, stress = refs[:2]
    windows = refs[2].shape[0]
    _, rows, cols = velocity_ref.shape
    own_tiles = cols // LANES
    bottom = margin + rows
    depths = field_depths(margin, windows)
    groups = message_groups(range(early), depths) + message_groups(range(early, count), depths)
    packed = -(-count // (LANES // margin)) * LANES
    me = lax.axis_index("lat")
    for ref, north in ((lat_x_ref, even("lat")), (lat_y_ref, jnp.logical_not(even("lat")))):
        exists = jnp.where(north, me < lat_count - 1, me > 0)

        def read(at):
            return jnp.where(exists, ref[at].astype(jnp.float32), 0.0)

        row = 0
        for group in groups:
            height = sum(depths[f] for f in group)
            value = read(slice(row, row + height))
            begin = 0
            for field in group:
                depth = depths[field]
                to = pl.multiple_of(jnp.where(north, bottom, margin - depth), 8)
                for tile in range(own_tiles):
                    lanes = slice(tile * LANES, (tile + 1) * LANES)
                    place(refs, early, field, tile, to, value[begin : begin + depth, lanes])
                begin += depth
            row += height
        to = pl.multiple_of(jnp.where(north, bottom, 0), 8)
        east, west = (read(slice(at, at + margin))[:, :packed] for at in (row, row + margin))
        place_sides(refs, early, count, margin, east, west, to)

    def subcycle(step, carry):
        window = step // SUB
        done = 2 * step + 1
        for half, rows_now in ((0, stress_rows), (1, velocity_rows)):
            for first in range(0, margin, 8):
                rows_now(refs, step, window, done + half + first)
                rows_now(refs, step, window, bottom - done - half + first)
        return carry

    steps = SUB * windows
    lax.fori_loop(0, steps, subcycle, 0)

    for tile in range(own_tiles):
        lanes = slice(tile * LANES, (tile + 1) * LANES)
        for row in range(0, rows, 8):
            at = slice(row, row + 8)
            own = slice(margin + row, margin + row + 8)
            velocity_ref[0, at, lanes] = velocity[steps, 0, tile, own, :]
            velocity_ref[1, at, lanes] = velocity[steps, 1, tile, own, :]
            p = stress[steps, 0, tile, own, :]
            q = stress[steps, 1, tile, own, :]
            stress_ref[0, at, lanes] = (p + q) * 0.5
            stress_ref[1, at, lanes] = (p - q) * 0.5
            stress_ref[2, at, lanes] = stress[steps, 2, tile, own, :] * 0.5


def params():
    return pltpu.CompilerParams(vmem_limit_bytes=VMEM_LIMIT)


def lon_swaps(first):
    n = lax.axis_size("lon")
    if n % 2:
        raise ValueError("odd ring")
    pairs = [(i, (i + 1) % n) for i in range(first, n, 2)]
    return pairs + [(j, i) for i, j in pairs]


def lat_swaps(first):
    m, n = lax.axis_size("lat"), lax.axis_size("lon")
    partner = {}
    for i in range(m):
        north = i + 1 if (i - first) % 2 == 0 else i - 1
        for k in range(n):
            to = (north, k) if 0 <= north < m else (i, k ^ 1)
            partner[k * m + i] = to[1] * m + to[0]
    return list(partner.items())


def lon_exchange(x, y):
    return lax.ppermute(x, "lon", lon_swaps(0)), lax.ppermute(y, "lon", lon_swaps(1))


def lat_exchange(x, y):
    axes = ("lon", "lat")
    return lax.ppermute(x, axes, lat_swaps(0)), lax.ppermute(y, axes, lat_swaps(1))


def shape(dims, dtype=jnp.float32):
    return jax.ShapeDtypeStruct(dims, dtype)


def local(
    velocity,
    stress,
    thickness,
    concentration,
    land_mask,
    covered,
    ocean_current,
    wind_stress,
    regrid_weights,
    tile_offset,
):
    _, rows, cols = velocity.shape
    windows = wind_stress.shape[0]
    margin = 2 * SUB * windows
    early = STATE + 2 * windows
    count = early + 2 * windows
    tiles = cols // LANES + 1
    packed = -(-count // (LANES // margin)) * LANES
    depths = field_depths(margin, windows)
    early_rows = sum(depths[:early])
    message_rows = sum(depths)
    bf16 = jnp.bfloat16

    tile_x, tile_y = lat_exchange(ocean_current, ocean_current)

    whole = pl.BlockSpec(memory_space=pltpu.VMEM)
    anywhere = pl.BlockSpec(memory_space=pl.ANY)
    chunks = rows // GROUP
    thick_out, fields, current, side, lon_x, lon_y, lat_x, lat_y = pl.pallas_call(
        functools.partial(local_kernel, margin),
        out_shape=(
            shape(thickness.shape),
            shape((early, rows, cols)),
            shape(wind_stress.shape),
            shape((rows, 2 * rows), bf16),
            shape((rows, packed), bf16),
            shape((rows, packed), bf16),
            shape((early_rows, cols), bf16),
            shape((early_rows, cols), bf16),
        ),
        in_specs=[anywhere] * 10,
        out_specs=(anywhere,) + (whole,) * 7,
        scratch_shapes=[
            pltpu.SMEM(covered.shape, jnp.int32),
            pltpu.VMEM((1, rows), jnp.int32),
            pltpu.VMEM(regrid_weights.shape, bf16),
            pltpu.VMEM(thickness.shape, jnp.float32),
            pltpu.VMEM(thickness.shape, jnp.float32),
            pltpu.VMEM(land_mask.shape, jnp.int32),
            pltpu.VMEM(velocity.shape, jnp.float32),
            pltpu.VMEM(stress.shape, jnp.float32),
            pltpu.VMEM(ocean_current.shape, bf16),
            pltpu.VMEM(wind_stress.shape, bf16),
            pltpu.SemaphoreType.DMA((8,)),
            pltpu.SemaphoreType.DMA((chunks,)),
            pltpu.SemaphoreType.DMA((chunks,)),
            pltpu.SemaphoreType.DMA((chunks,)),
        ],
        compiler_params=params(),
        cost_estimate=pl.CostEstimate(
            flops=100 * thickness.size, bytes_accessed=12 * thickness.size, transcendentals=0
        ),
        name="local",
    )(
        *(
            pltpu.with_memory_space_constraint(x, pltpu.HBM)
            for x in (
                covered,
                tile_offset.reshape(1, rows),
                regrid_weights,
                thickness,
                concentration,
                land_mask,
                velocity,
                stress,
                ocean_current,
                wind_stress,
            )
        )
    )

    force, lon_x, lon_y, lat_x, lat_y = pl.pallas_call(
        functools.partial(force_kernel, margin, early),
        out_shape=(
            shape((2 * windows, rows, cols)),
            shape((rows, packed), bf16),
            shape((rows, packed), bf16),
            shape((message_rows + 2 * margin, cols), bf16),
            shape((message_rows + 2 * margin, cols), bf16),
        ),
        in_specs=[whole] * 9,
        out_specs=(whole,) * 5,
        compiler_params=params(),
        name="force",
    )(side, tile_x, tile_y, current, fields, lon_x, lon_y, lat_x, lat_y)

    lon_x, lon_y = lon_exchange(lon_x, lon_y)
    north_end = rows - margin
    start_x = jnp.where(even("lat"), north_end, 0)
    for number, part in enumerate((lon_x, lon_y)):
        at = message_rows + number * margin
        corner_x = lax.dynamic_slice_in_dim(part, start_x, margin, 0)
        corner_y = lax.dynamic_slice_in_dim(part, north_end - start_x, margin, 0)
        lat_x = lat_x.at[at : at + margin, :packed].set(corner_x)
        lat_y = lat_y.at[at : at + margin, :packed].set(corner_y)
    lat_x, lat_y = lat_exchange(lat_x, lat_y)

    steps = SUB * windows

    def widened(*lead):
        return shape((*lead, tiles, rows + 2 * margin, LANES))

    domain = (
        widened(steps + 1, 2),
        widened(steps + 1, 3),
        widened(windows),
        widened(windows),
        widened(windows),
        widened(windows, 2),
    )
    refs = pl.pallas_call(
        functools.partial(interior_kernel, margin),
        out_shape=domain,
        in_specs=[whole] * 4,
        out_specs=(whole,) * 6,
        compiler_params=params(),
        cost_estimate=pl.CostEstimate(
            flops=60 * steps * rows * cols, bytes_accessed=2**22, transcendentals=0
        ),
        name="interior",
    )(fields, force, lon_x, lon_y)

    velocity_out, stress_out = pl.pallas_call(
        functools.partial(rim_kernel, margin, early, count, lax.axis_size("lat")),
        out_shape=(shape(velocity.shape), shape(stress.shape)) + domain,
        in_specs=[whole] * 8,
        out_specs=(whole,) * 8,
        input_output_aliases={2 + i: 2 + i for i in range(6)},
        compiler_params=params(),
        name="rim",
    )(lat_x, lat_y, *refs)[:2]
    return (velocity_out, stress_out, thick_out)


def solution(mesh):
    return jax.shard_map(
        local,
        mesh=mesh,
        in_specs=(
            P(None, "lat", "lon"),
            P(None, "lat", "lon"),
            P(None, "lat", "lon"),
            P(None, "lat", "lon"),
            P("lat", "lon"),
            P("lat", None),
            P(None, None, "lat", "lon"),
            P(None, None, "lat", "lon"),
            P("lat", None),
            P("lat"),
        ),
        out_specs=(P(None, "lat", "lon"), P(None, "lat", "lon"), P(None, "lat", "lon")),
        check_vma=False,
    )
```

```python
import functools

import jax
import jax.numpy as jnp
from jax import lax
from jax.experimental import pallas as pl
from jax.experimental.pallas import tpu as pltpu
from jax.sharding import PartitionSpec as P

BLK = 128
SUB = 4
LANES = 128
GROUP = 16
STATE = 5
VMEM_LIMIT = 16 * 1024 * 1024

growth_rate = 0.3
mixing_rate = 0.3


def total(terms):
    result = terms[0]
    for term in terms[1:]:
        result = result + term
    return result


def field_depths(margin, windows):
    depths = [margin] * STATE
    for copies in (2, 2):
        for window in range(windows):
            depths += [margin - 2 * SUB * window] * copies
    return depths


def message_groups(fields, depths):
    groups, held = [], []
    for field in fields:
        held.append(field)
        if sum(depths[f] for f in held) % GROUP == 0:
            groups.append(held)
            held = []
    return groups + ([held] if held else [])


def even(axis):
    return lax.axis_index(axis) % 2 == 0


def pack_rows(message_ref, row, groups, depths, value_of, northward, rows):
    for group in groups:
        parts = []
        for field in group:
            start = jnp.where(northward, rows - depths[field], 0)
            parts.append(value_of(field, pl.ds(pl.multiple_of(start, 8), depths[field])))
        value = parts[0] if len(parts) == 1 else jnp.concatenate(parts, axis=0)
        message_ref[row : row + value.shape[0]] = value.astype(jnp.bfloat16)
        row += value.shape[0]
    return row


def local_kernel(
    margin,
    covered_hbm,
    offset_hbm,
    weights_hbm,
    thick_hbm,
    conc_hbm,
    mask_hbm,
    velocity_hbm,
    stress_hbm,
    ocean_hbm,
    wind_hbm,
    thick_out_hbm,
    fields_ref,
    current_ref,
    side_ref,
    lon_x_ref,
    lon_y_ref,
    lat_x_ref,
    lat_y_ref,
    covered,
    offset,
    weights,
    thick,
    conc,
    mask_in,
    velocity,
    stress,
    ocean,
    wind,
    in_sems,
    thick_sems,
    conc_sems,
    out_sems,
):
    cats, rows, cols = thick.shape
    windows = wind.shape[0]
    step = GROUP
    chunks = rows // step

    def rows_of(chunk):
        return pl.ds(chunk * step, step)

    small = [
        pltpu.make_async_copy(source, target, in_sems.at[i])
        for i, (source, target) in enumerate(
            (
                (covered_hbm, covered),
                (mask_hbm, mask_in),
                (velocity_hbm, velocity),
                (stress_hbm, stress),
                (ocean_hbm, ocean),
                (wind_hbm, wind),
                (weights_hbm, weights),
                (offset_hbm, offset),
            )
        )
    ]
    pairs = [
        [
            pltpu.make_async_copy(hbm.at[:, rows_of(c)], vmem.at[:, rows_of(c)], sems.at[c])
            for hbm, vmem, sems in ((thick_hbm, thick, thick_sems), (conc_hbm, conc, conc_sems))
        ]
        for c in range(chunks)
    ]
    writes = [
        pltpu.make_async_copy(thick.at[:, rows_of(c)], thick_out_hbm.at[:, rows_of(c)], out_sems.at[c])
        for c in range(chunks)
    ]
    for copy in small[:2] + [copy for pair in pairs for copy in pair] + small[2:]:
        copy.start()

    blocks = cols // BLK
    first = lax.axis_index("lon") * blocks
    small[0].wait()
    live = [covered[0, first + block] > 0 for block in range(blocks)]
    small[1].wait()
    for c in range(chunks):
        at = slice(c * step, (c + 1) * step)
        for copy in pairs[c]:
            copy.wait()
        for block in range(blocks):
            lanes = slice(block * BLK, (block + 1) * BLK)
            part = [conc[k, at, lanes] for k in range(cats)]
            height = [thick[k, at, lanes] for k in range(cats)]
            mask = mask_in[at, lanes].astype(jnp.float32)
            area = total(part)
            inverse = 1.0 / area
            factor = jnp.exp(-2.0 * (1.0 - area)) * (mask * (1.0 / 3.0))
            half = 0.5 * mask
            volume = total([a * h for a, h in zip(part, height)])
            for window in range(windows):
                mean = volume * inverse
                grown = [h + growth_rate / (0.5 + h) + mixing_rate * (mean - h) for h in height]
                height = [jnp.where(live[block], g, h) for g, h in zip(grown, height)]
                volume = total([a * h for a, h in zip(part, height)])
                fields_ref[STATE + 2 * window, at, lanes] = volume * factor
                fields_ref[STATE + 2 * window + 1, at, lanes] = half / (volume + 1.0)
            for k in range(cats):
                thick[k, at, lanes] = height[k]
        writes[c].start()

    small[2].wait()
    small[3].wait()
    for row in range(0, rows, step):
        at = slice(row, row + step)
        mask = mask_in[at].astype(jnp.float32)
        fields_ref[0, at] = velocity[0, at]
        fields_ref[1, at] = velocity[1, at]
        fields_ref[2, at] = (stress[0, at] + stress[1, at]) * mask
        fields_ref[3, at] = (stress[0, at] - stress[1, at]) * mask
        fields_ref[4, at] = (stress[2, at] + stress[2, at]) * mask

    count = fields_ref.shape[0]
    per = LANES // margin
    slot_of_lane = lax.broadcasted_iota(jnp.int32, (rows, LANES), 1) // margin
    eastward = even("lon")
    for group in range(lon_x_ref.shape[1] // LANES):
        east = jnp.zeros((rows, LANES), jnp.float32)
        west = jnp.zeros((rows, LANES), jnp.float32)
        for slot in range(min(per, count - group * per)):
            field = group * per + slot
            east, west = add_slot(
                east, west, fields_ref.at[field], slot_of_lane == slot, slot * margin, margin
            )
        store_sides(lon_x_ref, lon_y_ref, group, east, west, eastward)
    depths = field_depths(margin, windows)
    groups = message_groups(range(count), depths)
    northward = even("lat")

    def value_of(field, at):
        return fields_ref[field, at, :]

    pack_rows(lat_x_ref, 0, groups, depths, value_of, northward, rows)
    pack_rows(lat_y_ref, 0, groups, depths, value_of, jnp.logical_not(northward), rows)

    for copy in small[4:]:
        copy.wait()
    own_weights = weights[:, :rows]
    for w in range(windows):
        for k in range(2):
            current_ref[w, k] = wind[w, k].astype(jnp.float32) + jnp.dot(
                own_weights, ocean[w, k], preferred_element_type=jnp.float32
            )
    square = (rows, rows)
    diagonal = lax.broadcasted_iota(jnp.int32, square, 0) == lax.broadcasted_iota(
        jnp.int32, square, 1
    )
    up = offset[...] > 0
    for number, north in enumerate((northward, jnp.logical_not(northward))):
        wanted = jnp.where(north, up.astype(jnp.int32), 1 - up.astype(jnp.int32)) > 0
        pick = jnp.where(diagonal & wanted, 1.0, 0.0).astype(jnp.bfloat16)
        side_ref[:, number * rows : (number + 1) * rows] = jnp.dot(
            pick, weights[:, rows:], preferred_element_type=jnp.float32
        ).astype(jnp.bfloat16)

    for copy in writes:
        copy.wait()


def add_slot(east, west, field_ref, here, shift, margin):
    cols = field_ref.shape[1]
    last = pltpu.roll(field_ref[:, cols - LANES :], (shift + margin) % LANES, 1)
    leading = field_ref[:, :LANES]
    if shift:
        leading = pltpu.roll(leading, shift, 1)
    return jnp.where(here, last, east), jnp.where(here, leading, west)


def store_sides(x_ref, y_ref, group, east, west, eastward):
    lanes = slice(group * LANES, (group + 1) * LANES)
    x_ref[:, lanes] = jnp.where(eastward, east, west).astype(jnp.bfloat16)
    y_ref[:, lanes] = jnp.where(eastward, west, east).astype(jnp.bfloat16)


def force_kernel(
    margin,
    early,
    side_ref,
    tile_x_ref,
    tile_y_ref,
    current_ref,
    fields_ref,
    lon_x_in,
    lon_y_in,
    lat_x_in,
    lat_y_in,
    force_ref,
    lon_x_ref,
    lon_y_ref,
    lat_x_ref,
    lat_y_ref,
):
    windows, _, rows, cols = current_ref.shape
    side_x = side_ref[:, :rows]
    side_y = side_ref[:, rows:]

    def dot(a, b):
        return jnp.dot(a, b, preferred_element_type=jnp.float32)

    for w in range(windows):
        b = fields_ref[STATE + 2 * w + 1]
        for k in range(2):
            current = dot(side_x, tile_x_ref[w, k]) + dot(side_y, tile_y_ref[w, k])
            force_ref[2 * w + k] = b * (current_ref[w, k] + current)

    per = LANES // margin
    count = early + force_ref.shape[0]
    slot_of_lane = lax.broadcasted_iota(jnp.int32, (rows, LANES), 1) // margin
    eastward = even("lon")
    for group in range(lon_x_ref.shape[1] // LANES):
        lanes = slice(group * LANES, (group + 1) * LANES)
        x = lon_x_in[:, lanes].astype(jnp.float32)
        y = lon_y_in[:, lanes].astype(jnp.float32)
        east, west = jnp.where(eastward, x, y), jnp.where(eastward, y, x)
        for field in range(max(early, group * per), min(count, (group + 1) * per)):
            slot = field - group * per
            east, west = add_slot(
                east, west, force_ref.at[field - early], slot_of_lane == slot, slot * margin, margin
            )
        store_sides(lon_x_ref, lon_y_ref, group, east, west, eastward)

    depths = field_depths(margin, windows)
    groups = message_groups(range(early, count), depths)
    northward = even("lat")

    def value_of(field, at):
        return force_ref[field - early, at, :]

    for old_ref, ref, north in (
        (lat_x_in, lat_x_ref, northward),
        (lat_y_in, lat_y_ref, jnp.logical_not(northward)),
    ):
        row = old_ref.shape[0]
        ref[:row] = old_ref[...]
        row = pack_rows(ref, row, groups, depths, value_of, north, rows)
        ref[row:] = jnp.zeros((ref.shape[0] - row, cols), jnp.bfloat16)


def place(refs, early, field, tile, row, value):
    velocity, stress, strength, keep, push, force = refs
    at = pl.ds(row, value.shape[0])
    if field < 2:
        velocity[0, field, tile, at, :] = value
    elif field < STATE:
        stress[0, field - 2, tile, at, :] = value
    elif field >= early:
        window, kind = divmod(field - early, 2)
        force[window, kind, tile, at, :] = value
    else:
        window, kind = divmod(field - STATE, 2)
        if kind == 0:
            strength[window, tile, at, :] = value
        else:
            push[window, tile, at, :] = value * 0.25
            keep[window, tile, at, :] = jnp.where(value > 0.0, 1.0 - value, 0.0)


def place_sides(refs, early, count, margin, x, y, row):
    last = refs[0].shape[2] - 1
    per = LANES // margin
    wide = lax.broadcasted_iota(jnp.int32, (x.shape[0], LANES), 1)
    from_x_is_east = even("lon")
    for group in range(x.shape[1] // LANES):
        lanes = slice(group * LANES, (group + 1) * LANES)
        x_now, y_now = x[:, lanes], y[:, lanes]
        east = jnp.where(from_x_is_east, x_now, y_now)
        west = jnp.where(from_x_is_east, y_now, x_now)
        for slot in range(min(per, count - group * per)):
            shift = slot * margin
            back = (LANES - margin - shift) % LANES
            e = pltpu.roll(east, LANES - shift, 1) if shift else east
            w = pltpu.roll(west, back, 1) if back else west
            value = jnp.where(wide < margin, e, jnp.where(wide >= LANES - margin, w, 0.0))
            place(refs, early, group * per + slot, last, row, value)


def across(values):
    tiles = len(values)
    lane = lax.broadcasted_iota(jnp.int32, values[0].shape, 1)
    ahead = [pltpu.roll(x, LANES - 1, 1) for x in values]
    behind = [pltpu.roll(x, 1, 1) for x in values]
    return [
        jnp.where(lane == LANES - 1, ahead[(j + 1) % tiles], ahead[j])
        - jnp.where(lane == 0, behind[j - 1], behind[j])
        for j in range(tiles)
    ]


def stress_rows(refs, step, window, row):
    velocity, stress, strength, _, _, _ = refs
    every = range(velocity.shape[2])
    at, north, south = pl.ds(row, 8), pl.ds(row + 1, 8), pl.ds(row - 1, 8)
    u_x = across([velocity[step, 0, j, at, :] for j in every])
    v_x = across([velocity[step, 1, j, at, :] for j in every])
    for j in every:
        u_y = velocity[step, 0, j, north, :] - velocity[step, 0, j, south, :]
        v_y = velocity[step, 1, j, north, :] - velocity[step, 1, j, south, :]
        shear = u_y + v_x[j]
        spread = u_x[j] + v_y
        tension = u_x[j] - v_y
        tension4 = tension * 0.25
        shear4 = shear * 0.25
        squares = spread * spread + tension * tension4 + (shear * shear4 + 1.0)
        k = strength[window, j, at, :]
        kr = k * lax.rsqrt(squares)
        old = [stress[step, i, j, at, :] * (2.0 / 3.0) for i in range(3)]
        stress[step + 1, 0, j, at, :] = old[0] + (kr * (spread + tension4) - k)
        stress[step + 1, 1, j, at, :] = old[1] + (kr * (spread - tension4) - k)
        stress[step + 1, 2, j, at, :] = old[2] + kr * shear4


def velocity_rows(refs, step, window, row):
    velocity, stress, _, keep, push, force = refs
    every = range(velocity.shape[2])
    at, north, south = pl.ds(row, 8), pl.ds(row + 1, 8), pl.ds(row - 1, 8)
    now = step + 1
    p_x = across([stress[now, 0, j, at, :] for j in every])
    t_x = across([stress[now, 2, j, at, :] for j in every])
    for j in every:
        q_y = stress[now, 1, j, north, :] - stress[now, 1, j, south, :]
        t_y = stress[now, 2, j, north, :] - stress[now, 2, j, south, :]
        a = keep[window, j, at, :]
        b = push[window, j, at, :]
        velocity[now, 0, j, at, :] = (
            a * velocity[step, 0, j, at, :] + b * (p_x[j] + t_y) + force[window, 0, j, at, :]
        )
        velocity[now, 1, j, at, :] = (
            a * velocity[step, 1, j, at, :] + b * (t_x[j] + q_y) + force[window, 1, j, at, :]
        )


def write_rows(refs, out_hbm, stage, sem, margin, begin, height):
    velocity, stress = refs[:2]
    steps = velocity.shape[0] - 1
    for tile in range(stage.shape[2] // LANES):
        lanes = slice(tile * LANES, (tile + 1) * LANES)
        for row in range(0, height, 8):
            to = slice(row, row + 8)
            at = slice(margin + begin + row, margin + begin + row + 8)
            p, q, t = (stress[steps, i, tile, at, :] for i in range(3))
            stage[0, to, lanes] = velocity[steps, 0, tile, at, :]
            stage[1, to, lanes] = velocity[steps, 1, tile, at, :]
            stage[2, to, lanes] = (p + q) * 0.5
            stage[3, to, lanes] = (p - q) * 0.5
            stage[4, to, lanes] = t * 0.5
    copies = [
        pltpu.make_async_copy(
            stage.at[first : first + hbm.shape[0]], hbm.at[:, pl.ds(begin, height)], sem.at[i]
        )
        for i, (first, hbm) in enumerate(zip((0, 2), out_hbm))
    ]
    for copy in copies:
        copy.start()
    return copies


def interior_kernel(margin, fields_ref, force_ref, lon_x_ref, lon_y_ref, *args):
    refs, out_hbm, (stage, sem) = args[:6], args[6:8], args[8:]
    early, rows, cols = fields_ref.shape
    count = early + force_ref.shape[0]
    windows = refs[2].shape[0]
    for field in range(count):
        for tile in range(cols // LANES):
            lanes = slice(tile * LANES, (tile + 1) * LANES)
            own = fields_ref[field, :, lanes] if field < early else force_ref[field - early, :, lanes]
            place(refs, early, field, tile, margin, own)
    lon_x, lon_y = lon_x_ref[...].astype(jnp.float32), lon_y_ref[...].astype(jnp.float32)
    place_sides(refs, early, count, margin, lon_x, lon_y, margin)
    for window in range(windows):
        lost = 2 * SUB * window
        row_list = range(margin + lost, margin + rows - lost, 8)

        def subcycle(number, carry):
            step = window * SUB + number
            for row in row_list:
                stress_rows(refs, step, window, row)
            for row in row_list:
                velocity_rows(refs, step, window, row)
            return carry

        lax.fori_loop(0, SUB, subcycle, 0)

    for copy in write_rows(refs, out_hbm, stage, sem, margin, margin, rows - 2 * margin):
        copy.wait()


def rim_kernel(margin, early, count, lat_count, *args):
    lat_x_ref, lat_y_ref = args[:2]
    refs = args[2:8]
    out_hbm = args[16:18]
    stages, sems = args[18:20], args[20]
    windows = refs[2].shape[0]
    _, rows, cols = out_hbm[0].shape
    own_tiles = cols // LANES
    bottom = margin + rows
    depths = field_depths(margin, windows)
    groups = message_groups(range(early), depths) + message_groups(range(early, count), depths)
    packed = -(-count // (LANES // margin)) * LANES
    me = lax.axis_index("lat")
    for ref, north in ((lat_x_ref, even("lat")), (lat_y_ref, jnp.logical_not(even("lat")))):
        exists = jnp.where(north, me < lat_count - 1, me > 0)

        def read(at):
            return jnp.where(exists, ref[at].astype(jnp.float32), 0.0)

        row = 0
        for group in groups:
            height = sum(depths[f] for f in group)
            value = read(slice(row, row + height))
            begin = 0
            for field in group:
                depth = depths[field]
                to = pl.multiple_of(jnp.where(north, bottom, margin - depth), 8)
                for tile in range(own_tiles):
                    lanes = slice(tile * LANES, (tile + 1) * LANES)
                    place(refs, early, field, tile, to, value[begin : begin + depth, lanes])
                begin += depth
            row += height
        to = pl.multiple_of(jnp.where(north, bottom, 0), 8)
        east, west = (read(slice(at, at + margin))[:, :packed] for at in (row, row + margin))
        place_sides(refs, early, count, margin, east, west, to)

    for step in range(SUB * windows):
        window = step // SUB
        done = 2 * step + 1
        for half, rows_now in ((0, stress_rows), (1, velocity_rows)):
            for first in range(0, margin, 8):
                rows_now(refs, step, window, done + half + first)
                rows_now(refs, step, window, bottom - done - half + first)

    copies = []
    for number, begin in enumerate((0, rows - margin)):
        copies += write_rows(
            refs, out_hbm, stages[number], sems.at[number], margin, begin, margin
        )
    for copy in copies:
        copy.wait()


def params():
    return pltpu.CompilerParams(vmem_limit_bytes=VMEM_LIMIT)


def lon_swaps(first):
    n = lax.axis_size("lon")
    if n % 2:
        raise ValueError("odd ring")
    pairs = [(i, (i + 1) % n) for i in range(first, n, 2)]
    return pairs + [(j, i) for i, j in pairs]


def lat_swaps(first):
    m, n = lax.axis_size("lat"), lax.axis_size("lon")
    partner = {}
    for i in range(m):
        north = i + 1 if (i - first) % 2 == 0 else i - 1
        for k in range(n):
            to = (north, k) if 0 <= north < m else (i, k ^ 1)
            partner[k * m + i] = to[1] * m + to[0]
    return list(partner.items())


def lon_exchange(x, y):
    return lax.ppermute(x, "lon", lon_swaps(0)), lax.ppermute(y, "lon", lon_swaps(1))


def lat_exchange(x, y):
    axes = ("lon", "lat")
    return lax.ppermute(x, axes, lat_swaps(0)), lax.ppermute(y, axes, lat_swaps(1))


def shape(dims, dtype=jnp.float32):
    return jax.ShapeDtypeStruct(dims, dtype)


def local(
    velocity,
    stress,
    thickness,
    concentration,
    land_mask,
    covered,
    ocean_current,
    wind_stress,
    regrid_weights,
    tile_offset,
):
    _, rows, cols = velocity.shape
    windows = wind_stress.shape[0]
    margin = 2 * SUB * windows
    early = STATE + 2 * windows
    count = early + 2 * windows
    tiles = cols // LANES + 1
    packed = -(-count // (LANES // margin)) * LANES
    depths = field_depths(margin, windows)
    early_rows = sum(depths[:early])
    message_rows = sum(depths)
    bf16 = jnp.bfloat16

    tile_x, tile_y = lat_exchange(ocean_current, ocean_current)

    whole = pl.BlockSpec(memory_space=pltpu.VMEM)
    anywhere = pl.BlockSpec(memory_space=pl.ANY)
    chunks = rows // GROUP
    thick_out, fields, current, side, lon_x, lon_y, lat_x, lat_y = pl.pallas_call(
        functools.partial(local_kernel, margin),
        out_shape=(
            shape(thickness.shape),
            shape((early, rows, cols)),
            shape(wind_stress.shape),
            shape((rows, 2 * rows), bf16),
            shape((rows, packed), bf16),
            shape((rows, packed), bf16),
            shape((early_rows, cols), bf16),
            shape((early_rows, cols), bf16),
        ),
        in_specs=[anywhere] * 10,
        out_specs=(anywhere,) + (whole,) * 7,
        scratch_shapes=[
            pltpu.SMEM(covered.shape, jnp.int32),
            pltpu.VMEM((1, rows), jnp.int32),
            pltpu.VMEM(regrid_weights.shape, bf16),
            pltpu.VMEM(thickness.shape, jnp.float32),
            pltpu.VMEM(thickness.shape, jnp.float32),
            pltpu.VMEM(land_mask.shape, jnp.int32),
            pltpu.VMEM(velocity.shape, jnp.float32),
            pltpu.VMEM(stress.shape, jnp.float32),
            pltpu.VMEM(ocean_current.shape, bf16),
            pltpu.VMEM(wind_stress.shape, bf16),
            pltpu.SemaphoreType.DMA((8,)),
            pltpu.SemaphoreType.DMA((chunks,)),
            pltpu.SemaphoreType.DMA((chunks,)),
            pltpu.SemaphoreType.DMA((chunks,)),
        ],
        compiler_params=params(),
        cost_estimate=pl.CostEstimate(
            flops=100 * thickness.size, bytes_accessed=12 * thickness.size, transcendentals=0
        ),
        name="local",
    )(
        *(
            pltpu.with_memory_space_constraint(x, pltpu.HBM)
            for x in (
                covered,
                tile_offset.reshape(1, rows),
                regrid_weights,
                thickness,
                concentration,
                land_mask,
                velocity,
                stress,
                ocean_current,
                wind_stress,
            )
        )
    )

    force, lon_x, lon_y, lat_x, lat_y = pl.pallas_call(
        functools.partial(force_kernel, margin, early),
        out_shape=(
            shape((2 * windows, rows, cols)),
            shape((rows, packed), bf16),
            shape((rows, packed), bf16),
            shape((message_rows + 2 * margin, cols), bf16),
            shape((message_rows + 2 * margin, cols), bf16),
        ),
        in_specs=[whole] * 9,
        out_specs=(whole,) * 5,
        compiler_params=params(),
        name="force",
    )(side, tile_x, tile_y, current, fields, lon_x, lon_y, lat_x, lat_y)

    lon_x, lon_y = lon_exchange(lon_x, lon_y)
    north_end = rows - margin
    start_x = jnp.where(even("lat"), north_end, 0)
    for number, part in enumerate((lon_x, lon_y)):
        at = message_rows + number * margin
        corner_x = lax.dynamic_slice_in_dim(part, start_x, margin, 0)
        corner_y = lax.dynamic_slice_in_dim(part, north_end - start_x, margin, 0)
        lat_x = lat_x.at[at : at + margin, :packed].set(corner_x)
        lat_y = lat_y.at[at : at + margin, :packed].set(corner_y)
    lat_x, lat_y = lat_exchange(lat_x, lat_y)

    steps = SUB * windows

    def widened(*lead):
        return shape((*lead, tiles, rows + 2 * margin, LANES))

    domain = (
        widened(steps + 1, 2),
        widened(steps + 1, 3),
        widened(windows),
        widened(windows),
        widened(windows),
        widened(windows, 2),
    )
    outs = (shape(velocity.shape), shape(stress.shape))
    refs = pl.pallas_call(
        functools.partial(interior_kernel, margin),
        out_shape=domain + outs,
        in_specs=[whole] * 4,
        out_specs=(whole,) * 6 + (anywhere,) * 2,
        scratch_shapes=[
            pltpu.VMEM((STATE, rows - 2 * margin, cols), jnp.float32),
            pltpu.SemaphoreType.DMA((2,)),
        ],
        compiler_params=params(),
        cost_estimate=pl.CostEstimate(
            flops=60 * steps * rows * cols, bytes_accessed=2**22, transcendentals=0
        ),
        name="interior",
    )(fields, force, lon_x, lon_y)

    velocity_out, stress_out = pl.pallas_call(
        functools.partial(rim_kernel, margin, early, count, lax.axis_size("lat")),
        out_shape=domain + outs,
        in_specs=[whole] * 8 + [anywhere] * 2,
        out_specs=(whole,) * 6 + (anywhere,) * 2,
        input_output_aliases={2 + i: i for i in range(8)},
        scratch_shapes=[
            pltpu.VMEM((STATE, margin, cols), jnp.float32),
            pltpu.VMEM((STATE, margin, cols), jnp.float32),
            pltpu.SemaphoreType.DMA((2, 2)),
        ],
        compiler_params=params(),
        name="rim",
    )(lat_x, lat_y, *refs)[6:]
    return (velocity_out, stress_out, thick_out)


def solution(mesh):
    return jax.shard_map(
        local,
        mesh=mesh,
        in_specs=(
            P(None, "lat", "lon"),
            P(None, "lat", "lon"),
            P(None, "lat", "lon"),
            P(None, "lat", "lon"),
            P("lat", "lon"),
            P("lat", None),
            P(None, None, "lat", "lon"),
            P(None, None, "lat", "lon"),
            P("lat", None),
            P("lat"),
        ),
        out_specs=(P(None, "lat", "lon"), P(None, "lat", "lon"), P(None, "lat", "lon")),
        check_vma=False,
    )
```

```python
import functools

import jax
import jax.numpy as jnp
from jax import lax
from jax.experimental import pallas as pl
from jax.experimental.pallas import tpu as pltpu
from jax.sharding import PartitionSpec as P

BLK = 128
SUB = 4
LANES = 128
GROUP = 16
STATE = 5
VMEM_LIMIT = 16 * 1024 * 1024

growth_rate = 0.3
mixing_rate = 0.3


def total(terms):
    result = terms[0]
    for term in terms[1:]:
        result = result + term
    return result


def field_depths(margin, windows):
    depths = [margin] * STATE
    for copies in (2, 2):
        for window in range(windows):
            depths += [margin - 2 * SUB * window] * copies
    return depths


def message_groups(fields, depths):
    groups, held = [], []
    for field in fields:
        held.append(field)
        if sum(depths[f] for f in held) % GROUP == 0:
            groups.append(held)
            held = []
    return groups + ([held] if held else [])


def even(axis):
    return lax.axis_index(axis) % 2 == 0


def pack_rows(message_ref, row, groups, depths, value_of, northward, rows):
    for group in groups:
        parts = []
        for field in group:
            start = jnp.where(northward, rows - depths[field], 0)
            parts.append(value_of(field, pl.ds(pl.multiple_of(start, 8), depths[field])))
        value = parts[0] if len(parts) == 1 else jnp.concatenate(parts, axis=0)
        message_ref[row : row + value.shape[0]] = value.astype(jnp.bfloat16)
        row += value.shape[0]
    return row


def local_kernel(
    margin,
    covered_hbm,
    offset_hbm,
    weights_hbm,
    thick_hbm,
    conc_hbm,
    mask_hbm,
    velocity_hbm,
    stress_hbm,
    ocean_hbm,
    wind_hbm,
    thick_out_hbm,
    fields_ref,
    current_ref,
    side_ref,
    lon_x_ref,
    lon_y_ref,
    lat_x_ref,
    lat_y_ref,
    covered,
    offset,
    weights,
    thick,
    conc,
    mask_in,
    velocity,
    stress,
    ocean,
    wind,
    in_sems,
    thick_sems,
    conc_sems,
    out_sems,
):
    cats, rows, cols = thick.shape
    windows = wind.shape[0]
    step = GROUP
    chunks = rows // step

    def rows_of(chunk):
        return pl.ds(chunk * step, step)

    small = [
        pltpu.make_async_copy(source, target, in_sems.at[i])
        for i, (source, target) in enumerate(
            (
                (covered_hbm, covered),
                (mask_hbm, mask_in),
                (velocity_hbm, velocity),
                (stress_hbm, stress),
                (ocean_hbm, ocean),
                (wind_hbm, wind),
                (weights_hbm, weights),
                (offset_hbm, offset),
            )
        )
    ]
    pairs = [
        [
            pltpu.make_async_copy(hbm.at[:, rows_of(c)], vmem.at[:, rows_of(c)], sems.at[c])
            for hbm, vmem, sems in ((thick_hbm, thick, thick_sems), (conc_hbm, conc, conc_sems))
        ]
        for c in range(chunks)
    ]
    writes = [
        pltpu.make_async_copy(thick.at[:, rows_of(c)], thick_out_hbm.at[:, rows_of(c)], out_sems.at[c])
        for c in range(chunks)
    ]
    for copy in small[:2] + [copy for pair in pairs for copy in pair] + small[2:]:
        copy.start()

    blocks = cols // BLK
    first = lax.axis_index("lon") * blocks
    small[0].wait()
    live = [covered[0, first + block] > 0 for block in range(blocks)]
    small[1].wait()
    for c in range(chunks):
        at = slice(c * step, (c + 1) * step)
        for copy in pairs[c]:
            copy.wait()
        for block in range(blocks):
            lanes = slice(block * BLK, (block + 1) * BLK)
            part = [conc[k, at, lanes] for k in range(cats)]
            height = [thick[k, at, lanes] for k in range(cats)]
            mask = mask_in[at, lanes].astype(jnp.float32)
            area = total(part)
            inverse = 1.0 / area
            factor = jnp.exp(-2.0 * (1.0 - area)) * (mask * (1.0 / 3.0))
            half = 0.5 * mask
            volume = total([a * h for a, h in zip(part, height)])
            for window in range(windows):
                mean = volume * inverse
                grown = [h + growth_rate / (0.5 + h) + mixing_rate * (mean - h) for h in height]
                height = [jnp.where(live[block], g, h) for g, h in zip(grown, height)]
                volume = total([a * h for a, h in zip(part, height)])
                fields_ref[STATE + 2 * window, at, lanes] = volume * factor
                fields_ref[STATE + 2 * window + 1, at, lanes] = half / (volume + 1.0)
            for k in range(cats):
                thick[k, at, lanes] = height[k]
        writes[c].start()

    small[2].wait()
    small[3].wait()
    for row in range(0, rows, step):
        at = slice(row, row + step)
        mask = mask_in[at].astype(jnp.float32)
        fields_ref[0, at] = velocity[0, at]
        fields_ref[1, at] = velocity[1, at]
        fields_ref[2, at] = (stress[0, at] + stress[1, at]) * mask
        fields_ref[3, at] = (stress[0, at] - stress[1, at]) * mask
        fields_ref[4, at] = (stress[2, at] + stress[2, at]) * mask

    count = fields_ref.shape[0]
    per = LANES // margin
    slot_of_lane = lax.broadcasted_iota(jnp.int32, (rows, LANES), 1) // margin
    eastward = even("lon")
    for group in range(lon_x_ref.shape[1] // LANES):
        east = jnp.zeros((rows, LANES), jnp.float32)
        west = jnp.zeros((rows, LANES), jnp.float32)
        for slot in range(min(per, count - group * per)):
            field = group * per + slot
            east, west = add_slot(
                east, west, fields_ref.at[field], slot_of_lane == slot, slot * margin, margin
            )
        store_sides(lon_x_ref, lon_y_ref, group, east, west, eastward)
    depths = field_depths(margin, windows)
    groups = message_groups(range(count), depths)
    northward = even("lat")

    def value_of(field, at):
        return fields_ref[field, at, :]

    pack_rows(lat_x_ref, 0, groups, depths, value_of, northward, rows)
    pack_rows(lat_y_ref, 0, groups, depths, value_of, jnp.logical_not(northward), rows)

    for copy in small[4:]:
        copy.wait()
    own_weights = weights[:, :rows]
    for w in range(windows):
        for k in range(2):
            current_ref[w, k] = wind[w, k].astype(jnp.float32) + jnp.dot(
                own_weights, ocean[w, k], preferred_element_type=jnp.float32
            )
    square = (rows, rows)
    diagonal = lax.broadcasted_iota(jnp.int32, square, 0) == lax.broadcasted_iota(
        jnp.int32, square, 1
    )
    up = offset[...] > 0
    for number, north in enumerate((northward, jnp.logical_not(northward))):
        wanted = jnp.where(north, up.astype(jnp.int32), 1 - up.astype(jnp.int32)) > 0
        pick = jnp.where(diagonal & wanted, 1.0, 0.0).astype(jnp.bfloat16)
        side_ref[:, number * rows : (number + 1) * rows] = jnp.dot(
            pick, weights[:, rows:], preferred_element_type=jnp.float32
        ).astype(jnp.bfloat16)

    for copy in writes:
        copy.wait()


def add_slot(east, west, field_ref, here, shift, margin):
    cols = field_ref.shape[1]
    last = pltpu.roll(field_ref[:, cols - LANES :], (shift + margin) % LANES, 1)
    leading = field_ref[:, :LANES]
    if shift:
        leading = pltpu.roll(leading, shift, 1)
    return jnp.where(here, last, east), jnp.where(here, leading, west)


def store_sides(x_ref, y_ref, group, east, west, eastward):
    lanes = slice(group * LANES, (group + 1) * LANES)
    x_ref[:, lanes] = jnp.where(eastward, east, west).astype(jnp.bfloat16)
    y_ref[:, lanes] = jnp.where(eastward, west, east).astype(jnp.bfloat16)


def force_kernel(
    margin,
    early,
    side_ref,
    tile_x_ref,
    tile_y_ref,
    current_ref,
    fields_ref,
    lon_x_in,
    lon_y_in,
    force_ref,
    lon_x_ref,
    lon_y_ref,
    lat_x_ref,
    lat_y_ref,
):
    windows, _, rows, cols = current_ref.shape
    side_x = side_ref[:, :rows]
    side_y = side_ref[:, rows:]

    def dot(a, b):
        return jnp.dot(a, b, preferred_element_type=jnp.float32)

    for w in range(windows):
        b = fields_ref[STATE + 2 * w + 1]
        for k in range(2):
            current = dot(side_x, tile_x_ref[w, k]) + dot(side_y, tile_y_ref[w, k])
            force_ref[2 * w + k] = b * (current_ref[w, k] + current)

    per = LANES // margin
    count = early + force_ref.shape[0]
    slot_of_lane = lax.broadcasted_iota(jnp.int32, (rows, LANES), 1) // margin
    eastward = even("lon")
    for group in range(lon_x_ref.shape[1] // LANES):
        lanes = slice(group * LANES, (group + 1) * LANES)
        x = lon_x_in[:, lanes].astype(jnp.float32)
        y = lon_y_in[:, lanes].astype(jnp.float32)
        east, west = jnp.where(eastward, x, y), jnp.where(eastward, y, x)
        for field in range(max(early, group * per), min(count, (group + 1) * per)):
            slot = field - group * per
            east, west = add_slot(
                east, west, force_ref.at[field - early], slot_of_lane == slot, slot * margin, margin
            )
        store_sides(lon_x_ref, lon_y_ref, group, east, west, eastward)

    depths = field_depths(margin, windows)
    groups = message_groups(range(early, count), depths)
    northward = even("lat")

    def value_of(field, at):
        return force_ref[field - early, at, :]

    for ref, north in ((lat_x_ref, northward), (lat_y_ref, jnp.logical_not(northward))):
        pack_rows(ref, 0, groups, depths, value_of, north, rows)


def corner_kernel(
    margin, rows, lat_x_in, lat_y_in, lon_x_ref, lon_y_ref, early_x_ref, early_y_ref, lat_x_ref, lat_y_ref
):
    for old_ref, ref, north in (
        (lat_x_in, lat_x_ref, even("lat")),
        (lat_y_in, lat_y_ref, jnp.logical_not(even("lat"))),
    ):
        row, cols = old_ref.shape
        ref[:row] = old_ref[...]
        start = pl.multiple_of(jnp.where(north, rows - margin, 0), GROUP)
        for lon_ref in (lon_x_ref, lon_y_ref):
            packed = lon_ref.shape[1]
            ref[row : row + margin, :packed] = lon_ref[pl.ds(start, margin), :]
            if packed < cols:
                ref[row : row + margin, packed:] = jnp.zeros((margin, cols - packed), ref.dtype)
            row += margin


def place(refs, early, field, tile, row, value):
    velocity, stress, strength, keep, push, force = refs
    at = pl.ds(row, value.shape[0])
    if field < 2:
        velocity[0, field, tile, at, :] = value
    elif field < STATE:
        stress[0, field - 2, tile, at, :] = value
    elif field >= early:
        window, kind = divmod(field - early, 2)
        force[window, kind, tile, at, :] = value
    else:
        window, kind = divmod(field - STATE, 2)
        if kind == 0:
            strength[window, tile, at, :] = value
        else:
            push[window, tile, at, :] = value * 0.25
            keep[window, tile, at, :] = jnp.where(value > 0.0, 1.0 - value, 0.0)


def place_sides(refs, early, count, margin, x, y, row):
    last = refs[0].shape[2] - 1
    per = LANES // margin
    wide = lax.broadcasted_iota(jnp.int32, (x.shape[0], LANES), 1)
    from_x_is_east = even("lon")
    for group in range(x.shape[1] // LANES):
        lanes = slice(group * LANES, (group + 1) * LANES)
        x_now, y_now = x[:, lanes], y[:, lanes]
        east = jnp.where(from_x_is_east, x_now, y_now)
        west = jnp.where(from_x_is_east, y_now, x_now)
        for slot in range(min(per, count - group * per)):
            shift = slot * margin
            back = (LANES - margin - shift) % LANES
            e = pltpu.roll(east, LANES - shift, 1) if shift else east
            w = pltpu.roll(west, back, 1) if back else west
            value = jnp.where(wide < margin, e, jnp.where(wide >= LANES - margin, w, 0.0))
            place(refs, early, group * per + slot, last, row, value)


def across(values):
    tiles = len(values)
    lane = lax.broadcasted_iota(jnp.int32, values[0].shape, 1)
    ahead = [pltpu.roll(x, LANES - 1, 1) for x in values]
    behind = [pltpu.roll(x, 1, 1) for x in values]
    return [
        jnp.where(lane == LANES - 1, ahead[(j + 1) % tiles], ahead[j])
        - jnp.where(lane == 0, behind[j - 1], behind[j])
        for j in range(tiles)
    ]


def stress_rows(refs, step, window, row):
    velocity, stress, strength, _, _, _ = refs
    every = range(velocity.shape[2])
    at, north, south = pl.ds(row, 8), pl.ds(row + 1, 8), pl.ds(row - 1, 8)
    u_x = across([velocity[step, 0, j, at, :] for j in every])
    v_x = across([velocity[step, 1, j, at, :] for j in every])
    for j in every:
        u_y = velocity[step, 0, j, north, :] - velocity[step, 0, j, south, :]
        v_y = velocity[step, 1, j, north, :] - velocity[step, 1, j, south, :]
        shear = u_y + v_x[j]
        spread = u_x[j] + v_y
        tension = u_x[j] - v_y
        tension4 = tension * 0.25
        shear4 = shear * 0.25
        squares = spread * spread + tension * tension4 + (shear * shear4 + 1.0)
        k = strength[window, j, at, :]
        kr = k * lax.rsqrt(squares)
        old = [stress[step, i, j, at, :] * (2.0 / 3.0) for i in range(3)]
        stress[step + 1, 0, j, at, :] = old[0] + (kr * (spread + tension4) - k)
        stress[step + 1, 1, j, at, :] = old[1] + (kr * (spread - tension4) - k)
        stress[step + 1, 2, j, at, :] = old[2] + kr * shear4


def velocity_rows(refs, step, window, row):
    velocity, stress, _, keep, push, force = refs
    every = range(velocity.shape[2])
    at, north, south = pl.ds(row, 8), pl.ds(row + 1, 8), pl.ds(row - 1, 8)
    now = step + 1
    p_x = across([stress[now, 0, j, at, :] for j in every])
    t_x = across([stress[now, 2, j, at, :] for j in every])
    for j in every:
        q_y = stress[now, 1, j, north, :] - stress[now, 1, j, south, :]
        t_y = stress[now, 2, j, north, :] - stress[now, 2, j, south, :]
        a = keep[window, j, at, :]
        b = push[window, j, at, :]
        velocity[now, 0, j, at, :] = (
            a * velocity[step, 0, j, at, :] + b * (p_x[j] + t_y) + force[window, 0, j, at, :]
        )
        velocity[now, 1, j, at, :] = (
            a * velocity[step, 1, j, at, :] + b * (t_x[j] + q_y) + force[window, 1, j, at, :]
        )


def write_rows(refs, out_hbm, stage, sem, margin, begin, height):
    velocity, stress = refs[:2]
    steps = velocity.shape[0] - 1
    for tile in range(stage.shape[2] // LANES):
        lanes = slice(tile * LANES, (tile + 1) * LANES)
        for row in range(0, height, 8):
            to = slice(row, row + 8)
            at = slice(margin + begin + row, margin + begin + row + 8)
            p, q, t = (stress[steps, i, tile, at, :] for i in range(3))
            stage[0, to, lanes] = velocity[steps, 0, tile, at, :]
            stage[1, to, lanes] = velocity[steps, 1, tile, at, :]
            stage[2, to, lanes] = (p + q) * 0.5
            stage[3, to, lanes] = (p - q) * 0.5
            stage[4, to, lanes] = t * 0.5
    copies = [
        pltpu.make_async_copy(
            stage.at[first : first + hbm.shape[0]], hbm.at[:, pl.ds(begin, height)], sem.at[i]
        )
        for i, (first, hbm) in enumerate(zip((0, 2), out_hbm))
    ]
    for copy in copies:
        copy.start()
    return copies


def place_rows(refs, early, fields, margin, rows, lat_count, x_ref, y_ref):
    depths = field_depths(margin, refs[2].shape[0])
    me = lax.axis_index("lat")
    sides = []
    for ref, north in ((x_ref, even("lat")), (y_ref, jnp.logical_not(even("lat")))):
        exists = jnp.where(north, me < lat_count - 1, me > 0)

        def read(at, ref=ref, exists=exists):
            return jnp.where(exists, ref[at].astype(jnp.float32), 0.0)

        row = 0
        for group in message_groups(fields, depths):
            height = sum(depths[f] for f in group)
            value = read(slice(row, row + height))
            begin = 0
            for field in group:
                depth = depths[field]
                to = pl.multiple_of(jnp.where(north, margin + rows, margin - depth), 8)
                for tile in range(refs[0].shape[2] - 1):
                    lanes = slice(tile * LANES, (tile + 1) * LANES)
                    place(refs, early, field, tile, to, value[begin : begin + depth, lanes])
                begin += depth
            row += height
        sides.append((north, read, row))
    return sides


def interior_kernel(
    margin, lat_count, fields_ref, force_ref, lon_x_ref, lon_y_ref, early_x_ref, early_y_ref, *refs
):
    early, rows, cols = fields_ref.shape
    count = early + force_ref.shape[0]
    windows = refs[2].shape[0]
    for field in range(count):
        for tile in range(cols // LANES):
            lanes = slice(tile * LANES, (tile + 1) * LANES)
            own = fields_ref[field, :, lanes] if field < early else force_ref[field - early, :, lanes]
            place(refs, early, field, tile, margin, own)
    lon_x, lon_y = lon_x_ref[...].astype(jnp.float32), lon_y_ref[...].astype(jnp.float32)
    place_sides(refs, early, count, margin, lon_x, lon_y, margin)
    place_rows(refs, early, range(early), margin, rows, lat_count, early_x_ref, early_y_ref)
    for window in range(windows):
        lost = 2 * SUB * window
        row_list = range(margin + lost, margin + rows - lost, 8)

        def subcycle(number, carry):
            step = window * SUB + number
            for row in row_list:
                stress_rows(refs, step, window, row)
            for row in row_list:
                velocity_rows(refs, step, window, row)
            return carry

        lax.fori_loop(0, SUB, subcycle, 0)


def rim_kernel(margin, early, count, lat_count, *args):
    lat_x_ref, lat_y_ref = args[:2]
    refs = args[2:8]
    out_hbm = args[8:10]
    stages, sems = args[16:19], args[19]
    windows = refs[2].shape[0]
    _, rows, cols = out_hbm[0].shape
    inner = rows - 2 * margin
    copies = write_rows(refs, out_hbm, stages[2], sems.at[2], margin, margin, inner)
    bottom = margin + rows
    packed = -(-count // (LANES // margin)) * LANES
    late = range(early, count)
    for north, read, row in place_rows(
        refs, early, late, margin, rows, lat_count, lat_x_ref, lat_y_ref
    ):
        to = pl.multiple_of(jnp.where(north, bottom, 0), 8)
        east, west = (read(slice(at, at + margin))[:, :packed] for at in (row, row + margin))
        place_sides(refs, early, count, margin, east, west, to)

    for step in range(SUB * windows):
        window = step // SUB
        done = 2 * step + 1
        for half, rows_now in ((0, stress_rows), (1, velocity_rows)):
            for first in range(0, margin, 8):
                rows_now(refs, step, window, done + half + first)
                rows_now(refs, step, window, bottom - done - half + first)

    for number, begin in enumerate((0, rows - margin)):
        copies += write_rows(
            refs, out_hbm, stages[number], sems.at[number], margin, begin, margin
        )
    for copy in copies:
        copy.wait()


def params():
    return pltpu.CompilerParams(vmem_limit_bytes=VMEM_LIMIT)


def lon_swaps(first):
    n = lax.axis_size("lon")
    if n % 2:
        raise ValueError("odd ring")
    pairs = [(i, (i + 1) % n) for i in range(first, n, 2)]
    return pairs + [(j, i) for i, j in pairs]


def lat_swaps(first):
    m, n = lax.axis_size("lat"), lax.axis_size("lon")
    partner = {}
    for i in range(m):
        north = i + 1 if (i - first) % 2 == 0 else i - 1
        for k in range(n):
            to = (north, k) if 0 <= north < m else (i, k ^ 1)
            partner[k * m + i] = to[1] * m + to[0]
    return list(partner.items())


def lon_exchange(x, y):
    return lax.ppermute(x, "lon", lon_swaps(0)), lax.ppermute(y, "lon", lon_swaps(1))


def lat_exchange(x, y):
    axes = ("lon", "lat")
    return lax.ppermute(x, axes, lat_swaps(0)), lax.ppermute(y, axes, lat_swaps(1))


def shape(dims, dtype=jnp.float32):
    return jax.ShapeDtypeStruct(dims, dtype)


def local(
    velocity,
    stress,
    thickness,
    concentration,
    land_mask,
    covered,
    ocean_current,
    wind_stress,
    regrid_weights,
    tile_offset,
):
    _, rows, cols = velocity.shape
    windows = wind_stress.shape[0]
    margin = 2 * SUB * windows
    early = STATE + 2 * windows
    count = early + 2 * windows
    tiles = cols // LANES + 1
    packed = -(-count // (LANES // margin)) * LANES
    depths = field_depths(margin, windows)
    early_rows = sum(depths[:early])
    late_rows = sum(depths[early:])
    bf16 = jnp.bfloat16

    tile_x, tile_y = lat_exchange(ocean_current, ocean_current)

    whole = pl.BlockSpec(memory_space=pltpu.VMEM)
    anywhere = pl.BlockSpec(memory_space=pl.ANY)
    chunks = rows // GROUP
    thick_out, fields, current, side, lon_x, lon_y, lat_x, lat_y = pl.pallas_call(
        functools.partial(local_kernel, margin),
        out_shape=(
            shape(thickness.shape),
            shape((early, rows, cols)),
            shape(wind_stress.shape),
            shape((rows, 2 * rows), bf16),
            shape((rows, packed), bf16),
            shape((rows, packed), bf16),
            shape((early_rows, cols), bf16),
            shape((early_rows, cols), bf16),
        ),
        in_specs=[anywhere] * 10,
        out_specs=(anywhere,) + (whole,) * 7,
        scratch_shapes=[
            pltpu.SMEM(covered.shape, jnp.int32),
            pltpu.VMEM((1, rows), jnp.int32),
            pltpu.VMEM(regrid_weights.shape, bf16),
            pltpu.VMEM(thickness.shape, jnp.float32),
            pltpu.VMEM(thickness.shape, jnp.float32),
            pltpu.VMEM(land_mask.shape, jnp.int32),
            pltpu.VMEM(velocity.shape, jnp.float32),
            pltpu.VMEM(stress.shape, jnp.float32),
            pltpu.VMEM(ocean_current.shape, bf16),
            pltpu.VMEM(wind_stress.shape, bf16),
            pltpu.SemaphoreType.DMA((8,)),
            pltpu.SemaphoreType.DMA((chunks,)),
            pltpu.SemaphoreType.DMA((chunks,)),
            pltpu.SemaphoreType.DMA((chunks,)),
        ],
        compiler_params=params(),
        cost_estimate=pl.CostEstimate(
            flops=100 * thickness.size, bytes_accessed=12 * thickness.size, transcendentals=0
        ),
        name="local",
    )(
        *(
            pltpu.with_memory_space_constraint(x, pltpu.HBM)
            for x in (
                covered,
                tile_offset.reshape(1, rows),
                regrid_weights,
                thickness,
                concentration,
                land_mask,
                velocity,
                stress,
                ocean_current,
                wind_stress,
            )
        )
    )

    early_x, early_y = lat_exchange(lat_x, lat_y)
    force, lon_x, lon_y, lat_x, lat_y = pl.pallas_call(
        functools.partial(force_kernel, margin, early),
        out_shape=(
            shape((2 * windows, rows, cols)),
            shape((rows, packed), bf16),
            shape((rows, packed), bf16),
            shape((late_rows, cols), bf16),
            shape((late_rows, cols), bf16),
        ),
        in_specs=[whole] * 7,
        out_specs=(whole,) * 5,
        compiler_params=params(),
        cost_estimate=pl.CostEstimate(flops=1, bytes_accessed=1, transcendentals=0),
        name="force",
    )(side, tile_x, tile_y, current, fields, lon_x, lon_y)

    lon_x, lon_y = lon_exchange(lon_x, lon_y)
    message = shape((late_rows + 2 * margin, cols), bf16)
    lat_x, lat_y = pl.pallas_call(
        functools.partial(corner_kernel, margin, rows),
        out_shape=(message, message),
        in_specs=[whole] * 6,
        out_specs=(whole,) * 2,
        compiler_params=params(),
        cost_estimate=pl.CostEstimate(flops=1, bytes_accessed=1, transcendentals=0),
        name="corner",
    )(lat_x, lat_y, lon_x, lon_y, early_x, early_y)
    lat_x, lat_y = lat_exchange(lat_x, lat_y)

    steps = SUB * windows

    def widened(*lead):
        return shape((*lead, tiles, rows + 2 * margin, LANES))

    domain = (
        widened(steps + 1, 2),
        widened(steps + 1, 3),
        widened(windows),
        widened(windows),
        widened(windows),
        widened(windows, 2),
    )
    outs = (shape(velocity.shape), shape(stress.shape))
    refs = pl.pallas_call(
        functools.partial(interior_kernel, margin, lax.axis_size("lat")),
        out_shape=domain,
        in_specs=[whole] * 6,
        out_specs=(whole,) * 6,
        compiler_params=params(),
        cost_estimate=pl.CostEstimate(
            flops=60 * steps * rows * cols, bytes_accessed=2**22, transcendentals=0
        ),
        name="interior",
    )(fields, force, lon_x, lon_y, early_x, early_y)

    velocity_out, stress_out = pl.pallas_call(
        functools.partial(rim_kernel, margin, early, count, lax.axis_size("lat")),
        out_shape=(shape(velocity.shape), shape(stress.shape)) + domain,
        in_specs=[whole] * 8,
        out_specs=(anywhere,) * 2 + (whole,) * 6,
        input_output_aliases={2 + i: 2 + i for i in range(6)},
        scratch_shapes=[
            pltpu.VMEM((STATE, margin, cols), jnp.float32),
            pltpu.VMEM((STATE, margin, cols), jnp.float32),
            pltpu.VMEM((STATE, rows - 2 * margin, cols), jnp.float32),
            pltpu.SemaphoreType.DMA((3, 2)),
        ],
        compiler_params=params(),
        name="rim",
    )(lat_x, lat_y, *refs)[:2]
    return (velocity_out, stress_out, thick_out)


def solution(mesh):
    return jax.shard_map(
        local,
        mesh=mesh,
        in_specs=(
            P(None, "lat", "lon"),
            P(None, "lat", "lon"),
            P(None, "lat", "lon"),
            P(None, "lat", "lon"),
            P("lat", "lon"),
            P("lat", None),
            P(None, None, "lat", "lon"),
            P(None, None, "lat", "lon"),
            P("lat", None),
            P("lat"),
        ),
        out_specs=(P(None, "lat", "lon"), P(None, "lat", "lon"), P(None, "lat", "lon")),
        check_vma=False,
    )
```

```python
import functools

import jax
import jax.numpy as jnp
from jax import lax
from jax.experimental import pallas as pl
from jax.experimental.pallas import tpu as pltpu
from jax.sharding import PartitionSpec as P

BLK = 128
SUB = 4
LANES = 128
GROUP = 16
STATE = 5
VMEM_LIMIT = 16 * 1024 * 1024

growth_rate = 0.3
mixing_rate = 0.3


def total(terms):
    result = terms[0]
    for term in terms[1:]:
        result = result + term
    return result


def field_depths(margin, windows):
    depths = [margin] * STATE
    for copies in (2, 2):
        for window in range(windows):
            depths += [margin - 2 * SUB * window] * copies
    return depths


def message_groups(fields, depths):
    groups, held = [], []
    for field in fields:
        held.append(field)
        if sum(depths[f] for f in held) % GROUP == 0:
            groups.append(held)
            held = []
    return groups + ([held] if held else [])


def even(axis):
    return lax.axis_index(axis) % 2 == 0


def pack_rows(message_ref, row, groups, depths, value_of, northward, rows):
    for group in groups:
        parts = []
        for field in group:
            start = jnp.where(northward, rows - depths[field], 0)
            parts.append(value_of(field, pl.ds(pl.multiple_of(start, 8), depths[field])))
        value = parts[0] if len(parts) == 1 else jnp.concatenate(parts, axis=0)
        message_ref[row : row + value.shape[0]] = value.astype(jnp.bfloat16)
        row += value.shape[0]
    return row


def local_kernel(
    margin,
    covered_hbm,
    offset_hbm,
    weights_hbm,
    thick_hbm,
    conc_hbm,
    mask_hbm,
    velocity_hbm,
    stress_hbm,
    ocean_hbm,
    wind_hbm,
    thick_out_hbm,
    fields_ref,
    current_ref,
    side_ref,
    lon_x_ref,
    lon_y_ref,
    lat_x_ref,
    lat_y_ref,
    covered,
    offset,
    weights,
    thick,
    conc,
    mask_in,
    velocity,
    stress,
    ocean,
    wind,
    in_sems,
    thick_sems,
    conc_sems,
    out_sems,
):
    cats, rows, cols = thick.shape
    windows = wind.shape[0]
    step = GROUP
    chunks = rows // step

    def rows_of(chunk):
        return pl.ds(chunk * step, step)

    small = [
        pltpu.make_async_copy(source, target, in_sems.at[i])
        for i, (source, target) in enumerate(
            (
                (covered_hbm, covered),
                (mask_hbm, mask_in),
                (velocity_hbm, velocity),
                (stress_hbm, stress),
                (ocean_hbm, ocean),
                (wind_hbm, wind),
                (weights_hbm, weights),
                (offset_hbm, offset),
            )
        )
    ]
    pairs = [
        [
            pltpu.make_async_copy(hbm.at[:, rows_of(c)], vmem.at[:, rows_of(c)], sems.at[c])
            for hbm, vmem, sems in ((thick_hbm, thick, thick_sems), (conc_hbm, conc, conc_sems))
        ]
        for c in range(chunks)
    ]
    writes = [
        pltpu.make_async_copy(thick.at[:, rows_of(c)], thick_out_hbm.at[:, rows_of(c)], out_sems.at[c])
        for c in range(chunks)
    ]
    for copy in small[:2] + [copy for pair in pairs for copy in pair] + small[2:]:
        copy.start()

    blocks = cols // BLK
    first = lax.axis_index("lon") * blocks
    small[0].wait()
    live = [covered[0, first + block] > 0 for block in range(blocks)]
    small[1].wait()
    for c in range(chunks):
        at = slice(c * step, (c + 1) * step)
        for copy in pairs[c]:
            copy.wait()
        for block in range(blocks):
            lanes = slice(block * BLK, (block + 1) * BLK)
            part = [conc[k, at, lanes] for k in range(cats)]
            height = [thick[k, at, lanes] for k in range(cats)]
            mask = mask_in[at, lanes].astype(jnp.float32)
            area = total(part)
            inverse = 1.0 / area
            factor = jnp.exp(-2.0 * (1.0 - area)) * (mask * (1.0 / 3.0))
            half = 0.5 * mask
            volume = total([a * h for a, h in zip(part, height)])
            for window in range(windows):
                mean = volume * inverse
                grown = [h + growth_rate / (0.5 + h) + mixing_rate * (mean - h) for h in height]
                height = [jnp.where(live[block], g, h) for g, h in zip(grown, height)]
                volume = total([a * h for a, h in zip(part, height)])
                fields_ref[STATE + 2 * window, at, lanes] = volume * factor
                fields_ref[STATE + 2 * window + 1, at, lanes] = half / (volume + 1.0)
            for k in range(cats):
                thick[k, at, lanes] = height[k]
        writes[c].start()

    small[2].wait()
    small[3].wait()
    for row in range(0, rows, step):
        at = slice(row, row + step)
        mask = mask_in[at].astype(jnp.float32)
        fields_ref[0, at] = velocity[0, at]
        fields_ref[1, at] = velocity[1, at]
        fields_ref[2, at] = (stress[0, at] + stress[1, at]) * mask
        fields_ref[3, at] = (stress[0, at] - stress[1, at]) * mask
        fields_ref[4, at] = (stress[2, at] + stress[2, at]) * mask

    count = fields_ref.shape[0]
    per = LANES // margin
    slot_of_lane = lax.broadcasted_iota(jnp.int32, (rows, LANES), 1) // margin
    eastward = even("lon")
    for group in range(lon_x_ref.shape[1] // LANES):
        east = jnp.zeros((rows, LANES), jnp.float32)
        west = jnp.zeros((rows, LANES), jnp.float32)
        for slot in range(min(per, count - group * per)):
            field = group * per + slot
            east, west = add_slot(
                east, west, fields_ref.at[field], slot_of_lane == slot, slot * margin, margin
            )
        store_sides(lon_x_ref, lon_y_ref, group, east, west, eastward)
    depths = field_depths(margin, windows)
    groups = message_groups(range(count), depths)
    northward = even("lat")

    def value_of(field, at):
        return fields_ref[field, at, :]

    pack_rows(lat_x_ref, 0, groups, depths, value_of, northward, rows)
    pack_rows(lat_y_ref, 0, groups, depths, value_of, jnp.logical_not(northward), rows)

    for copy in small[4:]:
        copy.wait()
    own_weights = weights[:, :rows]
    for w in range(windows):
        for k in range(2):
            current_ref[w, k] = wind[w, k].astype(jnp.float32) + jnp.dot(
                own_weights, ocean[w, k], preferred_element_type=jnp.float32
            )
    square = (rows, rows)
    diagonal = lax.broadcasted_iota(jnp.int32, square, 0) == lax.broadcasted_iota(
        jnp.int32, square, 1
    )
    up = offset[...] > 0
    for number, north in enumerate((northward, jnp.logical_not(northward))):
        wanted = jnp.where(north, up.astype(jnp.int32), 1 - up.astype(jnp.int32)) > 0
        pick = jnp.where(diagonal & wanted, 1.0, 0.0).astype(jnp.bfloat16)
        side_ref[:, number * rows : (number + 1) * rows] = jnp.dot(
            pick, weights[:, rows:], preferred_element_type=jnp.float32
        ).astype(jnp.bfloat16)

    for copy in writes:
        copy.wait()


def add_slot(east, west, field_ref, here, shift, margin):
    cols = field_ref.shape[1]
    last = pltpu.roll(field_ref[:, cols - LANES :], (shift + margin) % LANES, 1)
    leading = field_ref[:, :LANES]
    if shift:
        leading = pltpu.roll(leading, shift, 1)
    return jnp.where(here, last, east), jnp.where(here, leading, west)


def store_sides(x_ref, y_ref, group, east, west, eastward):
    lanes = slice(group * LANES, (group + 1) * LANES)
    x_ref[:, lanes] = jnp.where(eastward, east, west).astype(jnp.bfloat16)
    y_ref[:, lanes] = jnp.where(eastward, west, east).astype(jnp.bfloat16)


def force_kernel(
    margin,
    early,
    side_ref,
    tile_x_ref,
    tile_y_ref,
    current_ref,
    fields_ref,
    lon_x_in,
    lon_y_in,
    force_ref,
    lon_x_ref,
    lon_y_ref,
    lat_x_ref,
    lat_y_ref,
):
    windows, _, rows, cols = current_ref.shape
    side_x = side_ref[:, :rows]
    side_y = side_ref[:, rows:]

    def dot(a, b):
        return jnp.dot(a, b, preferred_element_type=jnp.float32)

    for w in range(windows):
        b = fields_ref[STATE + 2 * w + 1]
        for k in range(2):
            current = dot(side_x, tile_x_ref[w, k]) + dot(side_y, tile_y_ref[w, k])
            force_ref[2 * w + k] = b * (current_ref[w, k] + current)

    per = LANES // margin
    count = early + force_ref.shape[0]
    slot_of_lane = lax.broadcasted_iota(jnp.int32, (rows, LANES), 1) // margin
    eastward = even("lon")
    for group in range(lon_x_ref.shape[1] // LANES):
        lanes = slice(group * LANES, (group + 1) * LANES)
        x = lon_x_in[:, lanes].astype(jnp.float32)
        y = lon_y_in[:, lanes].astype(jnp.float32)
        east, west = jnp.where(eastward, x, y), jnp.where(eastward, y, x)
        for field in range(max(early, group * per), min(count, (group + 1) * per)):
            slot = field - group * per
            east, west = add_slot(
                east, west, force_ref.at[field - early], slot_of_lane == slot, slot * margin, margin
            )
        store_sides(lon_x_ref, lon_y_ref, group, east, west, eastward)

    depths = field_depths(margin, windows)
    groups = message_groups(range(early, count), depths)
    northward = even("lat")

    def value_of(field, at):
        return force_ref[field - early, at, :]

    for ref, north in ((lat_x_ref, northward), (lat_y_ref, jnp.logical_not(northward))):
        pack_rows(ref, 0, groups, depths, value_of, north, rows)


def corner_kernel(
    margin, rows, lat_x_in, lat_y_in, lon_x_ref, lon_y_ref, early_x_ref, early_y_ref, lat_x_ref, lat_y_ref
):
    for old_ref, ref, north in (
        (lat_x_in, lat_x_ref, even("lat")),
        (lat_y_in, lat_y_ref, jnp.logical_not(even("lat"))),
    ):
        row, cols = old_ref.shape
        ref[:row] = old_ref[...]
        start = pl.multiple_of(jnp.where(north, rows - margin, 0), GROUP)
        for lon_ref in (lon_x_ref, lon_y_ref):
            packed = lon_ref.shape[1]
            ref[row : row + margin, :packed] = lon_ref[pl.ds(start, margin), :]
            if packed < cols:
                ref[row : row + margin, packed:] = jnp.zeros((margin, cols - packed), ref.dtype)
            row += margin


def place(refs, early, field, tile, row, value):
    velocity, stress, strength, keep, push, force = refs
    at = pl.ds(row, value.shape[0])
    if field < 2:
        velocity[0, field, tile, at, :] = value
    elif field < STATE:
        stress[0, field - 2, tile, at, :] = value
    elif field >= early:
        window, kind = divmod(field - early, 2)
        force[window, kind, tile, at, :] = value
    else:
        window, kind = divmod(field - STATE, 2)
        if kind == 0:
            strength[window, tile, at, :] = value
        else:
            push[window, tile, at, :] = value * 0.25
            keep[window, tile, at, :] = jnp.where(value > 0.0, 1.0 - value, 0.0)


def place_sides(refs, early, count, margin, x, y, row):
    last = refs[0].shape[2] - 1
    per = LANES // margin
    wide = lax.broadcasted_iota(jnp.int32, (x.shape[0], LANES), 1)
    from_x_is_east = even("lon")
    for group in range(x.shape[1] // LANES):
        lanes = slice(group * LANES, (group + 1) * LANES)
        x_now, y_now = x[:, lanes], y[:, lanes]
        east = jnp.where(from_x_is_east, x_now, y_now)
        west = jnp.where(from_x_is_east, y_now, x_now)
        for slot in range(min(per, count - group * per)):
            shift = slot * margin
            back = (LANES - margin - shift) % LANES
            e = pltpu.roll(east, LANES - shift, 1) if shift else east
            w = pltpu.roll(west, back, 1) if back else west
            value = jnp.where(wide < margin, e, jnp.where(wide >= LANES - margin, w, 0.0))
            place(refs, early, group * per + slot, last, row, value)


def across(values):
    tiles = len(values)
    lane = lax.broadcasted_iota(jnp.int32, values[0].shape, 1)
    ahead = [pltpu.roll(x, LANES - 1, 1) for x in values]
    behind = [pltpu.roll(x, 1, 1) for x in values]
    return [
        jnp.where(lane == LANES - 1, ahead[(j + 1) % tiles], ahead[j])
        - jnp.where(lane == 0, behind[j - 1], behind[j])
        for j in range(tiles)
    ]


def stress_rows(refs, step, window, row):
    velocity, stress, strength, _, _, _ = refs
    every = range(velocity.shape[2])
    at, north, south = pl.ds(row, 8), pl.ds(row + 1, 8), pl.ds(row - 1, 8)
    u_x = across([velocity[step, 0, j, at, :] for j in every])
    v_x = across([velocity[step, 1, j, at, :] for j in every])
    for j in every:
        u_y = velocity[step, 0, j, north, :] - velocity[step, 0, j, south, :]
        v_y = velocity[step, 1, j, north, :] - velocity[step, 1, j, south, :]
        shear = u_y + v_x[j]
        spread = u_x[j] + v_y
        tension = u_x[j] - v_y
        tension4 = tension * 0.25
        shear4 = shear * 0.25
        squares = spread * spread + tension * tension4 + (shear * shear4 + 1.0)
        k = strength[window, j, at, :]
        kr = k * lax.rsqrt(squares)
        old = [stress[step, i, j, at, :] * (2.0 / 3.0) for i in range(3)]
        stress[step + 1, 0, j, at, :] = old[0] + (kr * (spread + tension4) - k)
        stress[step + 1, 1, j, at, :] = old[1] + (kr * (spread - tension4) - k)
        stress[step + 1, 2, j, at, :] = old[2] + kr * shear4


def velocity_rows(refs, step, window, row):
    velocity, stress, _, keep, push, force = refs
    every = range(velocity.shape[2])
    at, north, south = pl.ds(row, 8), pl.ds(row + 1, 8), pl.ds(row - 1, 8)
    now = step + 1
    p_x = across([stress[now, 0, j, at, :] for j in every])
    t_x = across([stress[now, 2, j, at, :] for j in every])
    for j in every:
        q_y = stress[now, 1, j, north, :] - stress[now, 1, j, south, :]
        t_y = stress[now, 2, j, north, :] - stress[now, 2, j, south, :]
        a = keep[window, j, at, :]
        b = push[window, j, at, :]
        velocity[now, 0, j, at, :] = (
            a * velocity[step, 0, j, at, :] + b * (p_x[j] + t_y) + force[window, 0, j, at, :]
        )
        velocity[now, 1, j, at, :] = (
            a * velocity[step, 1, j, at, :] + b * (t_x[j] + q_y) + force[window, 1, j, at, :]
        )


def write_rows(refs, out_hbm, stage, sem, margin, begin, height, which):
    values = refs[which]
    last = values.shape[0] - 1
    first = 2 * which
    for tile in range(stage.shape[2] // LANES):
        lanes = slice(tile * LANES, (tile + 1) * LANES)
        for row in range(0, height, 8):
            to = slice(row, row + 8)
            at = slice(margin + begin + row, margin + begin + row + 8)
            now = [values[last, i, tile, at, :] for i in range(values.shape[1])]
            if which:
                now = [(now[0] + now[1]) * 0.5, (now[0] - now[1]) * 0.5, now[2] * 0.5]
            for i, value in enumerate(now):
                stage[first + i, to, lanes] = value
    copy = pltpu.make_async_copy(
        stage.at[first : first + values.shape[1]],
        out_hbm[which].at[:, pl.ds(begin, height)],
        sem.at[which],
    )
    copy.start()
    return [copy]


def place_rows(refs, early, fields, margin, rows, lat_count, x_ref, y_ref):
    depths = field_depths(margin, refs[2].shape[0])
    me = lax.axis_index("lat")
    sides = []
    for ref, north in ((x_ref, even("lat")), (y_ref, jnp.logical_not(even("lat")))):
        exists = jnp.where(north, me < lat_count - 1, me > 0)

        def read(at, ref=ref, exists=exists):
            return jnp.where(exists, ref[at].astype(jnp.float32), 0.0)

        row = 0
        for group in message_groups(fields, depths):
            height = sum(depths[f] for f in group)
            value = read(slice(row, row + height))
            begin = 0
            for field in group:
                depth = depths[field]
                to = pl.multiple_of(jnp.where(north, margin + rows, margin - depth), 8)
                for tile in range(refs[0].shape[2] - 1):
                    lanes = slice(tile * LANES, (tile + 1) * LANES)
                    place(refs, early, field, tile, to, value[begin : begin + depth, lanes])
                begin += depth
            row += height
        sides.append((north, read, row))
    return sides


def interior_kernel(
    margin, lat_count, fields_ref, force_ref, lon_x_ref, lon_y_ref, early_x_ref, early_y_ref, *refs
):
    early, rows, cols = fields_ref.shape
    count = early + force_ref.shape[0]
    windows = refs[2].shape[0]
    for field in range(count):
        for tile in range(cols // LANES):
            lanes = slice(tile * LANES, (tile + 1) * LANES)
            own = fields_ref[field, :, lanes] if field < early else force_ref[field - early, :, lanes]
            place(refs, early, field, tile, margin, own)
    lon_x, lon_y = lon_x_ref[...].astype(jnp.float32), lon_y_ref[...].astype(jnp.float32)
    place_sides(refs, early, count, margin, lon_x, lon_y, margin)
    place_rows(refs, early, range(early), margin, rows, lat_count, early_x_ref, early_y_ref)
    for window in range(windows):
        lost = 2 * SUB * window

        def subcycle(number, carry):
            step = window * SUB + number
            base = step // (SUB * windows) * 8
            row_list = [
                pl.multiple_of(base + row, 8) for row in range(margin + lost, margin + rows - lost, 8)
            ]
            for row in row_list:
                stress_rows(refs, step, window, row)
            for row in row_list:
                velocity_rows(refs, step, window, row)
            return carry

        lax.fori_loop(0, SUB, subcycle, 0)


def rim_kernel(margin, early, count, lat_count, *args):
    lat_x_ref, lat_y_ref = args[:2]
    refs = args[2:8]
    out_hbm = args[8:10]
    stages, sems = args[16:19], args[19]
    windows = refs[2].shape[0]
    _, rows, cols = out_hbm[0].shape
    inner = rows - 2 * margin
    copies = []
    for which in range(2):
        copies += write_rows(refs, out_hbm, stages[2], sems.at[2], margin, margin, inner, which)
    bottom = margin + rows
    packed = -(-count // (LANES // margin)) * LANES
    late = range(early, count)
    for north, read, row in place_rows(
        refs, early, late, margin, rows, lat_count, lat_x_ref, lat_y_ref
    ):
        to = pl.multiple_of(jnp.where(north, bottom, 0), 8)
        east, west = (read(slice(at, at + margin))[:, :packed] for at in (row, row + margin))
        place_sides(refs, early, count, margin, east, west, to)

    def half_step(step, half):
        done = 2 * step + 1 + half
        rows_now = velocity_rows if half else stress_rows
        for first in range(0, margin, 8):
            rows_now(refs, step, step // SUB, done + first)
            rows_now(refs, step, step // SUB, bottom - done + first)

    def subcycles(number, carry):
        for step in (2 * number, 2 * number + 1):
            half_step(step, 0)
            half_step(step, 1)
        return carry

    last = SUB * windows - 1
    lax.fori_loop(0, last // 2, subcycles, 0)
    for step in range(last // 2 * 2, last):
        half_step(step, 0)
        half_step(step, 1)
    half_step(last, 0)
    ends = list(enumerate((0, rows - margin)))
    for number, begin in ends:
        copies += write_rows(refs, out_hbm, stages[number], sems.at[number], margin, begin, margin, 1)
    half_step(last, 1)
    for number, begin in ends:
        copies += write_rows(refs, out_hbm, stages[number], sems.at[number], margin, begin, margin, 0)
    for copy in copies:
        copy.wait()


def params():
    return pltpu.CompilerParams(vmem_limit_bytes=VMEM_LIMIT)


def lon_swaps(first):
    n = lax.axis_size("lon")
    if n % 2:
        raise ValueError("odd ring")
    pairs = [(i, (i + 1) % n) for i in range(first, n, 2)]
    return pairs + [(j, i) for i, j in pairs]


def lat_swaps(first):
    m, n = lax.axis_size("lat"), lax.axis_size("lon")
    partner = {}
    for i in range(m):
        north = i + 1 if (i - first) % 2 == 0 else i - 1
        for k in range(n):
            to = (north, k) if 0 <= north < m else (i, k ^ 1)
            partner[k * m + i] = to[1] * m + to[0]
    return list(partner.items())


def lon_exchange(x, y):
    return lax.ppermute(x, "lon", lon_swaps(0)), lax.ppermute(y, "lon", lon_swaps(1))


def lat_exchange(x, y):
    axes = ("lon", "lat")
    return lax.ppermute(x, axes, lat_swaps(0)), lax.ppermute(y, axes, lat_swaps(1))


def shape(dims, dtype=jnp.float32):
    return jax.ShapeDtypeStruct(dims, dtype)


def local(
    velocity,
    stress,
    thickness,
    concentration,
    land_mask,
    covered,
    ocean_current,
    wind_stress,
    regrid_weights,
    tile_offset,
):
    _, rows, cols = velocity.shape
    windows = wind_stress.shape[0]
    margin = 2 * SUB * windows
    early = STATE + 2 * windows
    count = early + 2 * windows
    tiles = cols // LANES + 1
    packed = -(-count // (LANES // margin)) * LANES
    depths = field_depths(margin, windows)
    early_rows = sum(depths[:early])
    late_rows = sum(depths[early:])
    bf16 = jnp.bfloat16

    tile_x, tile_y = lat_exchange(ocean_current, ocean_current)

    whole = pl.BlockSpec(memory_space=pltpu.VMEM)
    anywhere = pl.BlockSpec(memory_space=pl.ANY)
    chunks = rows // GROUP
    thick_out, fields, current, side, lon_x, lon_y, lat_x, lat_y = pl.pallas_call(
        functools.partial(local_kernel, margin),
        out_shape=(
            shape(thickness.shape),
            shape((early, rows, cols)),
            shape(wind_stress.shape),
            shape((rows, 2 * rows), bf16),
            shape((rows, packed), bf16),
            shape((rows, packed), bf16),
            shape((early_rows, cols), bf16),
            shape((early_rows, cols), bf16),
        ),
        in_specs=[anywhere] * 10,
        out_specs=(anywhere,) + (whole,) * 7,
        scratch_shapes=[
            pltpu.SMEM(covered.shape, jnp.int32),
            pltpu.VMEM((1, rows), jnp.int32),
            pltpu.VMEM(regrid_weights.shape, bf16),
            pltpu.VMEM(thickness.shape, jnp.float32),
            pltpu.VMEM(thickness.shape, jnp.float32),
            pltpu.VMEM(land_mask.shape, jnp.int32),
            pltpu.VMEM(velocity.shape, jnp.float32),
            pltpu.VMEM(stress.shape, jnp.float32),
            pltpu.VMEM(ocean_current.shape, bf16),
            pltpu.VMEM(wind_stress.shape, bf16),
            pltpu.SemaphoreType.DMA((8,)),
            pltpu.SemaphoreType.DMA((chunks,)),
            pltpu.SemaphoreType.DMA((chunks,)),
            pltpu.SemaphoreType.DMA((chunks,)),
        ],
        compiler_params=params(),
        cost_estimate=pl.CostEstimate(
            flops=100 * thickness.size, bytes_accessed=12 * thickness.size, transcendentals=0
        ),
        name="local",
    )(
        *(
            pltpu.with_memory_space_constraint(x, pltpu.HBM)
            for x in (
                covered,
                tile_offset.reshape(1, rows),
                regrid_weights,
                thickness,
                concentration,
                land_mask,
                velocity,
                stress,
                ocean_current,
                wind_stress,
            )
        )
    )

    early_x, early_y = lat_exchange(lat_x, lat_y)
    force, lon_x, lon_y, lat_x, lat_y = pl.pallas_call(
        functools.partial(force_kernel, margin, early),
        out_shape=(
            shape((2 * windows, rows, cols)),
            shape((rows, packed), bf16),
            shape((rows, packed), bf16),
            shape((late_rows, cols), bf16),
            shape((late_rows, cols), bf16),
        ),
        in_specs=[whole] * 7,
        out_specs=(whole,) * 5,
        compiler_params=params(),
        cost_estimate=pl.CostEstimate(flops=1, bytes_accessed=1, transcendentals=0),
        name="force",
    )(side, tile_x, tile_y, current, fields, lon_x, lon_y)

    lon_x, lon_y = lon_exchange(lon_x, lon_y)
    message = shape((late_rows + 2 * margin, cols), bf16)
    lat_x, lat_y = pl.pallas_call(
        functools.partial(corner_kernel, margin, rows),
        out_shape=(message, message),
        in_specs=[whole] * 6,
        out_specs=(whole,) * 2,
        compiler_params=params(),
        cost_estimate=pl.CostEstimate(flops=1, bytes_accessed=1, transcendentals=0),
        name="corner",
    )(lat_x, lat_y, lon_x, lon_y, early_x, early_y)
    lat_x, lat_y = lat_exchange(lat_x, lat_y)

    steps = SUB * windows

    def widened(*lead):
        return shape((*lead, tiles, rows + 2 * margin, LANES))

    domain = (
        widened(steps + 1, 2),
        widened(steps + 1, 3),
        widened(windows),
        widened(windows),
        widened(windows),
        widened(windows, 2),
    )
    outs = (shape(velocity.shape), shape(stress.shape))
    refs = pl.pallas_call(
        functools.partial(interior_kernel, margin, lax.axis_size("lat")),
        out_shape=domain,
        in_specs=[whole] * 6,
        out_specs=(whole,) * 6,
        compiler_params=params(),
        cost_estimate=pl.CostEstimate(
            flops=60 * steps * rows * cols, bytes_accessed=2**22, transcendentals=0
        ),
        name="interior",
    )(fields, force, lon_x, lon_y, early_x, early_y)

    velocity_out, stress_out = pl.pallas_call(
        functools.partial(rim_kernel, margin, early, count, lax.axis_size("lat")),
        out_shape=(shape(velocity.shape), shape(stress.shape)) + domain,
        in_specs=[whole] * 8,
        out_specs=(anywhere,) * 2 + (whole,) * 6,
        input_output_aliases={2 + i: 2 + i for i in range(6)},
        scratch_shapes=[
            pltpu.VMEM((STATE, margin, cols), jnp.float32),
            pltpu.VMEM((STATE, margin, cols), jnp.float32),
            pltpu.VMEM((STATE, rows - 2 * margin, cols), jnp.float32),
            pltpu.SemaphoreType.DMA((3, 2)),
        ],
        compiler_params=params(),
        name="rim",
    )(lat_x, lat_y, *refs)[:2]
    return (velocity_out, stress_out, thick_out)


def solution(mesh):
    return jax.shard_map(
        local,
        mesh=mesh,
        in_specs=(
            P(None, "lat", "lon"),
            P(None, "lat", "lon"),
            P(None, "lat", "lon"),
            P(None, "lat", "lon"),
            P("lat", "lon"),
            P("lat", None),
            P(None, None, "lat", "lon"),
            P(None, None, "lat", "lon"),
            P("lat", None),
            P("lat"),
        ),
        out_specs=(P(None, "lat", "lon"), P(None, "lat", "lon"), P(None, "lat", "lon")),
        check_vma=False,
    )
```

```python
import functools

import jax
import jax.numpy as jnp
from jax import lax
from jax.experimental import pallas as pl
from jax.experimental.pallas import tpu as pltpu
from jax.sharding import PartitionSpec as P

BLK = 128
SUB = 4
LANES = 128
GROUP = 16
STATE = 5
VMEM_LIMIT = 16 * 1024 * 1024

growth_rate = 0.3
mixing_rate = 0.3


def total(terms):
    result = terms[0]
    for term in terms[1:]:
        result = result + term
    return result


def field_depths(margin, windows):
    depths = [margin] * STATE
    for copies in (2, 2):
        for window in range(windows):
            depths += [margin - 2 * SUB * window] * copies
    return depths


def message_groups(fields, depths):
    groups, held = [], []
    for field in fields:
        held.append(field)
        if sum(depths[f] for f in held) % GROUP == 0:
            groups.append(held)
            held = []
    return groups + ([held] if held else [])


def even(axis):
    return lax.axis_index(axis) % 2 == 0


def pack_rows(message_ref, row, groups, depths, value_of, northward, rows):
    for group in groups:
        parts = []
        for field in group:
            start = jnp.where(northward, rows - depths[field], 0)
            parts.append(value_of(field, pl.ds(pl.multiple_of(start, 8), depths[field])))
        value = parts[0] if len(parts) == 1 else jnp.concatenate(parts, axis=0)
        message_ref[row : row + value.shape[0]] = value.astype(jnp.bfloat16)
        row += value.shape[0]
    return row


def local_kernel(
    margin,
    covered_hbm,
    offset_hbm,
    weights_hbm,
    thick_hbm,
    conc_hbm,
    mask_hbm,
    velocity_hbm,
    stress_hbm,
    ocean_hbm,
    wind_hbm,
    thick_out_hbm,
    fields_ref,
    current_ref,
    side_ref,
    lon_x_ref,
    lon_y_ref,
    lat_x_ref,
    lat_y_ref,
    covered,
    offset,
    weights,
    thick,
    conc,
    mask_in,
    velocity,
    stress,
    ocean,
    wind,
    in_sems,
    thick_sems,
    conc_sems,
    out_sems,
):
    cats, rows, cols = thick.shape
    windows = wind.shape[0]
    step = GROUP
    chunks = rows // step

    def rows_of(chunk):
        return pl.ds(chunk * step, step)

    small = [
        pltpu.make_async_copy(source, target, in_sems.at[i])
        for i, (source, target) in enumerate(
            (
                (covered_hbm, covered),
                (mask_hbm, mask_in),
                (velocity_hbm, velocity),
                (stress_hbm, stress),
                (ocean_hbm, ocean),
                (wind_hbm, wind),
                (weights_hbm, weights),
                (offset_hbm, offset),
            )
        )
    ]
    pairs = [
        [
            pltpu.make_async_copy(hbm.at[:, rows_of(c)], vmem.at[:, rows_of(c)], sems.at[c])
            for hbm, vmem, sems in ((thick_hbm, thick, thick_sems), (conc_hbm, conc, conc_sems))
        ]
        for c in range(chunks)
    ]
    writes = [
        pltpu.make_async_copy(thick.at[:, rows_of(c)], thick_out_hbm.at[:, rows_of(c)], out_sems.at[c])
        for c in range(chunks)
    ]
    for copy in small[:2] + [copy for pair in pairs for copy in pair] + small[2:]:
        copy.start()

    blocks = cols // BLK
    first = lax.axis_index("lon") * blocks
    small[0].wait()
    live = [covered[0, first + block] > 0 for block in range(blocks)]
    small[1].wait()
    for c in range(chunks):
        at = slice(c * step, (c + 1) * step)
        for copy in pairs[c]:
            copy.wait()
        for block in range(blocks):
            lanes = slice(block * BLK, (block + 1) * BLK)
            part = [conc[k, at, lanes] for k in range(cats)]
            height = [thick[k, at, lanes] for k in range(cats)]
            mask = mask_in[at, lanes].astype(jnp.float32)
            area = total(part)
            inverse = 1.0 / area
            factor = jnp.exp(-2.0 * (1.0 - area)) * (mask * (1.0 / 3.0))
            half = 0.5 * mask
            volume = total([a * h for a, h in zip(part, height)])
            for window in range(windows):
                mean = volume * inverse
                grown = [h + growth_rate / (0.5 + h) + mixing_rate * (mean - h) for h in height]
                height = [jnp.where(live[block], g, h) for g, h in zip(grown, height)]
                volume = total([a * h for a, h in zip(part, height)])
                fields_ref[STATE + 2 * window, at, lanes] = volume * factor
                fields_ref[STATE + 2 * window + 1, at, lanes] = half / (volume + 1.0)
            for k in range(cats):
                thick[k, at, lanes] = height[k]
        writes[c].start()

    small[2].wait()
    small[3].wait()
    for row in range(0, rows, step):
        at = slice(row, row + step)
        mask = mask_in[at].astype(jnp.float32)
        fields_ref[0, at] = velocity[0, at]
        fields_ref[1, at] = velocity[1, at]
        fields_ref[2, at] = (stress[0, at] + stress[1, at]) * mask
        fields_ref[3, at] = (stress[0, at] - stress[1, at]) * mask
        fields_ref[4, at] = (stress[2, at] + stress[2, at]) * mask

    count = fields_ref.shape[0]
    per = LANES // margin
    slot_of_lane = lax.broadcasted_iota(jnp.int32, (rows, LANES), 1) // margin
    eastward = even("lon")
    for group in range(lon_x_ref.shape[1] // LANES):
        east = jnp.zeros((rows, LANES), jnp.float32)
        west = jnp.zeros((rows, LANES), jnp.float32)
        for slot in range(min(per, count - group * per)):
            field = group * per + slot
            east, west = add_slot(
                east, west, fields_ref.at[field], slot_of_lane == slot, slot * margin, margin
            )
        store_sides(lon_x_ref, lon_y_ref, group, east, west, eastward)
    depths = field_depths(margin, windows)
    groups = message_groups(range(count), depths)
    northward = even("lat")

    def value_of(field, at):
        return fields_ref[field, at, :]

    pack_rows(lat_x_ref, 0, groups, depths, value_of, northward, rows)
    pack_rows(lat_y_ref, 0, groups, depths, value_of, jnp.logical_not(northward), rows)

    for copy in small[4:]:
        copy.wait()
    own_weights = weights[:, :rows]
    for w in range(windows):
        for k in range(2):
            current_ref[w, k] = wind[w, k].astype(jnp.float32) + jnp.dot(
                own_weights, ocean[w, k], preferred_element_type=jnp.float32
            )
    square = (rows, rows)
    diagonal = lax.broadcasted_iota(jnp.int32, square, 0) == lax.broadcasted_iota(
        jnp.int32, square, 1
    )
    up = offset[...] > 0
    for number, north in enumerate((northward, jnp.logical_not(northward))):
        wanted = jnp.where(north, up.astype(jnp.int32), 1 - up.astype(jnp.int32)) > 0
        pick = jnp.where(diagonal & wanted, 1.0, 0.0).astype(jnp.bfloat16)
        side_ref[:, number * rows : (number + 1) * rows] = jnp.dot(
            pick, weights[:, rows:], preferred_element_type=jnp.float32
        ).astype(jnp.bfloat16)

    for copy in writes:
        copy.wait()


def add_slot(east, west, field_ref, here, shift, margin):
    cols = field_ref.shape[1]
    last = pltpu.roll(field_ref[:, cols - LANES :], (shift + margin) % LANES, 1)
    leading = field_ref[:, :LANES]
    if shift:
        leading = pltpu.roll(leading, shift, 1)
    return jnp.where(here, last, east), jnp.where(here, leading, west)


def store_sides(x_ref, y_ref, group, east, west, eastward):
    lanes = slice(group * LANES, (group + 1) * LANES)
    x_ref[:, lanes] = jnp.where(eastward, east, west).astype(jnp.bfloat16)
    y_ref[:, lanes] = jnp.where(eastward, west, east).astype(jnp.bfloat16)


def force_kernel(
    margin,
    early,
    side_ref,
    tile_x_ref,
    tile_y_ref,
    current_ref,
    fields_ref,
    lon_x_in,
    lon_y_in,
    early_y_in,
    force_ref,
    lon_x_ref,
    lon_y_ref,
    lat_x_ref,
    lat_y_ref,
    early_y_ref,
):
    windows, _, rows, cols = current_ref.shape
    side_x = side_ref[:, :rows]
    side_y = side_ref[:, rows:]

    def dot(a, b):
        return jnp.dot(a, b, preferred_element_type=jnp.float32)

    for w in range(windows):
        b = fields_ref[STATE + 2 * w + 1]
        for k in range(2):
            current = dot(side_x, tile_x_ref[w, k]) + dot(side_y, tile_y_ref[w, k])
            force_ref[2 * w + k] = b * (current_ref[w, k] + current)

    per = LANES // margin
    count = early + force_ref.shape[0]
    slot_of_lane = lax.broadcasted_iota(jnp.int32, (rows, LANES), 1) // margin
    eastward = even("lon")
    for group in range(lon_x_ref.shape[1] // LANES):
        lanes = slice(group * LANES, (group + 1) * LANES)
        x = lon_x_in[:, lanes].astype(jnp.float32)
        y = lon_y_in[:, lanes].astype(jnp.float32)
        east, west = jnp.where(eastward, x, y), jnp.where(eastward, y, x)
        for field in range(max(early, group * per), min(count, (group + 1) * per)):
            slot = field - group * per
            east, west = add_slot(
                east, west, force_ref.at[field - early], slot_of_lane == slot, slot * margin, margin
            )
        store_sides(lon_x_ref, lon_y_ref, group, east, west, eastward)

    depths = field_depths(margin, windows)
    groups = message_groups(range(early, count), depths)
    northward = even("lat")

    def value_of(field, at):
        return force_ref[field - early, at, :]

    for ref, north in ((lat_x_ref, northward), (lat_y_ref, jnp.logical_not(northward))):
        pack_rows(ref, 0, groups, depths, value_of, north, rows)
    early_y_ref[...] = early_y_in[...]


def corner_kernel(
    margin, rows, lat_x_in, lat_y_in, lon_x_ref, lon_y_ref, early_x_ref, lat_x_ref, lat_y_ref
):
    for old_ref, ref, north in (
        (lat_x_in, lat_x_ref, even("lat")),
        (lat_y_in, lat_y_ref, jnp.logical_not(even("lat"))),
    ):
        row, cols = old_ref.shape
        ref[:row] = old_ref[...]
        start = pl.multiple_of(jnp.where(north, rows - margin, 0), GROUP)
        for lon_ref in (lon_x_ref, lon_y_ref):
            packed = lon_ref.shape[1]
            ref[row : row + margin, :packed] = lon_ref[pl.ds(start, margin), :]
            if packed < cols:
                ref[row : row + margin, packed:] = jnp.zeros((margin, cols - packed), ref.dtype)
            row += margin


def place(refs, early, field, tile, row, value):
    velocity, stress, strength, keep, push, force = refs
    at = pl.ds(row, value.shape[0])
    if field < 2:
        velocity[0, field, tile, at, :] = value
    elif field < STATE:
        stress[0, field - 2, tile, at, :] = value
    elif field >= early:
        window, kind = divmod(field - early, 2)
        force[window, kind, tile, at, :] = value
    else:
        window, kind = divmod(field - STATE, 2)
        if kind == 0:
            strength[window, tile, at, :] = value
        else:
            push[window, tile, at, :] = value * 0.25
            keep[window, tile, at, :] = jnp.where(value > 0.0, 1.0 - value, 0.0)


def place_sides(refs, early, count, margin, x, y, row):
    last = refs[0].shape[2] - 1
    per = LANES // margin
    wide = lax.broadcasted_iota(jnp.int32, (x.shape[0], LANES), 1)
    from_x_is_east = even("lon")
    for group in range(x.shape[1] // LANES):
        lanes = slice(group * LANES, (group + 1) * LANES)
        x_now, y_now = x[:, lanes], y[:, lanes]
        east = jnp.where(from_x_is_east, x_now, y_now)
        west = jnp.where(from_x_is_east, y_now, x_now)
        for slot in range(min(per, count - group * per)):
            shift = slot * margin
            back = (LANES - margin - shift) % LANES
            e = pltpu.roll(east, LANES - shift, 1) if shift else east
            w = pltpu.roll(west, back, 1) if back else west
            value = jnp.where(wide < margin, e, jnp.where(wide >= LANES - margin, w, 0.0))
            place(refs, early, group * per + slot, last, row, value)


def across(values):
    tiles = len(values)
    lane = lax.broadcasted_iota(jnp.int32, values[0].shape, 1)
    ahead = [pltpu.roll(x, LANES - 1, 1) for x in values]
    behind = [pltpu.roll(x, 1, 1) for x in values]
    return [
        jnp.where(lane == LANES - 1, ahead[(j + 1) % tiles], ahead[j])
        - jnp.where(lane == 0, behind[j - 1], behind[j])
        for j in range(tiles)
    ]


def stress_rows(refs, step, window, row):
    velocity, stress, strength, _, _, _ = refs
    every = range(velocity.shape[2])
    at, north, south = pl.ds(row, 8), pl.ds(row + 1, 8), pl.ds(row - 1, 8)
    u_x = across([velocity[step, 0, j, at, :] for j in every])
    v_x = across([velocity[step, 1, j, at, :] for j in every])
    for j in every:
        u_y = velocity[step, 0, j, north, :] - velocity[step, 0, j, south, :]
        v_y = velocity[step, 1, j, north, :] - velocity[step, 1, j, south, :]
        shear = u_y + v_x[j]
        spread = u_x[j] + v_y
        tension = u_x[j] - v_y
        tension4 = tension * 0.25
        shear4 = shear * 0.25
        squares = spread * spread + tension * tension4 + (shear * shear4 + 1.0)
        k = strength[window, j, at, :]
        kr = k * lax.rsqrt(squares)
        old = [stress[step, i, j, at, :] * (2.0 / 3.0) for i in range(3)]
        stress[step + 1, 0, j, at, :] = old[0] + (kr * (spread + tension4) - k)
        stress[step + 1, 1, j, at, :] = old[1] + (kr * (spread - tension4) - k)
        stress[step + 1, 2, j, at, :] = old[2] + kr * shear4


def velocity_rows(refs, step, window, row):
    velocity, stress, _, keep, push, force = refs
    every = range(velocity.shape[2])
    at, north, south = pl.ds(row, 8), pl.ds(row + 1, 8), pl.ds(row - 1, 8)
    now = step + 1
    p_x = across([stress[now, 0, j, at, :] for j in every])
    t_x = across([stress[now, 2, j, at, :] for j in every])
    for j in every:
        q_y = stress[now, 1, j, north, :] - stress[now, 1, j, south, :]
        t_y = stress[now, 2, j, north, :] - stress[now, 2, j, south, :]
        a = keep[window, j, at, :]
        b = push[window, j, at, :]
        velocity[now, 0, j, at, :] = (
            a * velocity[step, 0, j, at, :] + b * (p_x[j] + t_y) + force[window, 0, j, at, :]
        )
        velocity[now, 1, j, at, :] = (
            a * velocity[step, 1, j, at, :] + b * (t_x[j] + q_y) + force[window, 1, j, at, :]
        )


def write_rows(refs, out_hbm, stage, sem, margin, begin, height, which):
    values = refs[which]
    last = values.shape[0] - 1
    first = 2 * which
    for tile in range(stage.shape[2] // LANES):
        lanes = slice(tile * LANES, (tile + 1) * LANES)
        for row in range(0, height, 8):
            to = slice(row, row + 8)
            at = slice(margin + begin + row, margin + begin + row + 8)
            now = [values[last, i, tile, at, :] for i in range(values.shape[1])]
            if which:
                now = [(now[0] + now[1]) * 0.5, (now[0] - now[1]) * 0.5, now[2] * 0.5]
            for i, value in enumerate(now):
                stage[first + i, to, lanes] = value
    copy = pltpu.make_async_copy(
        stage.at[first : first + values.shape[1]],
        out_hbm[which].at[:, pl.ds(begin, height)],
        sem.at[which],
    )
    copy.start()
    return [copy]


def place_rows(refs, early, fields, margin, rows, lat_count, x_ref, y_ref):
    depths = field_depths(margin, refs[2].shape[0])
    me = lax.axis_index("lat")
    sides = []
    for ref, north in ((x_ref, even("lat")), (y_ref, jnp.logical_not(even("lat")))):
        exists = jnp.where(north, me < lat_count - 1, me > 0)

        def read(at, ref=ref, exists=exists):
            return jnp.where(exists, ref[at].astype(jnp.float32), 0.0)

        row = 0
        for group in message_groups(fields, depths):
            height = sum(depths[f] for f in group)
            value = read(slice(row, row + height))
            begin = 0
            for field in group:
                depth = depths[field]
                to = pl.multiple_of(jnp.where(north, margin + rows, margin - depth), 8)
                for tile in range(refs[0].shape[2] - 1):
                    lanes = slice(tile * LANES, (tile + 1) * LANES)
                    place(refs, early, field, tile, to, value[begin : begin + depth, lanes])
                begin += depth
            row += height
        sides.append((north, read, row))
    return sides


def interior_kernel(
    margin, lat_count, fields_ref, force_ref, lon_x_ref, lon_y_ref, early_x_ref, early_y_ref, *refs
):
    early, rows, cols = fields_ref.shape
    count = early + force_ref.shape[0]
    windows = refs[2].shape[0]
    for field in range(count):
        for tile in range(cols // LANES):
            lanes = slice(tile * LANES, (tile + 1) * LANES)
            own = fields_ref[field, :, lanes] if field < early else force_ref[field - early, :, lanes]
            place(refs, early, field, tile, margin, own)
    lon_x, lon_y = lon_x_ref[...].astype(jnp.float32), lon_y_ref[...].astype(jnp.float32)
    place_sides(refs, early, count, margin, lon_x, lon_y, margin)
    place_rows(refs, early, range(early), margin, rows, lat_count, early_x_ref, early_y_ref)
    for window in range(windows):
        lost = 2 * SUB * window
        row_list = range(margin + lost, margin + rows - lost, 8)

        def subcycle(number, carry):
            step = window * SUB + number
            for row in row_list:
                stress_rows(refs, step, window, row)
            for row in row_list:
                velocity_rows(refs, step, window, row)
            return carry

        lax.fori_loop(0, SUB, subcycle, 0)


def rim_kernel(margin, early, count, lat_count, *args):
    lat_x_ref, lat_y_ref = args[:2]
    refs = args[2:8]
    out_hbm = args[8:10]
    stages, sems = args[16:19], args[19]
    windows = refs[2].shape[0]
    _, rows, cols = out_hbm[0].shape
    inner = rows - 2 * margin
    copies = []
    for which in range(2):
        copies += write_rows(refs, out_hbm, stages[2], sems.at[2], margin, margin, inner, which)
    bottom = margin + rows
    packed = -(-count // (LANES // margin)) * LANES
    late = range(early, count)
    for north, read, row in place_rows(
        refs, early, late, margin, rows, lat_count, lat_x_ref, lat_y_ref
    ):
        to = pl.multiple_of(jnp.where(north, bottom, 0), 8)
        east, west = (read(slice(at, at + margin))[:, :packed] for at in (row, row + margin))
        place_sides(refs, early, count, margin, east, west, to)

    def half_step(step, half):
        done = 2 * step + 1 + half
        rows_now = velocity_rows if half else stress_rows
        for first in range(0, margin, 8):
            rows_now(refs, step, step // SUB, done + first)
            rows_now(refs, step, step // SUB, bottom - done + first)

    last = SUB * windows - 1
    for step in range(last):
        half_step(step, 0)
        half_step(step, 1)
    half_step(last, 0)
    ends = list(enumerate((0, rows - margin)))
    for number, begin in ends:
        copies += write_rows(refs, out_hbm, stages[number], sems.at[number], margin, begin, margin, 1)
    half_step(last, 1)
    for number, begin in ends:
        copies += write_rows(refs, out_hbm, stages[number], sems.at[number], margin, begin, margin, 0)
    for copy in copies:
        copy.wait()


def params():
    return pltpu.CompilerParams(vmem_limit_bytes=VMEM_LIMIT)


def lon_swaps(first):
    n = lax.axis_size("lon")
    if n % 2:
        raise ValueError("odd ring")
    pairs = [(i, (i + 1) % n) for i in range(first, n, 2)]
    return pairs + [(j, i) for i, j in pairs]


def lat_swaps(first):
    m, n = lax.axis_size("lat"), lax.axis_size("lon")
    partner = {}
    for i in range(m):
        north = i + 1 if (i - first) % 2 == 0 else i - 1
        for k in range(n):
            to = (north, k) if 0 <= north < m else (i, k ^ 1)
            partner[k * m + i] = to[1] * m + to[0]
    return list(partner.items())


def lon_exchange(x, y):
    return lax.ppermute(x, "lon", lon_swaps(0)), lax.ppermute(y, "lon", lon_swaps(1))


def lat_exchange(x, first):
    return lax.ppermute(x, ("lon", "lat"), lat_swaps(first))


def shape(dims, dtype=jnp.float32):
    return jax.ShapeDtypeStruct(dims, dtype)


def local(
    velocity,
    stress,
    thickness,
    concentration,
    land_mask,
    covered,
    ocean_current,
    wind_stress,
    regrid_weights,
    tile_offset,
):
    _, rows, cols = velocity.shape
    windows = wind_stress.shape[0]
    margin = 2 * SUB * windows
    early = STATE + 2 * windows
    count = early + 2 * windows
    tiles = cols // LANES + 1
    packed = -(-count // (LANES // margin)) * LANES
    depths = field_depths(margin, windows)
    early_rows = sum(depths[:early])
    late_rows = sum(depths[early:])
    bf16 = jnp.bfloat16

    tile_x, tile_y = lat_exchange(ocean_current, 0), lat_exchange(ocean_current, 1)

    whole = pl.BlockSpec(memory_space=pltpu.VMEM)
    anywhere = pl.BlockSpec(memory_space=pl.ANY)
    chunks = rows // GROUP
    thick_out, fields, current, side, lon_x, lon_y, lat_x, lat_y = pl.pallas_call(
        functools.partial(local_kernel, margin),
        out_shape=(
            shape(thickness.shape),
            shape((early, rows, cols)),
            shape(wind_stress.shape),
            shape((rows, 2 * rows), bf16),
            shape((rows, packed), bf16),
            shape((rows, packed), bf16),
            shape((early_rows, cols), bf16),
            shape((early_rows, cols), bf16),
        ),
        in_specs=[anywhere] * 10,
        out_specs=(anywhere,) + (whole,) * 7,
        scratch_shapes=[
            pltpu.SMEM(covered.shape, jnp.int32),
            pltpu.VMEM((1, rows), jnp.int32),
            pltpu.VMEM(regrid_weights.shape, bf16),
            pltpu.VMEM(thickness.shape, jnp.float32),
            pltpu.VMEM(thickness.shape, jnp.float32),
            pltpu.VMEM(land_mask.shape, jnp.int32),
            pltpu.VMEM(velocity.shape, jnp.float32),
            pltpu.VMEM(stress.shape, jnp.float32),
            pltpu.VMEM(ocean_current.shape, bf16),
            pltpu.VMEM(wind_stress.shape, bf16),
            pltpu.SemaphoreType.DMA((8,)),
            pltpu.SemaphoreType.DMA((chunks,)),
            pltpu.SemaphoreType.DMA((chunks,)),
            pltpu.SemaphoreType.DMA((chunks,)),
        ],
        compiler_params=params(),
        cost_estimate=pl.CostEstimate(
            flops=100 * thickness.size, bytes_accessed=12 * thickness.size, transcendentals=0
        ),
        name="local",
    )(
        *(
            pltpu.with_memory_space_constraint(x, pltpu.HBM)
            for x in (
                covered,
                tile_offset.reshape(1, rows),
                regrid_weights,
                thickness,
                concentration,
                land_mask,
                velocity,
                stress,
                ocean_current,
                wind_stress,
            )
        )
    )

    early_x = lat_exchange(lat_x, 0)
    force, lon_x, lon_y, late_x, late_y, lat_y = pl.pallas_call(
        functools.partial(force_kernel, margin, early),
        out_shape=(
            shape((2 * windows, rows, cols)),
            shape((rows, packed), bf16),
            shape((rows, packed), bf16),
            shape((late_rows, cols), bf16),
            shape((late_rows, cols), bf16),
            shape((early_rows, cols), bf16),
        ),
        in_specs=[whole] * 8,
        out_specs=(whole,) * 6,
        compiler_params=params(),
        cost_estimate=pl.CostEstimate(flops=1, bytes_accessed=1, transcendentals=0),
        name="force",
    )(side, tile_x, tile_y, current, fields, lon_x, lon_y, lat_y)

    lon_x, lon_y = lon_exchange(lon_x, lon_y)
    early_y = lat_exchange(lat_y, 1)
    message = shape((late_rows + 2 * margin, cols), bf16)
    late_x, late_y = pl.pallas_call(
        functools.partial(corner_kernel, margin, rows),
        out_shape=(message, message),
        in_specs=[whole] * 5,
        out_specs=(whole,) * 2,
        compiler_params=params(),
        cost_estimate=pl.CostEstimate(flops=1, bytes_accessed=1, transcendentals=0),
        name="corner",
    )(late_x, late_y, lon_x, lon_y, early_x)
    late_x, late_y = lat_exchange(late_x, 0), lat_exchange(late_y, 1)

    steps = SUB * windows

    def widened(*lead):
        return shape((*lead, tiles, rows + 2 * margin, LANES))

    domain = (
        widened(steps + 1, 2),
        widened(steps + 1, 3),
        widened(windows),
        widened(windows),
        widened(windows),
        widened(windows, 2),
    )
    outs = (shape(velocity.shape), shape(stress.shape))
    refs = pl.pallas_call(
        functools.partial(interior_kernel, margin, lax.axis_size("lat")),
        out_shape=domain,
        in_specs=[whole] * 6,
        out_specs=(whole,) * 6,
        compiler_params=params(),
        cost_estimate=pl.CostEstimate(
            flops=60 * steps * rows * cols, bytes_accessed=2**22, transcendentals=0
        ),
        name="interior",
    )(fields, force, lon_x, lon_y, early_x, early_y)

    velocity_out, stress_out = pl.pallas_call(
        functools.partial(rim_kernel, margin, early, count, lax.axis_size("lat")),
        out_shape=(shape(velocity.shape), shape(stress.shape)) + domain,
        in_specs=[whole] * 8,
        out_specs=(anywhere,) * 2 + (whole,) * 6,
        input_output_aliases={2 + i: 2 + i for i in range(6)},
        scratch_shapes=[
            pltpu.VMEM((STATE, margin, cols), jnp.float32),
            pltpu.VMEM((STATE, margin, cols), jnp.float32),
            pltpu.VMEM((STATE, rows - 2 * margin, cols), jnp.float32),
            pltpu.SemaphoreType.DMA((3, 2)),
        ],
        compiler_params=params(),
        name="rim",
    )(late_x, late_y, *refs)[:2]
    return (velocity_out, stress_out, thick_out)


def solution(mesh):
    return jax.shard_map(
        local,
        mesh=mesh,
        in_specs=(
            P(None, "lat", "lon"),
            P(None, "lat", "lon"),
            P(None, "lat", "lon"),
            P(None, "lat", "lon"),
            P("lat", "lon"),
            P("lat", None),
            P(None, None, "lat", "lon"),
            P(None, None, "lat", "lon"),
            P("lat", None),
            P("lat"),
        ),
        out_specs=(P(None, "lat", "lon"), P(None, "lat", "lon"), P(None, "lat", "lon")),
        check_vma=False,
    )
```

```python
import functools

import jax
import jax.numpy as jnp
from jax import lax
from jax.experimental import pallas as pl
from jax.experimental.pallas import tpu as pltpu
from jax.sharding import PartitionSpec as P

BLK = 128
SUB = 4
LANES = 128
GROUP = 16
STATE = 5
VMEM_LIMIT = 16 * 1024 * 1024

growth_rate = 0.3
mixing_rate = 0.3


def total(terms):
    result = terms[0]
    for term in terms[1:]:
        result = result + term
    return result


def field_depths(margin, windows):
    depths = [margin] * STATE
    for copies in (2, 2):
        for window in range(windows):
            depths += [margin - 2 * SUB * window] * copies
    return depths


def message_groups(fields, depths):
    groups, held = [], []
    for field in fields:
        held.append(field)
        if sum(depths[f] for f in held) % GROUP == 0:
            groups.append(held)
            held = []
    return groups + ([held] if held else [])


def even(axis):
    return lax.axis_index(axis) % 2 == 0


def pack_rows(message_ref, row, groups, depths, value_of, northward, rows):
    for group in groups:
        parts = []
        for field in group:
            start = jnp.where(northward, rows - depths[field], 0)
            parts.append(value_of(field, pl.ds(pl.multiple_of(start, 8), depths[field])))
        value = parts[0] if len(parts) == 1 else jnp.concatenate(parts, axis=0)
        message_ref[row : row + value.shape[0]] = value.astype(jnp.bfloat16)
        row += value.shape[0]
    return row


def local_kernel(
    margin,
    covered_hbm,
    offset_hbm,
    weights_hbm,
    thick_hbm,
    conc_hbm,
    mask_hbm,
    velocity_hbm,
    stress_hbm,
    ocean_hbm,
    wind_hbm,
    thick_out_hbm,
    fields_ref,
    current_ref,
    side_ref,
    lon_x_ref,
    lon_y_ref,
    lat_x_ref,
    lat_y_ref,
    covered,
    offset,
    weights,
    thick,
    conc,
    mask_in,
    velocity,
    stress,
    ocean,
    wind,
    in_sems,
    thick_sems,
    conc_sems,
    out_sems,
):
    cats, rows, cols = thick.shape
    windows = wind.shape[0]
    step = GROUP
    chunks = rows // step

    def rows_of(chunk):
        return pl.ds(chunk * step, step)

    small = [
        pltpu.make_async_copy(source, target, in_sems.at[i])
        for i, (source, target) in enumerate(
            (
                (covered_hbm, covered),
                (mask_hbm, mask_in),
                (velocity_hbm, velocity),
                (stress_hbm, stress),
                (ocean_hbm, ocean),
                (wind_hbm, wind),
                (weights_hbm, weights),
                (offset_hbm, offset),
            )
        )
    ]
    pairs = [
        [
            pltpu.make_async_copy(hbm.at[:, rows_of(c)], vmem.at[:, rows_of(c)], sems.at[c])
            for hbm, vmem, sems in ((thick_hbm, thick, thick_sems), (conc_hbm, conc, conc_sems))
        ]
        for c in range(chunks)
    ]
    writes = [
        pltpu.make_async_copy(thick.at[:, rows_of(c)], thick_out_hbm.at[:, rows_of(c)], out_sems.at[c])
        for c in range(chunks)
    ]
    for copy in small[:2] + [copy for pair in pairs for copy in pair] + small[2:]:
        copy.start()

    blocks = cols // BLK
    first = lax.axis_index("lon") * blocks
    small[0].wait()
    live = [covered[0, first + block] > 0 for block in range(blocks)]
    small[1].wait()
    for c in range(chunks):
        at = slice(c * step, (c + 1) * step)
        for copy in pairs[c]:
            copy.wait()
        for block in range(blocks):
            lanes = slice(block * BLK, (block + 1) * BLK)
            part = [conc[k, at, lanes] for k in range(cats)]
            height = [thick[k, at, lanes] for k in range(cats)]
            mask = mask_in[at, lanes].astype(jnp.float32)
            area = total(part)
            inverse = 1.0 / area
            factor = jnp.exp(-2.0 * (1.0 - area)) * (mask * (1.0 / 3.0))
            half = 0.5 * mask
            volume = total([a * h for a, h in zip(part, height)])
            for window in range(windows):
                mean = volume * inverse
                grown = [h + growth_rate / (0.5 + h) + mixing_rate * (mean - h) for h in height]
                height = [jnp.where(live[block], g, h) for g, h in zip(grown, height)]
                volume = total([a * h for a, h in zip(part, height)])
                fields_ref[STATE + 2 * window, at, lanes] = volume * factor
                fields_ref[STATE + 2 * window + 1, at, lanes] = half / (volume + 1.0)
            for k in range(cats):
                thick[k, at, lanes] = height[k]
        writes[c].start()

    small[2].wait()
    small[3].wait()
    for row in range(0, rows, step):
        at = slice(row, row + step)
        mask = mask_in[at].astype(jnp.float32)
        fields_ref[0, at] = velocity[0, at]
        fields_ref[1, at] = velocity[1, at]
        fields_ref[2, at] = (stress[0, at] + stress[1, at]) * mask
        fields_ref[3, at] = (stress[0, at] - stress[1, at]) * mask
        fields_ref[4, at] = (stress[2, at] + stress[2, at]) * mask

    count = fields_ref.shape[0]
    per = LANES // margin
    slot_of_lane = lax.broadcasted_iota(jnp.int32, (rows, LANES), 1) // margin
    eastward = even("lon")
    for group in range(lon_x_ref.shape[1] // LANES):
        east = jnp.zeros((rows, LANES), jnp.float32)
        west = jnp.zeros((rows, LANES), jnp.float32)
        for slot in range(min(per, count - group * per)):
            field = group * per + slot
            east, west = add_slot(
                east, west, fields_ref.at[field], slot_of_lane == slot, slot * margin, margin
            )
        store_sides(lon_x_ref, lon_y_ref, group, east, west, eastward)
    depths = field_depths(margin, windows)
    groups = message_groups(range(count), depths)
    northward = even("lat")

    def value_of(field, at):
        return fields_ref[field, at, :]

    pack_rows(lat_x_ref, 0, groups, depths, value_of, northward, rows)
    pack_rows(lat_y_ref, 0, groups, depths, value_of, jnp.logical_not(northward), rows)

    for copy in small[4:]:
        copy.wait()
    own_weights = weights[:, :rows]
    for w in range(windows):
        for k in range(2):
            current_ref[w, k] = wind[w, k].astype(jnp.float32) + jnp.dot(
                own_weights, ocean[w, k], preferred_element_type=jnp.float32
            )
    square = (rows, rows)
    diagonal = lax.broadcasted_iota(jnp.int32, square, 0) == lax.broadcasted_iota(
        jnp.int32, square, 1
    )
    up = offset[...] > 0
    for number, north in enumerate((northward, jnp.logical_not(northward))):
        wanted = jnp.where(north, up.astype(jnp.int32), 1 - up.astype(jnp.int32)) > 0
        pick = jnp.where(diagonal & wanted, 1.0, 0.0).astype(jnp.bfloat16)
        side_ref[:, number * rows : (number + 1) * rows] = jnp.dot(
            pick, weights[:, rows:], preferred_element_type=jnp.float32
        ).astype(jnp.bfloat16)

    for copy in writes:
        copy.wait()


def add_slot(east, west, field_ref, here, shift, margin):
    cols = field_ref.shape[1]
    last = pltpu.roll(field_ref[:, cols - LANES :], (shift + margin) % LANES, 1)
    leading = field_ref[:, :LANES]
    if shift:
        leading = pltpu.roll(leading, shift, 1)
    return jnp.where(here, last, east), jnp.where(here, leading, west)


def store_sides(x_ref, y_ref, group, east, west, eastward):
    lanes = slice(group * LANES, (group + 1) * LANES)
    x_ref[:, lanes] = jnp.where(eastward, east, west).astype(jnp.bfloat16)
    y_ref[:, lanes] = jnp.where(eastward, west, east).astype(jnp.bfloat16)


def side_kernel(side_ref, tile_ref, current_ref, sum_ref):
    windows, parts, rows, _ = current_ref.shape
    weights = side_ref[:, :rows]
    for w in range(windows):
        for k in range(parts):
            sum_ref[w, k] = current_ref[w, k] + jnp.dot(
                weights, tile_ref[w, k], preferred_element_type=jnp.float32
            )


def force_kernel(
    margin,
    early,
    side_ref,
    tile_ref,
    current_ref,
    fields_ref,
    lon_x_in,
    lon_y_in,
    early_y_in,
    force_ref,
    lon_x_ref,
    lon_y_ref,
    lat_x_ref,
    lat_y_ref,
    early_y_ref,
):
    windows, _, rows, cols = current_ref.shape
    weights = side_ref[:, rows:]
    for w in range(windows):
        b = fields_ref[STATE + 2 * w + 1]
        for k in range(2):
            current = jnp.dot(weights, tile_ref[w, k], preferred_element_type=jnp.float32)
            force_ref[2 * w + k] = b * (current_ref[w, k] + current)

    per = LANES // margin
    count = early + force_ref.shape[0]
    slot_of_lane = lax.broadcasted_iota(jnp.int32, (rows, LANES), 1) // margin
    eastward = even("lon")
    for group in range(lon_x_ref.shape[1] // LANES):
        lanes = slice(group * LANES, (group + 1) * LANES)
        x = lon_x_in[:, lanes].astype(jnp.float32)
        y = lon_y_in[:, lanes].astype(jnp.float32)
        east, west = jnp.where(eastward, x, y), jnp.where(eastward, y, x)
        for field in range(max(early, group * per), min(count, (group + 1) * per)):
            slot = field - group * per
            east, west = add_slot(
                east, west, force_ref.at[field - early], slot_of_lane == slot, slot * margin, margin
            )
        store_sides(lon_x_ref, lon_y_ref, group, east, west, eastward)

    depths = field_depths(margin, windows)
    groups = message_groups(range(early, count), depths)
    northward = even("lat")

    def value_of(field, at):
        return force_ref[field - early, at, :]

    for ref, north in ((lat_x_ref, northward), (lat_y_ref, jnp.logical_not(northward))):
        pack_rows(ref, 0, groups, depths, value_of, north, rows)
    early_y_ref[...] = early_y_in[...]


def corner_kernel(
    margin, rows, lat_x_in, lat_y_in, lon_x_ref, lon_y_ref, early_x_ref, lat_x_ref, lat_y_ref
):
    for old_ref, ref, north in (
        (lat_x_in, lat_x_ref, even("lat")),
        (lat_y_in, lat_y_ref, jnp.logical_not(even("lat"))),
    ):
        row, cols = old_ref.shape
        ref[:row] = old_ref[...]
        start = pl.multiple_of(jnp.where(north, rows - margin, 0), GROUP)
        for lon_ref in (lon_x_ref, lon_y_ref):
            packed = lon_ref.shape[1]
            ref[row : row + margin, :packed] = lon_ref[pl.ds(start, margin), :]
            if packed < cols:
                ref[row : row + margin, packed:] = jnp.zeros((margin, cols - packed), ref.dtype)
            row += margin


def place(refs, early, field, tile, row, value):
    velocity, stress, strength, keep, push, force = refs
    at = pl.ds(row, value.shape[0])
    if field < 2:
        velocity[0, field, tile, at, :] = value
    elif field < STATE:
        stress[0, field - 2, tile, at, :] = value
    elif field >= early:
        window, kind = divmod(field - early, 2)
        force[window, kind, tile, at, :] = value
    else:
        window, kind = divmod(field - STATE, 2)
        if kind == 0:
            strength[window, tile, at, :] = value
        else:
            push[window, tile, at, :] = value * 0.25
            keep[window, tile, at, :] = jnp.where(value > 0.0, 1.0 - value, 0.0)


def place_sides(refs, early, count, margin, x, y, row):
    last = refs[0].shape[2] - 1
    per = LANES // margin
    wide = lax.broadcasted_iota(jnp.int32, (x.shape[0], LANES), 1)
    from_x_is_east = even("lon")
    for group in range(x.shape[1] // LANES):
        lanes = slice(group * LANES, (group + 1) * LANES)
        x_now, y_now = x[:, lanes], y[:, lanes]
        east = jnp.where(from_x_is_east, x_now, y_now)
        west = jnp.where(from_x_is_east, y_now, x_now)
        for slot in range(min(per, count - group * per)):
            shift = slot * margin
            back = (LANES - margin - shift) % LANES
            e = pltpu.roll(east, LANES - shift, 1) if shift else east
            w = pltpu.roll(west, back, 1) if back else west
            value = jnp.where(wide < margin, e, jnp.where(wide >= LANES - margin, w, 0.0))
            place(refs, early, group * per + slot, last, row, value)


def across(values):
    tiles = len(values)
    lane = lax.broadcasted_iota(jnp.int32, values[0].shape, 1)
    ahead = [pltpu.roll(x, LANES - 1, 1) for x in values]
    behind = [pltpu.roll(x, 1, 1) for x in values]
    return [
        jnp.where(lane == LANES - 1, ahead[(j + 1) % tiles], ahead[j])
        - jnp.where(lane == 0, behind[j - 1], behind[j])
        for j in range(tiles)
    ]


def stress_rows(refs, step, window, row):
    velocity, stress, strength, _, _, _ = refs
    every = range(velocity.shape[2])
    at, north, south = pl.ds(row, 8), pl.ds(row + 1, 8), pl.ds(row - 1, 8)
    u_x = across([velocity[step, 0, j, at, :] for j in every])
    v_x = across([velocity[step, 1, j, at, :] for j in every])
    for j in every:
        u_y = velocity[step, 0, j, north, :] - velocity[step, 0, j, south, :]
        v_y = velocity[step, 1, j, north, :] - velocity[step, 1, j, south, :]
        shear = u_y + v_x[j]
        spread = u_x[j] + v_y
        tension = u_x[j] - v_y
        tension4 = tension * 0.25
        shear4 = shear * 0.25
        squares = spread * spread + tension * tension4 + (shear * shear4 + 1.0)
        k = strength[window, j, at, :]
        kr = k * lax.rsqrt(squares)
        old = [stress[step, i, j, at, :] * (2.0 / 3.0) for i in range(3)]
        stress[step + 1, 0, j, at, :] = old[0] + (kr * (spread + tension4) - k)
        stress[step + 1, 1, j, at, :] = old[1] + (kr * (spread - tension4) - k)
        stress[step + 1, 2, j, at, :] = old[2] + kr * shear4


def velocity_rows(refs, step, window, row):
    velocity, stress, _, keep, push, force = refs
    every = range(velocity.shape[2])
    at, north, south = pl.ds(row, 8), pl.ds(row + 1, 8), pl.ds(row - 1, 8)
    now = step + 1
    p_x = across([stress[now, 0, j, at, :] for j in every])
    t_x = across([stress[now, 2, j, at, :] for j in every])
    for j in every:
        q_y = stress[now, 1, j, north, :] - stress[now, 1, j, south, :]
        t_y = stress[now, 2, j, north, :] - stress[now, 2, j, south, :]
        a = keep[window, j, at, :]
        b = push[window, j, at, :]
        velocity[now, 0, j, at, :] = (
            a * velocity[step, 0, j, at, :] + b * (p_x[j] + t_y) + force[window, 0, j, at, :]
        )
        velocity[now, 1, j, at, :] = (
            a * velocity[step, 1, j, at, :] + b * (t_x[j] + q_y) + force[window, 1, j, at, :]
        )


def write_rows(refs, out_hbm, stage, sem, margin, begin, height, which):
    values = refs[which]
    last = values.shape[0] - 1
    first = 2 * which
    for tile in range(stage.shape[2] // LANES):
        lanes = slice(tile * LANES, (tile + 1) * LANES)
        for row in range(0, height, 8):
            to = slice(row, row + 8)
            at = slice(margin + begin + row, margin + begin + row + 8)
            now = [values[last, i, tile, at, :] for i in range(values.shape[1])]
            if which:
                now = [(now[0] + now[1]) * 0.5, (now[0] - now[1]) * 0.5, now[2] * 0.5]
            for i, value in enumerate(now):
                stage[first + i, to, lanes] = value
    copy = pltpu.make_async_copy(
        stage.at[first : first + values.shape[1]],
        out_hbm[which].at[:, pl.ds(begin, height)],
        sem.at[which],
    )
    copy.start()
    return [copy]


def place_rows(refs, early, fields, margin, rows, lat_count, x_ref, y_ref):
    depths = field_depths(margin, refs[2].shape[0])
    me = lax.axis_index("lat")
    sides = []
    for ref, north in ((x_ref, even("lat")), (y_ref, jnp.logical_not(even("lat")))):
        exists = jnp.where(north, me < lat_count - 1, me > 0)

        def read(at, ref=ref, exists=exists):
            return jnp.where(exists, ref[at].astype(jnp.float32), 0.0)

        row = 0
        for group in message_groups(fields, depths):
            height = sum(depths[f] for f in group)
            value = read(slice(row, row + height))
            begin = 0
            for field in group:
                depth = depths[field]
                to = pl.multiple_of(jnp.where(north, margin + rows, margin - depth), 8)
                for tile in range(refs[0].shape[2] - 1):
                    lanes = slice(tile * LANES, (tile + 1) * LANES)
                    place(refs, early, field, tile, to, value[begin : begin + depth, lanes])
                begin += depth
            row += height
        sides.append((north, read, row))
    return sides


def interior_kernel(
    margin, lat_count, fields_ref, force_ref, lon_x_ref, lon_y_ref, early_x_ref, early_y_ref, *refs
):
    early, rows, cols = fields_ref.shape
    count = early + force_ref.shape[0]
    windows = refs[2].shape[0]
    for field in range(count):
        for tile in range(cols // LANES):
            lanes = slice(tile * LANES, (tile + 1) * LANES)
            own = fields_ref[field, :, lanes] if field < early else force_ref[field - early, :, lanes]
            place(refs, early, field, tile, margin, own)
    lon_x, lon_y = lon_x_ref[...].astype(jnp.float32), lon_y_ref[...].astype(jnp.float32)
    place_sides(refs, early, count, margin, lon_x, lon_y, margin)
    place_rows(refs, early, range(early), margin, rows, lat_count, early_x_ref, early_y_ref)
    for window in range(windows):
        lost = 2 * SUB * window
        row_list = range(margin + lost, margin + rows - lost, 8)

        def subcycle(number, carry):
            step = window * SUB + number
            for row in row_list:
                stress_rows(refs, step, window, row)
            for row in row_list:
                velocity_rows(refs, step, window, row)
            return carry

        lax.fori_loop(0, SUB, subcycle, 0)


def rim_kernel(margin, early, count, lat_count, *args):
    lat_x_ref, lat_y_ref = args[:2]
    refs = args[2:8]
    out_hbm = args[8:10]
    stages, sems = args[16:19], args[19]
    windows = refs[2].shape[0]
    _, rows, cols = out_hbm[0].shape
    inner = rows - 2 * margin
    copies = []
    for which in range(2):
        copies += write_rows(refs, out_hbm, stages[2], sems.at[2], margin, margin, inner, which)
    bottom = margin + rows
    packed = -(-count // (LANES // margin)) * LANES
    late = range(early, count)
    for north, read, row in place_rows(
        refs, early, late, margin, rows, lat_count, lat_x_ref, lat_y_ref
    ):
        to = pl.multiple_of(jnp.where(north, bottom, 0), 8)
        east, west = (read(slice(at, at + margin))[:, :packed] for at in (row, row + margin))
        place_sides(refs, early, count, margin, east, west, to)

    def half_step(step, half):
        done = 2 * step + 1 + half
        rows_now = velocity_rows if half else stress_rows
        for first in range(0, margin, 8):
            rows_now(refs, step, step // SUB, done + first)
            rows_now(refs, step, step // SUB, bottom - done + first)

    last = SUB * windows - 1
    for step in range(last):
        half_step(step, 0)
        half_step(step, 1)
    half_step(last, 0)
    ends = list(enumerate((0, rows - margin)))
    for number, begin in ends:
        copies += write_rows(refs, out_hbm, stages[number], sems.at[number], margin, begin, margin, 1)
    half_step(last, 1)
    for number, begin in ends:
        copies += write_rows(refs, out_hbm, stages[number], sems.at[number], margin, begin, margin, 0)
    for copy in copies:
        copy.wait()


def params():
    return pltpu.CompilerParams(vmem_limit_bytes=VMEM_LIMIT)


def lon_swaps(first):
    n = lax.axis_size("lon")
    if n % 2:
        raise ValueError("odd ring")
    pairs = [(i, (i + 1) % n) for i in range(first, n, 2)]
    return pairs + [(j, i) for i, j in pairs]


def lat_swaps(first):
    m, n = lax.axis_size("lat"), lax.axis_size("lon")
    partner = {}
    for i in range(m):
        north = i + 1 if (i - first) % 2 == 0 else i - 1
        for k in range(n):
            to = (north, k) if 0 <= north < m else (i, k ^ 1)
            partner[k * m + i] = to[1] * m + to[0]
    return list(partner.items())


def lon_exchange(x, y):
    return lax.ppermute(x, "lon", lon_swaps(0)), lax.ppermute(y, "lon", lon_swaps(1))


def lat_exchange(x, first):
    return lax.ppermute(x, ("lon", "lat"), lat_swaps(first))


def shape(dims, dtype=jnp.float32):
    return jax.ShapeDtypeStruct(dims, dtype)


def local(
    velocity,
    stress,
    thickness,
    concentration,
    land_mask,
    covered,
    ocean_current,
    wind_stress,
    regrid_weights,
    tile_offset,
):
    _, rows, cols = velocity.shape
    windows = wind_stress.shape[0]
    margin = 2 * SUB * windows
    early = STATE + 2 * windows
    count = early + 2 * windows
    tiles = cols // LANES + 1
    packed = -(-count // (LANES // margin)) * LANES
    depths = field_depths(margin, windows)
    early_rows = sum(depths[:early])
    late_rows = sum(depths[early:])
    bf16 = jnp.bfloat16

    tile_x, tile_y = lat_exchange(ocean_current, 0), lat_exchange(ocean_current, 1)

    whole = pl.BlockSpec(memory_space=pltpu.VMEM)
    anywhere = pl.BlockSpec(memory_space=pl.ANY)
    chunks = rows // GROUP
    thick_out, fields, current, side, lon_x, lon_y, lat_x, lat_y = pl.pallas_call(
        functools.partial(local_kernel, margin),
        out_shape=(
            shape(thickness.shape),
            shape((early, rows, cols)),
            shape(wind_stress.shape),
            shape((rows, 2 * rows), bf16),
            shape((rows, packed), bf16),
            shape((rows, packed), bf16),
            shape((early_rows, cols), bf16),
            shape((early_rows, cols), bf16),
        ),
        in_specs=[anywhere] * 10,
        out_specs=(anywhere,) + (whole,) * 7,
        scratch_shapes=[
            pltpu.SMEM(covered.shape, jnp.int32),
            pltpu.VMEM((1, rows), jnp.int32),
            pltpu.VMEM(regrid_weights.shape, bf16),
            pltpu.VMEM(thickness.shape, jnp.float32),
            pltpu.VMEM(thickness.shape, jnp.float32),
            pltpu.VMEM(land_mask.shape, jnp.int32),
            pltpu.VMEM(velocity.shape, jnp.float32),
            pltpu.VMEM(stress.shape, jnp.float32),
            pltpu.VMEM(ocean_current.shape, bf16),
            pltpu.VMEM(wind_stress.shape, bf16),
            pltpu.SemaphoreType.DMA((8,)),
            pltpu.SemaphoreType.DMA((chunks,)),
            pltpu.SemaphoreType.DMA((chunks,)),
            pltpu.SemaphoreType.DMA((chunks,)),
        ],
        compiler_params=params(),
        cost_estimate=pl.CostEstimate(
            flops=100 * thickness.size, bytes_accessed=12 * thickness.size, transcendentals=0
        ),
        name="local",
    )(
        *(
            pltpu.with_memory_space_constraint(x, pltpu.HBM)
            for x in (
                covered,
                tile_offset.reshape(1, rows),
                regrid_weights,
                thickness,
                concentration,
                land_mask,
                velocity,
                stress,
                ocean_current,
                wind_stress,
            )
        )
    )

    early_x = lat_exchange(lat_x, 0)
    current = pl.pallas_call(
        side_kernel,
        out_shape=shape(wind_stress.shape),
        in_specs=[whole] * 3,
        out_specs=whole,
        compiler_params=params(),
        cost_estimate=pl.CostEstimate(flops=1, bytes_accessed=1, transcendentals=0),
        name="side",
    )(side, tile_x, current)
    force, lon_x, lon_y, late_x, late_y, lat_y = pl.pallas_call(
        functools.partial(force_kernel, margin, early),
        out_shape=(
            shape((2 * windows, rows, cols)),
            shape((rows, packed), bf16),
            shape((rows, packed), bf16),
            shape((late_rows, cols), bf16),
            shape((late_rows, cols), bf16),
            shape((early_rows, cols), bf16),
        ),
        in_specs=[whole] * 7,
        out_specs=(whole,) * 6,
        compiler_params=params(),
        cost_estimate=pl.CostEstimate(flops=1, bytes_accessed=1, transcendentals=0),
        name="force",
    )(side, tile_y, current, fields, lon_x, lon_y, lat_y)

    lon_x, lon_y = lon_exchange(lon_x, lon_y)
    early_y = lat_exchange(lat_y, 1)
    message = shape((late_rows + 2 * margin, cols), bf16)
    late_x, late_y = pl.pallas_call(
        functools.partial(corner_kernel, margin, rows),
        out_shape=(message, message),
        in_specs=[whole] * 5,
        out_specs=(whole,) * 2,
        compiler_params=params(),
        cost_estimate=pl.CostEstimate(flops=1, bytes_accessed=1, transcendentals=0),
        name="corner",
    )(late_x, late_y, lon_x, lon_y, early_x)
    late_x, late_y = lat_exchange(late_x, 0), lat_exchange(late_y, 1)

    steps = SUB * windows

    def widened(*lead):
        return shape((*lead, tiles, rows + 2 * margin, LANES))

    domain = (
        widened(steps + 1, 2),
        widened(steps + 1, 3),
        widened(windows),
        widened(windows),
        widened(windows),
        widened(windows, 2),
    )
    outs = (shape(velocity.shape), shape(stress.shape))
    refs = pl.pallas_call(
        functools.partial(interior_kernel, margin, lax.axis_size("lat")),
        out_shape=domain,
        in_specs=[whole] * 6,
        out_specs=(whole,) * 6,
        compiler_params=params(),
        cost_estimate=pl.CostEstimate(
            flops=60 * steps * rows * cols, bytes_accessed=2**22, transcendentals=0
        ),
        name="interior",
    )(fields, force, lon_x, lon_y, early_x, early_y)

    velocity_out, stress_out = pl.pallas_call(
        functools.partial(rim_kernel, margin, early, count, lax.axis_size("lat")),
        out_shape=(shape(velocity.shape), shape(stress.shape)) + domain,
        in_specs=[whole] * 8,
        out_specs=(anywhere,) * 2 + (whole,) * 6,
        input_output_aliases={2 + i: 2 + i for i in range(6)},
        scratch_shapes=[
            pltpu.VMEM((STATE, margin, cols), jnp.float32),
            pltpu.VMEM((STATE, margin, cols), jnp.float32),
            pltpu.VMEM((STATE, rows - 2 * margin, cols), jnp.float32),
            pltpu.SemaphoreType.DMA((3, 2)),
        ],
        compiler_params=params(),
        name="rim",
    )(late_x, late_y, *refs)[:2]
    return (velocity_out, stress_out, thick_out)


def solution(mesh):
    return jax.shard_map(
        local,
        mesh=mesh,
        in_specs=(
            P(None, "lat", "lon"),
            P(None, "lat", "lon"),
            P(None, "lat", "lon"),
            P(None, "lat", "lon"),
            P("lat", "lon"),
            P("lat", None),
            P(None, None, "lat", "lon"),
            P(None, None, "lat", "lon"),
            P("lat", None),
            P("lat"),
        ),
        out_specs=(P(None, "lat", "lon"), P(None, "lat", "lon"), P(None, "lat", "lon")),
        check_vma=False,
    )
```

```python
import functools

import jax
import jax.numpy as jnp
from jax import lax
from jax.experimental import pallas as pl
from jax.experimental.pallas import tpu as pltpu
from jax.sharding import PartitionSpec as P

BLK = 128
SUB = 4
LANES = 128
GROUP = 16
STATE = 5
VMEM_LIMIT = 16 * 1024 * 1024

growth_rate = 0.3
mixing_rate = 0.3


def total(terms):
    result = terms[0]
    for term in terms[1:]:
        result = result + term
    return result


def field_depths(margin, windows):
    depths = [margin] * STATE
    for copies in (2, 2):
        for window in range(windows):
            depths += [margin - 2 * SUB * window] * copies
    return depths


def message_groups(fields, depths):
    groups, held = [], []
    for field in fields:
        held.append(field)
        if sum(depths[f] for f in held) % GROUP == 0:
            groups.append(held)
            held = []
    return groups + ([held] if held else [])


def even(axis):
    return lax.axis_index(axis) % 2 == 0


def pack_rows(message_ref, row, groups, depths, value_of, northward, rows):
    for group in groups:
        parts = []
        for field in group:
            start = jnp.where(northward, rows - depths[field], 0)
            parts.append(value_of(field, pl.ds(pl.multiple_of(start, 8), depths[field])))
        value = parts[0] if len(parts) == 1 else jnp.concatenate(parts, axis=0)
        message_ref[row : row + value.shape[0]] = value.astype(jnp.bfloat16)
        row += value.shape[0]
    return row


def local_kernel(
    margin,
    covered_hbm,
    offset_hbm,
    weights_hbm,
    thick_hbm,
    conc_hbm,
    mask_hbm,
    velocity_hbm,
    stress_hbm,
    ocean_hbm,
    wind_hbm,
    thick_out_hbm,
    fields_ref,
    current_ref,
    side_ref,
    lon_x_ref,
    lon_y_ref,
    lat_x_ref,
    lat_y_ref,
    covered,
    offset,
    weights,
    thick,
    conc,
    mask_in,
    velocity,
    stress,
    ocean,
    wind,
    in_sems,
    thick_sems,
    conc_sems,
    out_sems,
):
    cats, rows, cols = thick.shape
    windows = wind.shape[0]
    step = GROUP
    chunks = rows // step

    def rows_of(chunk):
        return pl.ds(chunk * step, step)

    small = [
        pltpu.make_async_copy(source, target, in_sems.at[i])
        for i, (source, target) in enumerate(
            (
                (covered_hbm, covered),
                (mask_hbm, mask_in),
                (velocity_hbm, velocity),
                (stress_hbm, stress),
                (ocean_hbm, ocean),
                (wind_hbm, wind),
                (weights_hbm, weights),
                (offset_hbm, offset),
            )
        )
    ]
    pairs = [
        [
            pltpu.make_async_copy(hbm.at[:, rows_of(c)], vmem.at[:, rows_of(c)], sems.at[c])
            for hbm, vmem, sems in ((thick_hbm, thick, thick_sems), (conc_hbm, conc, conc_sems))
        ]
        for c in range(chunks)
    ]
    writes = [
        pltpu.make_async_copy(thick.at[:, rows_of(c)], thick_out_hbm.at[:, rows_of(c)], out_sems.at[c])
        for c in range(chunks)
    ]
    for copy in small[:2] + [copy for pair in pairs for copy in pair] + small[2:]:
        copy.start()

    blocks = cols // BLK
    first = lax.axis_index("lon") * blocks
    small[0].wait()
    live = [covered[0, first + block] > 0 for block in range(blocks)]
    small[1].wait()
    for c in range(chunks):
        at = slice(c * step, (c + 1) * step)
        for copy in pairs[c]:
            copy.wait()
        for block in range(blocks):
            lanes = slice(block * BLK, (block + 1) * BLK)
            part = [conc[k, at, lanes] for k in range(cats)]
            height = [thick[k, at, lanes] for k in range(cats)]
            mask = mask_in[at, lanes].astype(jnp.float32)
            area = total(part)
            inverse = 1.0 / area
            factor = jnp.exp(-2.0 * (1.0 - area)) * (mask * (1.0 / 3.0))
            half = 0.5 * mask
            volume = total([a * h for a, h in zip(part, height)])
            for window in range(windows):
                mean = volume * inverse
                grown = [h + growth_rate / (0.5 + h) + mixing_rate * (mean - h) for h in height]
                height = [jnp.where(live[block], g, h) for g, h in zip(grown, height)]
                volume = total([a * h for a, h in zip(part, height)])
                fields_ref[STATE + 2 * window, at, lanes] = volume * factor
                fields_ref[STATE + 2 * window + 1, at, lanes] = half / (volume + 1.0)
            for k in range(cats):
                thick[k, at, lanes] = height[k]
        writes[c].start()

    small[2].wait()
    small[3].wait()
    for row in range(0, rows, step):
        at = slice(row, row + step)
        mask = mask_in[at].astype(jnp.float32)
        fields_ref[0, at] = velocity[0, at]
        fields_ref[1, at] = velocity[1, at]
        fields_ref[2, at] = (stress[0, at] + stress[1, at]) * mask
        fields_ref[3, at] = (stress[0, at] - stress[1, at]) * mask
        fields_ref[4, at] = (stress[2, at] + stress[2, at]) * mask

    count = fields_ref.shape[0]
    per = LANES // margin
    slot_of_lane = lax.broadcasted_iota(jnp.int32, (rows, LANES), 1) // margin
    eastward = even("lon")
    for group in range(lon_x_ref.shape[1] // LANES):
        east = jnp.zeros((rows, LANES), jnp.float32)
        west = jnp.zeros((rows, LANES), jnp.float32)
        for slot in range(min(per, count - group * per)):
            field = group * per + slot
            east, west = add_slot(
                east, west, fields_ref.at[field], slot_of_lane == slot, slot * margin, margin
            )
        store_sides(lon_x_ref, lon_y_ref, group, east, west, eastward)
    depths = field_depths(margin, windows)
    groups = message_groups(range(count), depths)
    northward = even("lat")

    def value_of(field, at):
        return fields_ref[field, at, :]

    pack_rows(lat_x_ref, 0, groups, depths, value_of, northward, rows)
    pack_rows(lat_y_ref, 0, groups, depths, value_of, jnp.logical_not(northward), rows)

    for copy in small[4:]:
        copy.wait()
    own_weights = weights[:, :rows]
    for w in range(windows):
        for k in range(2):
            current_ref[w, k] = wind[w, k].astype(jnp.float32) + jnp.dot(
                own_weights, ocean[w, k], preferred_element_type=jnp.float32
            )
    square = (rows, rows)
    diagonal = lax.broadcasted_iota(jnp.int32, square, 0) == lax.broadcasted_iota(
        jnp.int32, square, 1
    )
    up = offset[...] > 0
    for number, north in enumerate((northward, jnp.logical_not(northward))):
        wanted = jnp.where(north, up.astype(jnp.int32), 1 - up.astype(jnp.int32)) > 0
        pick = jnp.where(diagonal & wanted, 1.0, 0.0).astype(jnp.bfloat16)
        side_ref[:, number * rows : (number + 1) * rows] = jnp.dot(
            pick, weights[:, rows:], preferred_element_type=jnp.float32
        ).astype(jnp.bfloat16)

    for copy in writes:
        copy.wait()


def add_slot(east, west, field_ref, here, shift, margin):
    cols = field_ref.shape[1]
    last = pltpu.roll(field_ref[:, cols - LANES :], (shift + margin) % LANES, 1)
    leading = field_ref[:, :LANES]
    if shift:
        leading = pltpu.roll(leading, shift, 1)
    return jnp.where(here, last, east), jnp.where(here, leading, west)


def store_sides(x_ref, y_ref, group, east, west, eastward):
    lanes = slice(group * LANES, (group + 1) * LANES)
    x_ref[:, lanes] = jnp.where(eastward, east, west).astype(jnp.bfloat16)
    y_ref[:, lanes] = jnp.where(eastward, west, east).astype(jnp.bfloat16)


def side_kernel(side_ref, tile_ref, current_ref, sum_ref):
    windows, parts, rows, _ = current_ref.shape
    weights = side_ref[:, :rows]
    for w in range(windows):
        for k in range(parts):
            sum_ref[w, k] = current_ref[w, k] + jnp.dot(
                weights, tile_ref[w, k], preferred_element_type=jnp.float32
            )


def force_kernel(
    margin,
    early,
    side_ref,
    tile_ref,
    current_ref,
    fields_ref,
    lon_x_in,
    lon_y_in,
    early_y_in,
    force_ref,
    lon_x_ref,
    lon_y_ref,
    lat_x_ref,
    lat_y_ref,
    early_y_ref,
):
    windows, _, rows, cols = current_ref.shape
    weights = side_ref[:, rows:]
    for w in range(windows):
        b = fields_ref[STATE + 2 * w + 1]
        for k in range(2):
            current = jnp.dot(weights, tile_ref[w, k], preferred_element_type=jnp.float32)
            force_ref[2 * w + k] = b * (current_ref[w, k] + current)

    per = LANES // margin
    count = early + force_ref.shape[0]
    slot_of_lane = lax.broadcasted_iota(jnp.int32, (rows, LANES), 1) // margin
    eastward = even("lon")
    for group in range(lon_x_ref.shape[1] // LANES):
        lanes = slice(group * LANES, (group + 1) * LANES)
        x = lon_x_in[:, lanes].astype(jnp.float32)
        y = lon_y_in[:, lanes].astype(jnp.float32)
        east, west = jnp.where(eastward, x, y), jnp.where(eastward, y, x)
        for field in range(max(early, group * per), min(count, (group + 1) * per)):
            slot = field - group * per
            east, west = add_slot(
                east, west, force_ref.at[field - early], slot_of_lane == slot, slot * margin, margin
            )
        store_sides(lon_x_ref, lon_y_ref, group, east, west, eastward)

    depths = field_depths(margin, windows)
    groups = message_groups(range(early, count), depths)
    northward = even("lat")

    def value_of(field, at):
        return force_ref[field - early, at, :]

    for ref, north in ((lat_x_ref, northward), (lat_y_ref, jnp.logical_not(northward))):
        pack_rows(ref, 0, groups, depths, value_of, north, rows)
    early_y_ref[...] = early_y_in[...]


def corner_kernel(
    margin, rows, lat_x_in, lat_y_in, lon_x_ref, lon_y_ref, early_x_ref, lat_x_ref, lat_y_ref
):
    for old_ref, ref, north in (
        (lat_x_in, lat_x_ref, even("lat")),
        (lat_y_in, lat_y_ref, jnp.logical_not(even("lat"))),
    ):
        row, cols = old_ref.shape
        ref[:row] = old_ref[...]
        start = pl.multiple_of(jnp.where(north, rows - margin, 0), GROUP)
        for lon_ref in (lon_x_ref, lon_y_ref):
            packed = lon_ref.shape[1]
            ref[row : row + margin, :packed] = lon_ref[pl.ds(start, margin), :]
            if packed < cols:
                ref[row : row + margin, packed:] = jnp.zeros((margin, cols - packed), ref.dtype)
            row += margin


def place(refs, early, field, tile, row, value):
    velocity, stress, strength, keep, push, force = refs
    at = pl.ds(row, value.shape[0])
    if field < 2:
        velocity[0, field, tile, at, :] = value
    elif field < STATE:
        stress[0, field - 2, tile, at, :] = value
    elif field >= early:
        window, kind = divmod(field - early, 2)
        force[window, kind, tile, at, :] = value
    else:
        window, kind = divmod(field - STATE, 2)
        if kind == 0:
            strength[window, tile, at, :] = value
        else:
            push[window, tile, at, :] = value * 0.25
            keep[window, tile, at, :] = jnp.where(value > 0.0, 1.0 - value, 0.0)


def place_sides(refs, early, count, margin, x, y, row):
    last = refs[0].shape[2] - 1
    per = LANES // margin
    wide = lax.broadcasted_iota(jnp.int32, (x.shape[0], LANES), 1)
    from_x_is_east = even("lon")
    for group in range(x.shape[1] // LANES):
        lanes = slice(group * LANES, (group + 1) * LANES)
        x_now, y_now = x[:, lanes], y[:, lanes]
        east = jnp.where(from_x_is_east, x_now, y_now)
        west = jnp.where(from_x_is_east, y_now, x_now)
        for slot in range(min(per, count - group * per)):
            shift = slot * margin
            back = (LANES - margin - shift) % LANES
            e = pltpu.roll(east, LANES - shift, 1) if shift else east
            w = pltpu.roll(west, back, 1) if back else west
            value = jnp.where(wide < margin, e, jnp.where(wide >= LANES - margin, w, 0.0))
            place(refs, early, group * per + slot, last, row, value)


def across(values):
    tiles = len(values)
    lane = lax.broadcasted_iota(jnp.int32, values[0].shape, 1)
    ahead = [pltpu.roll(x, LANES - 1, 1) for x in values]
    behind = [pltpu.roll(x, 1, 1) for x in values]
    return [
        jnp.where(lane == LANES - 1, ahead[(j + 1) % tiles], ahead[j])
        - jnp.where(lane == 0, behind[j - 1], behind[j])
        for j in range(tiles)
    ]


def stress_rows(refs, step, window, row, height=GROUP):
    velocity, stress, strength, _, _, _ = refs
    every = range(velocity.shape[2])
    at, north, south = (pl.ds(row + shift, height) for shift in (0, 1, -1))
    u_x = across([velocity[step, 0, j, at, :] for j in every])
    v_x = across([velocity[step, 1, j, at, :] for j in every])
    for j in every:
        u_y = velocity[step, 0, j, north, :] - velocity[step, 0, j, south, :]
        v_y = velocity[step, 1, j, north, :] - velocity[step, 1, j, south, :]
        shear = u_y + v_x[j]
        spread = u_x[j] + v_y
        tension = u_x[j] - v_y
        tension4 = tension * 0.25
        shear4 = shear * 0.25
        squares = spread * spread + tension * tension4 + (shear * shear4 + 1.0)
        k = strength[window, j, at, :]
        kr = k * lax.rsqrt(squares)
        old = [stress[step, i, j, at, :] * (2.0 / 3.0) for i in range(3)]
        stress[step + 1, 0, j, at, :] = old[0] + (kr * (spread + tension4) - k)
        stress[step + 1, 1, j, at, :] = old[1] + (kr * (spread - tension4) - k)
        stress[step + 1, 2, j, at, :] = old[2] + kr * shear4


def velocity_rows(refs, step, window, row, height=GROUP):
    velocity, stress, _, keep, push, force = refs
    every = range(velocity.shape[2])
    at, north, south = (pl.ds(row + shift, height) for shift in (0, 1, -1))
    now = step + 1
    p_x = across([stress[now, 0, j, at, :] for j in every])
    t_x = across([stress[now, 2, j, at, :] for j in every])
    for j in every:
        q_y = stress[now, 1, j, north, :] - stress[now, 1, j, south, :]
        t_y = stress[now, 2, j, north, :] - stress[now, 2, j, south, :]
        a = keep[window, j, at, :]
        b = push[window, j, at, :]
        velocity[now, 0, j, at, :] = (
            a * velocity[step, 0, j, at, :] + b * (p_x[j] + t_y) + force[window, 0, j, at, :]
        )
        velocity[now, 1, j, at, :] = (
            a * velocity[step, 1, j, at, :] + b * (t_x[j] + q_y) + force[window, 1, j, at, :]
        )


def write_rows(refs, out_hbm, stage, sem, margin, begin, height, which):
    values = refs[which]
    last = values.shape[0] - 1
    first = 2 * which
    for tile in range(stage.shape[2] // LANES):
        lanes = slice(tile * LANES, (tile + 1) * LANES)
        for row in range(0, height, 8):
            to = slice(row, row + 8)
            at = slice(margin + begin + row, margin + begin + row + 8)
            now = [values[last, i, tile, at, :] for i in range(values.shape[1])]
            if which:
                now = [(now[0] + now[1]) * 0.5, (now[0] - now[1]) * 0.5, now[2] * 0.5]
            for i, value in enumerate(now):
                stage[first + i, to, lanes] = value
    copy = pltpu.make_async_copy(
        stage.at[first : first + values.shape[1]],
        out_hbm[which].at[:, pl.ds(begin, height)],
        sem.at[which],
    )
    copy.start()
    return [copy]


def place_rows(refs, early, fields, margin, rows, lat_count, x_ref, y_ref):
    depths = field_depths(margin, refs[2].shape[0])
    me = lax.axis_index("lat")
    sides = []
    for ref, north in ((x_ref, even("lat")), (y_ref, jnp.logical_not(even("lat")))):
        exists = jnp.where(north, me < lat_count - 1, me > 0)

        def read(at, ref=ref, exists=exists):
            return jnp.where(exists, ref[at].astype(jnp.float32), 0.0)

        row = 0
        for group in message_groups(fields, depths):
            height = sum(depths[f] for f in group)
            value = read(slice(row, row + height))
            begin = 0
            for field in group:
                depth = depths[field]
                to = pl.multiple_of(jnp.where(north, margin + rows, margin - depth), 8)
                for tile in range(refs[0].shape[2] - 1):
                    lanes = slice(tile * LANES, (tile + 1) * LANES)
                    place(refs, early, field, tile, to, value[begin : begin + depth, lanes])
                begin += depth
            row += height
        sides.append((north, read, row))
    return sides


def interior_kernel(
    margin, lat_count, fields_ref, force_ref, lon_x_ref, lon_y_ref, early_x_ref, early_y_ref, *refs
):
    early, rows, cols = fields_ref.shape
    count = early + force_ref.shape[0]
    windows = refs[2].shape[0]
    for field in range(count):
        for tile in range(cols // LANES):
            lanes = slice(tile * LANES, (tile + 1) * LANES)
            own = fields_ref[field, :, lanes] if field < early else force_ref[field - early, :, lanes]
            place(refs, early, field, tile, margin, own)
    lon_x, lon_y = lon_x_ref[...].astype(jnp.float32), lon_y_ref[...].astype(jnp.float32)
    place_sides(refs, early, count, margin, lon_x, lon_y, margin)
    place_rows(refs, early, range(early), margin, rows, lat_count, early_x_ref, early_y_ref)
    for window in range(windows):
        lost = 2 * SUB * window
        row_list = range(margin + lost, margin + rows - lost, GROUP)

        def subcycle(number, carry):
            step = window * SUB + number
            for row in row_list:
                stress_rows(refs, step, window, row)
            for row in row_list:
                velocity_rows(refs, step, window, row)
            return carry

        lax.fori_loop(0, SUB, subcycle, 0)


def rim_kernel(margin, early, count, lat_count, *args):
    lat_x_ref, lat_y_ref = args[:2]
    refs = args[2:8]
    out_hbm = args[8:10]
    stages, sems = args[16:19], args[19]
    windows = refs[2].shape[0]
    _, rows, cols = out_hbm[0].shape
    inner = rows - 2 * margin
    copies = []
    for which in range(2):
        copies += write_rows(refs, out_hbm, stages[2], sems.at[2], margin, margin, inner, which)
    bottom = margin + rows
    packed = -(-count // (LANES // margin)) * LANES
    late = range(early, count)
    for north, read, row in place_rows(
        refs, early, late, margin, rows, lat_count, lat_x_ref, lat_y_ref
    ):
        to = pl.multiple_of(jnp.where(north, bottom, 0), 8)
        east, west = (read(slice(at, at + margin))[:, :packed] for at in (row, row + margin))
        place_sides(refs, early, count, margin, east, west, to)

    def half_step(step, half):
        done = 2 * step + 1 + half
        rows_now = velocity_rows if half else stress_rows
        for first in range(0, margin, GROUP):
            rows_now(refs, step, step // SUB, done + first)
            rows_now(refs, step, step // SUB, bottom - done + first)

    last = SUB * windows - 1
    for step in range(last):
        half_step(step, 0)
        half_step(step, 1)
    half_step(last, 0)
    ends = list(enumerate((0, rows - margin)))
    for number, begin in ends:
        copies += write_rows(refs, out_hbm, stages[number], sems.at[number], margin, begin, margin, 1)
    half_step(last, 1)
    for number, begin in ends:
        copies += write_rows(refs, out_hbm, stages[number], sems.at[number], margin, begin, margin, 0)
    for copy in copies:
        copy.wait()


def params():
    return pltpu.CompilerParams(vmem_limit_bytes=VMEM_LIMIT)


def lon_swaps(first):
    n = lax.axis_size("lon")
    if n % 2:
        raise ValueError("odd ring")
    pairs = [(i, (i + 1) % n) for i in range(first, n, 2)]
    return pairs + [(j, i) for i, j in pairs]


def lat_swaps(first):
    m, n = lax.axis_size("lat"), lax.axis_size("lon")
    partner = {}
    for i in range(m):
        north = i + 1 if (i - first) % 2 == 0 else i - 1
        for k in range(n):
            to = (north, k) if 0 <= north < m else (i, k ^ 1)
            partner[k * m + i] = to[1] * m + to[0]
    return list(partner.items())


def lon_exchange(x, y):
    return lax.ppermute(x, "lon", lon_swaps(0)), lax.ppermute(y, "lon", lon_swaps(1))


def lat_exchange(x, first):
    return lax.ppermute(x, ("lon", "lat"), lat_swaps(first))


def shape(dims, dtype=jnp.float32):
    return jax.ShapeDtypeStruct(dims, dtype)


def local(
    velocity,
    stress,
    thickness,
    concentration,
    land_mask,
    covered,
    ocean_current,
    wind_stress,
    regrid_weights,
    tile_offset,
):
    _, rows, cols = velocity.shape
    windows = wind_stress.shape[0]
    margin = 2 * SUB * windows
    early = STATE + 2 * windows
    count = early + 2 * windows
    tiles = cols // LANES + 1
    packed = -(-count // (LANES // margin)) * LANES
    depths = field_depths(margin, windows)
    early_rows = sum(depths[:early])
    late_rows = sum(depths[early:])
    bf16 = jnp.bfloat16

    tile_x, tile_y = lat_exchange(ocean_current, 0), lat_exchange(ocean_current, 1)

    whole = pl.BlockSpec(memory_space=pltpu.VMEM)
    anywhere = pl.BlockSpec(memory_space=pl.ANY)
    chunks = rows // GROUP
    thick_out, fields, current, side, lon_x, lon_y, lat_x, lat_y = pl.pallas_call(
        functools.partial(local_kernel, margin),
        out_shape=(
            shape(thickness.shape),
            shape((early, rows, cols)),
            shape(wind_stress.shape),
            shape((rows, 2 * rows), bf16),
            shape((rows, packed), bf16),
            shape((rows, packed), bf16),
            shape((early_rows, cols), bf16),
            shape((early_rows, cols), bf16),
        ),
        in_specs=[anywhere] * 10,
        out_specs=(anywhere,) + (whole,) * 7,
        scratch_shapes=[
            pltpu.SMEM(covered.shape, jnp.int32),
            pltpu.VMEM((1, rows), jnp.int32),
            pltpu.VMEM(regrid_weights.shape, bf16),
            pltpu.VMEM(thickness.shape, jnp.float32),
            pltpu.VMEM(thickness.shape, jnp.float32),
            pltpu.VMEM(land_mask.shape, jnp.int32),
            pltpu.VMEM(velocity.shape, jnp.float32),
            pltpu.VMEM(stress.shape, jnp.float32),
            pltpu.VMEM(ocean_current.shape, bf16),
            pltpu.VMEM(wind_stress.shape, bf16),
            pltpu.SemaphoreType.DMA((8,)),
            pltpu.SemaphoreType.DMA((chunks,)),
            pltpu.SemaphoreType.DMA((chunks,)),
            pltpu.SemaphoreType.DMA((chunks,)),
        ],
        compiler_params=params(),
        cost_estimate=pl.CostEstimate(
            flops=100 * thickness.size, bytes_accessed=12 * thickness.size, transcendentals=0
        ),
        name="local",
    )(
        *(
            pltpu.with_memory_space_constraint(x, pltpu.HBM)
            for x in (
                covered,
                tile_offset.reshape(1, rows),
                regrid_weights,
                thickness,
                concentration,
                land_mask,
                velocity,
                stress,
                ocean_current,
                wind_stress,
            )
        )
    )

    early_x = lat_exchange(lat_x, 0)
    current = pl.pallas_call(
        side_kernel,
        out_shape=shape(wind_stress.shape),
        in_specs=[whole] * 3,
        out_specs=whole,
        compiler_params=params(),
        cost_estimate=pl.CostEstimate(flops=1, bytes_accessed=1, transcendentals=0),
        name="side",
    )(side, tile_x, current)
    force, lon_x, lon_y, late_x, late_y, lat_y = pl.pallas_call(
        functools.partial(force_kernel, margin, early),
        out_shape=(
            shape((2 * windows, rows, cols)),
            shape((rows, packed), bf16),
            shape((rows, packed), bf16),
            shape((late_rows, cols), bf16),
            shape((late_rows, cols), bf16),
            shape((early_rows, cols), bf16),
        ),
        in_specs=[whole] * 7,
        out_specs=(whole,) * 6,
        compiler_params=params(),
        cost_estimate=pl.CostEstimate(flops=1, bytes_accessed=1, transcendentals=0),
        name="force",
    )(side, tile_y, current, fields, lon_x, lon_y, lat_y)

    lon_x, lon_y = lon_exchange(lon_x, lon_y)
    early_y = lat_exchange(lat_y, 1)
    message = shape((late_rows + 2 * margin, cols), bf16)
    late_x, late_y = pl.pallas_call(
        functools.partial(corner_kernel, margin, rows),
        out_shape=(message, message),
        in_specs=[whole] * 5,
        out_specs=(whole,) * 2,
        compiler_params=params(),
        cost_estimate=pl.CostEstimate(flops=1, bytes_accessed=1, transcendentals=0),
        name="corner",
    )(late_x, late_y, lon_x, lon_y, early_x)
    late_x, late_y = lat_exchange(late_x, 0), lat_exchange(late_y, 1)

    steps = SUB * windows

    def widened(*lead):
        return shape((*lead, tiles, rows + 2 * margin, LANES))

    domain = (
        widened(steps + 1, 2),
        widened(steps + 1, 3),
        widened(windows),
        widened(windows),
        widened(windows),
        widened(windows, 2),
    )
    outs = (shape(velocity.shape), shape(stress.shape))
    refs = pl.pallas_call(
        functools.partial(interior_kernel, margin, lax.axis_size("lat")),
        out_shape=domain,
        in_specs=[whole] * 6,
        out_specs=(whole,) * 6,
        compiler_params=params(),
        cost_estimate=pl.CostEstimate(
            flops=60 * steps * rows * cols, bytes_accessed=2**22, transcendentals=0
        ),
        name="interior",
    )(fields, force, lon_x, lon_y, early_x, early_y)

    velocity_out, stress_out = pl.pallas_call(
        functools.partial(rim_kernel, margin, early, count, lax.axis_size("lat")),
        out_shape=(shape(velocity.shape), shape(stress.shape)) + domain,
        in_specs=[whole] * 8,
        out_specs=(anywhere,) * 2 + (whole,) * 6,
        input_output_aliases={2 + i: 2 + i for i in range(6)},
        scratch_shapes=[
            pltpu.VMEM((STATE, margin, cols), jnp.float32),
            pltpu.VMEM((STATE, margin, cols), jnp.float32),
            pltpu.VMEM((STATE, rows - 2 * margin, cols), jnp.float32),
            pltpu.SemaphoreType.DMA((3, 2)),
        ],
        compiler_params=params(),
        name="rim",
    )(late_x, late_y, *refs)[:2]
    return (velocity_out, stress_out, thick_out)


def solution(mesh):
    return jax.shard_map(
        local,
        mesh=mesh,
        in_specs=(
            P(None, "lat", "lon"),
            P(None, "lat", "lon"),
            P(None, "lat", "lon"),
            P(None, "lat", "lon"),
            P("lat", "lon"),
            P("lat", None),
            P(None, None, "lat", "lon"),
            P(None, None, "lat", "lon"),
            P("lat", None),
            P("lat"),
        ),
        out_specs=(P(None, "lat", "lon"), P(None, "lat", "lon"), P(None, "lat", "lon")),
        check_vma=False,
    )
```

```python
import functools

import jax
import jax.numpy as jnp
from jax import lax
from jax.experimental import pallas as pl
from jax.experimental.pallas import tpu as pltpu
from jax.sharding import PartitionSpec as P

BLK = 128
SUB = 4
LANES = 128
GROUP = 16
STATE = 5
VMEM_LIMIT = 16 * 1024 * 1024

growth_rate = 0.3
mixing_rate = 0.3


def total(terms):
    result = terms[0]
    for term in terms[1:]:
        result = result + term
    return result


def field_depths(margin, windows):
    depths = [margin] * STATE
    for copies in (2, 2):
        for window in range(windows):
            depths += [margin - 2 * SUB * window] * copies
    return depths


def message_groups(fields, depths):
    groups, held = [], []
    for field in fields:
        held.append(field)
        if sum(depths[f] for f in held) % GROUP == 0:
            groups.append(held)
            held = []
    return groups + ([held] if held else [])


def even(axis):
    return lax.axis_index(axis) % 2 == 0


def pack_rows(message_ref, row, groups, depths, value_of, northward, rows):
    for group in groups:
        parts = []
        for field in group:
            start = jnp.where(northward, rows - depths[field], 0)
            parts.append(value_of(field, pl.ds(pl.multiple_of(start, 8), depths[field])))
        value = parts[0] if len(parts) == 1 else jnp.concatenate(parts, axis=0)
        message_ref[row : row + value.shape[0]] = value.astype(jnp.bfloat16)
        row += value.shape[0]
    return row


def local_kernel(
    margin,
    covered_hbm,
    offset_hbm,
    weights_hbm,
    thick_hbm,
    conc_hbm,
    mask_hbm,
    velocity_hbm,
    stress_hbm,
    ocean_hbm,
    wind_hbm,
    thick_out_hbm,
    fields_ref,
    current_ref,
    side_ref,
    lon_x_ref,
    lon_y_ref,
    lat_x_ref,
    lat_y_ref,
    covered,
    offset,
    weights,
    thick,
    conc,
    mask_in,
    velocity,
    stress,
    ocean,
    wind,
    in_sems,
    thick_sems,
    conc_sems,
    out_sems,
):
    cats, rows, cols = thick.shape
    windows = wind.shape[0]
    step = GROUP
    chunks = rows // step

    def rows_of(chunk):
        return pl.ds(chunk * step, step)

    small = [
        pltpu.make_async_copy(source, target, in_sems.at[i])
        for i, (source, target) in enumerate(
            (
                (covered_hbm, covered),
                (mask_hbm, mask_in),
                (velocity_hbm, velocity),
                (stress_hbm, stress),
                (ocean_hbm, ocean),
                (wind_hbm, wind),
                (weights_hbm, weights),
                (offset_hbm, offset),
            )
        )
    ]
    pairs = [
        [
            pltpu.make_async_copy(hbm.at[:, rows_of(c)], vmem.at[:, rows_of(c)], sems.at[c])
            for hbm, vmem, sems in ((thick_hbm, thick, thick_sems), (conc_hbm, conc, conc_sems))
        ]
        for c in range(chunks)
    ]
    writes = [
        pltpu.make_async_copy(thick.at[:, rows_of(c)], thick_out_hbm.at[:, rows_of(c)], out_sems.at[c])
        for c in range(chunks)
    ]
    for copy in small[:2] + [copy for pair in pairs for copy in pair] + small[2:]:
        copy.start()

    blocks = cols // BLK
    first = lax.axis_index("lon") * blocks
    small[0].wait()
    live = [covered[0, first + block] > 0 for block in range(blocks)]
    small[1].wait()
    for c in range(chunks):
        at = slice(c * step, (c + 1) * step)
        for copy in pairs[c]:
            copy.wait()
        for block in range(blocks):
            lanes = slice(block * BLK, (block + 1) * BLK)
            part = [conc[k, at, lanes] for k in range(cats)]
            height = [thick[k, at, lanes] for k in range(cats)]
            mask = mask_in[at, lanes].astype(jnp.float32)
            area = total(part)
            inverse = 1.0 / area
            factor = jnp.exp(-2.0 * (1.0 - area)) * (mask * (1.0 / 3.0))
            half = 0.5 * mask
            volume = total([a * h for a, h in zip(part, height)])
            for window in range(windows):
                mean = volume * inverse
                grown = [h + growth_rate / (0.5 + h) + mixing_rate * (mean - h) for h in height]
                height = [jnp.where(live[block], g, h) for g, h in zip(grown, height)]
                volume = total([a * h for a, h in zip(part, height)])
                fields_ref[STATE + 2 * window, at, lanes] = volume * factor
                fields_ref[STATE + 2 * window + 1, at, lanes] = half / (volume + 1.0)
            for k in range(cats):
                thick[k, at, lanes] = height[k]
        writes[c].start()

    small[2].wait()
    small[3].wait()
    for row in range(0, rows, step):
        at = slice(row, row + step)
        mask = mask_in[at].astype(jnp.float32)
        fields_ref[0, at] = velocity[0, at]
        fields_ref[1, at] = velocity[1, at]
        fields_ref[2, at] = (stress[0, at] + stress[1, at]) * mask
        fields_ref[3, at] = (stress[0, at] - stress[1, at]) * mask
        fields_ref[4, at] = (stress[2, at] + stress[2, at]) * mask

    count = fields_ref.shape[0]
    per = LANES // margin
    slot_of_lane = lax.broadcasted_iota(jnp.int32, (rows, LANES), 1) // margin
    eastward = even("lon")
    for group in range(lon_x_ref.shape[1] // LANES):
        east = jnp.zeros((rows, LANES), jnp.float32)
        west = jnp.zeros((rows, LANES), jnp.float32)
        for slot in range(min(per, count - group * per)):
            field = group * per + slot
            east, west = add_slot(
                east, west, fields_ref.at[field], slot_of_lane == slot, slot * margin, margin
            )
        store_sides(lon_x_ref, lon_y_ref, group, east, west, eastward)
    depths = field_depths(margin, windows)
    groups = message_groups(range(count), depths)
    northward = even("lat")

    def value_of(field, at):
        return fields_ref[field, at, :]

    pack_rows(lat_x_ref, 0, groups, depths, value_of, northward, rows)
    pack_rows(lat_y_ref, 0, groups, depths, value_of, jnp.logical_not(northward), rows)

    for copy in small[4:]:
        copy.wait()
    own_weights = weights[:, :rows]
    for w in range(windows):
        for k in range(2):
            current_ref[w, k] = wind[w, k].astype(jnp.float32) + jnp.dot(
                own_weights, ocean[w, k], preferred_element_type=jnp.float32
            )
    square = (rows, rows)
    diagonal = lax.broadcasted_iota(jnp.int32, square, 0) == lax.broadcasted_iota(
        jnp.int32, square, 1
    )
    up = offset[...] > 0
    for number, north in enumerate((northward, jnp.logical_not(northward))):
        wanted = jnp.where(north, up.astype(jnp.int32), 1 - up.astype(jnp.int32)) > 0
        pick = jnp.where(diagonal & wanted, 1.0, 0.0).astype(jnp.bfloat16)
        side_ref[:, number * rows : (number + 1) * rows] = jnp.dot(
            pick, weights[:, rows:], preferred_element_type=jnp.float32
        ).astype(jnp.bfloat16)

    for copy in writes:
        copy.wait()


def add_slot(east, west, field_ref, here, shift, margin):
    cols = field_ref.shape[1]
    last = pltpu.roll(field_ref[:, cols - LANES :], (shift + margin) % LANES, 1)
    leading = field_ref[:, :LANES]
    if shift:
        leading = pltpu.roll(leading, shift, 1)
    return jnp.where(here, last, east), jnp.where(here, leading, west)


def store_sides(x_ref, y_ref, group, east, west, eastward):
    lanes = slice(group * LANES, (group + 1) * LANES)
    x_ref[:, lanes] = jnp.where(eastward, east, west).astype(jnp.bfloat16)
    y_ref[:, lanes] = jnp.where(eastward, west, east).astype(jnp.bfloat16)


def side_kernel(side_ref, tile_ref, current_ref, sum_ref):
    windows, parts, rows, _ = current_ref.shape
    weights = side_ref[:, :rows]
    for w in range(windows):
        for k in range(parts):
            sum_ref[w, k] = current_ref[w, k] + jnp.dot(
                weights, tile_ref[w, k], preferred_element_type=jnp.float32
            )


def force_kernel(
    margin,
    early,
    side_ref,
    tile_ref,
    current_ref,
    fields_ref,
    lon_x_in,
    lon_y_in,
    early_x_in,
    force_ref,
    lon_x_ref,
    lon_y_ref,
    lat_x_ref,
    lat_y_ref,
    early_x_ref,
):
    windows, _, rows, cols = current_ref.shape
    weights = side_ref[:, rows:]
    for w in range(windows):
        b = fields_ref[STATE + 2 * w + 1]
        for k in range(2):
            current = jnp.dot(weights, tile_ref[w, k], preferred_element_type=jnp.float32)
            force_ref[2 * w + k] = b * (current_ref[w, k] + current)

    per = LANES // margin
    count = early + force_ref.shape[0]
    slot_of_lane = lax.broadcasted_iota(jnp.int32, (rows, LANES), 1) // margin
    eastward = even("lon")
    for group in range(lon_x_ref.shape[1] // LANES):
        lanes = slice(group * LANES, (group + 1) * LANES)
        x = lon_x_in[:, lanes].astype(jnp.float32)
        y = lon_y_in[:, lanes].astype(jnp.float32)
        east, west = jnp.where(eastward, x, y), jnp.where(eastward, y, x)
        for field in range(max(early, group * per), min(count, (group + 1) * per)):
            slot = field - group * per
            east, west = add_slot(
                east, west, force_ref.at[field - early], slot_of_lane == slot, slot * margin, margin
            )
        store_sides(lon_x_ref, lon_y_ref, group, east, west, eastward)

    depths = field_depths(margin, windows)
    groups = message_groups(range(early, count), depths)
    northward = even("lat")

    def value_of(field, at):
        return force_ref[field - early, at, :]

    for ref, north in ((lat_x_ref, northward), (lat_y_ref, jnp.logical_not(northward))):
        pack_rows(ref, 0, groups, depths, value_of, north, rows)
    early_x_ref[...] = early_x_in[...]


def corner_kernel(
    margin, rows, lat_x_in, lat_y_in, lon_x_ref, lon_y_ref, early_y_ref, lat_x_ref, lat_y_ref
):
    for old_ref, ref, north in (
        (lat_x_in, lat_x_ref, even("lat")),
        (lat_y_in, lat_y_ref, jnp.logical_not(even("lat"))),
    ):
        row, cols = old_ref.shape
        ref[:row] = old_ref[...]
        start = pl.multiple_of(jnp.where(north, rows - margin, 0), GROUP)
        for lon_ref in (lon_x_ref, lon_y_ref):
            packed = lon_ref.shape[1]
            ref[row : row + margin, :packed] = lon_ref[pl.ds(start, margin), :]
            if packed < cols:
                ref[row : row + margin, packed:] = jnp.zeros((margin, cols - packed), ref.dtype)
            row += margin


def place(refs, early, field, tile, row, value):
    velocity, stress, strength, keep, push, force = refs
    at = pl.ds(row, value.shape[0])
    if field < 2:
        velocity[0, field, tile, at, :] = value
    elif field < STATE:
        stress[0, field - 2, tile, at, :] = value
    elif field >= early:
        window, kind = divmod(field - early, 2)
        force[window, kind, tile, at, :] = value
    else:
        window, kind = divmod(field - STATE, 2)
        if kind == 0:
            strength[window, tile, at, :] = value
        else:
            push[window, tile, at, :] = value * 0.25
            keep[window, tile, at, :] = jnp.where(value > 0.0, 1.0 - value, 0.0)


def place_sides(refs, early, count, margin, x, y, row):
    last = refs[0].shape[2] - 1
    per = LANES // margin
    wide = lax.broadcasted_iota(jnp.int32, (x.shape[0], LANES), 1)
    from_x_is_east = even("lon")
    for group in range(x.shape[1] // LANES):
        lanes = slice(group * LANES, (group + 1) * LANES)
        x_now, y_now = x[:, lanes], y[:, lanes]
        east = jnp.where(from_x_is_east, x_now, y_now)
        west = jnp.where(from_x_is_east, y_now, x_now)
        for slot in range(min(per, count - group * per)):
            shift = slot * margin
            back = (LANES - margin - shift) % LANES
            e = pltpu.roll(east, LANES - shift, 1) if shift else east
            w = pltpu.roll(west, back, 1) if back else west
            value = jnp.where(wide < margin, e, jnp.where(wide >= LANES - margin, w, 0.0))
            place(refs, early, group * per + slot, last, row, value)


def across(values):
    tiles = len(values)
    lane = lax.broadcasted_iota(jnp.int32, values[0].shape, 1)
    ahead = [pltpu.roll(x, LANES - 1, 1) for x in values]
    behind = [pltpu.roll(x, 1, 1) for x in values]
    return [
        jnp.where(lane == LANES - 1, ahead[(j + 1) % tiles], ahead[j])
        - jnp.where(lane == 0, behind[j - 1], behind[j])
        for j in range(tiles)
    ]


def stress_rows(refs, step, window, row, height=GROUP):
    velocity, stress, strength, _, _, _ = refs
    every = range(velocity.shape[2])
    at, north, south = (pl.ds(row + shift, height) for shift in (0, 1, -1))
    u_x = across([velocity[step, 0, j, at, :] for j in every])
    v_x = across([velocity[step, 1, j, at, :] for j in every])
    for j in every:
        u_y = velocity[step, 0, j, north, :] - velocity[step, 0, j, south, :]
        v_y = velocity[step, 1, j, north, :] - velocity[step, 1, j, south, :]
        shear = u_y + v_x[j]
        spread = u_x[j] + v_y
        tension = u_x[j] - v_y
        tension4 = tension * 0.25
        shear4 = shear * 0.25
        squares = spread * spread + tension * tension4 + (shear * shear4 + 1.0)
        k = strength[window, j, at, :]
        kr = k * lax.rsqrt(squares)
        old = [stress[step, i, j, at, :] * (2.0 / 3.0) for i in range(3)]
        stress[step + 1, 0, j, at, :] = old[0] + (kr * (spread + tension4) - k)
        stress[step + 1, 1, j, at, :] = old[1] + (kr * (spread - tension4) - k)
        stress[step + 1, 2, j, at, :] = old[2] + kr * shear4


def velocity_rows(refs, step, window, row, height=GROUP):
    velocity, stress, _, keep, push, force = refs
    every = range(velocity.shape[2])
    at, north, south = (pl.ds(row + shift, height) for shift in (0, 1, -1))
    now = step + 1
    p_x = across([stress[now, 0, j, at, :] for j in every])
    t_x = across([stress[now, 2, j, at, :] for j in every])
    for j in every:
        q_y = stress[now, 1, j, north, :] - stress[now, 1, j, south, :]
        t_y = stress[now, 2, j, north, :] - stress[now, 2, j, south, :]
        a = keep[window, j, at, :]
        b = push[window, j, at, :]
        velocity[now, 0, j, at, :] = (
            a * velocity[step, 0, j, at, :] + b * (p_x[j] + t_y) + force[window, 0, j, at, :]
        )
        velocity[now, 1, j, at, :] = (
            a * velocity[step, 1, j, at, :] + b * (t_x[j] + q_y) + force[window, 1, j, at, :]
        )


def write_rows(refs, out_hbm, stage, sem, margin, begin, height, which):
    values = refs[which]
    last = values.shape[0] - 1
    first = 2 * which
    for tile in range(stage.shape[2] // LANES):
        lanes = slice(tile * LANES, (tile + 1) * LANES)
        for row in range(0, height, 8):
            to = slice(row, row + 8)
            at = slice(margin + begin + row, margin + begin + row + 8)
            now = [values[last, i, tile, at, :] for i in range(values.shape[1])]
            if which:
                now = [(now[0] + now[1]) * 0.5, (now[0] - now[1]) * 0.5, now[2] * 0.5]
            for i, value in enumerate(now):
                stage[first + i, to, lanes] = value
    copy = pltpu.make_async_copy(
        stage.at[first : first + values.shape[1]],
        out_hbm[which].at[:, pl.ds(begin, height)],
        sem.at[which],
    )
    copy.start()
    return [copy]


def place_rows(refs, early, fields, margin, rows, lat_count, x_ref, y_ref):
    depths = field_depths(margin, refs[2].shape[0])
    me = lax.axis_index("lat")
    sides = []
    for ref, north in ((x_ref, even("lat")), (y_ref, jnp.logical_not(even("lat")))):
        exists = jnp.where(north, me < lat_count - 1, me > 0)

        def read(at, ref=ref, exists=exists):
            return jnp.where(exists, ref[at].astype(jnp.float32), 0.0)

        row = 0
        for group in message_groups(fields, depths):
            height = sum(depths[f] for f in group)
            value = read(slice(row, row + height))
            begin = 0
            for field in group:
                depth = depths[field]
                to = pl.multiple_of(jnp.where(north, margin + rows, margin - depth), 8)
                for tile in range(refs[0].shape[2] - 1):
                    lanes = slice(tile * LANES, (tile + 1) * LANES)
                    place(refs, early, field, tile, to, value[begin : begin + depth, lanes])
                begin += depth
            row += height
        sides.append((north, read, row))
    return sides


def interior_kernel(
    margin, lat_count, fields_ref, force_ref, lon_x_ref, lon_y_ref, early_x_ref, early_y_ref, *refs
):
    early, rows, cols = fields_ref.shape
    count = early + force_ref.shape[0]
    windows = refs[2].shape[0]
    for field in range(count):
        for tile in range(cols // LANES):
            lanes = slice(tile * LANES, (tile + 1) * LANES)
            own = fields_ref[field, :, lanes] if field < early else force_ref[field - early, :, lanes]
            place(refs, early, field, tile, margin, own)
    lon_x, lon_y = lon_x_ref[...].astype(jnp.float32), lon_y_ref[...].astype(jnp.float32)
    place_sides(refs, early, count, margin, lon_x, lon_y, margin)
    place_rows(refs, early, range(early), margin, rows, lat_count, early_x_ref, early_y_ref)
    for window in range(windows):
        lost = 2 * SUB * window
        row_list = range(margin + lost, margin + rows - lost, GROUP)

        def subcycle(number, carry):
            step = window * SUB + number
            for row in row_list:
                stress_rows(refs, step, window, row)
            for row in row_list:
                velocity_rows(refs, step, window, row)
            return carry

        lax.fori_loop(0, SUB, subcycle, 0)


def rim_kernel(margin, early, count, lat_count, *args):
    lat_x_ref, lat_y_ref = args[:2]
    refs = args[2:8]
    out_hbm = args[8:10]
    stages, sems = args[16:19], args[19]
    windows = refs[2].shape[0]
    _, rows, cols = out_hbm[0].shape
    inner = rows - 2 * margin
    copies = []
    for which in range(2):
        copies += write_rows(refs, out_hbm, stages[2], sems.at[2], margin, margin, inner, which)
    bottom = margin + rows
    packed = -(-count // (LANES // margin)) * LANES
    late = range(early, count)
    for north, read, row in place_rows(
        refs, early, late, margin, rows, lat_count, lat_x_ref, lat_y_ref
    ):
        to = pl.multiple_of(jnp.where(north, bottom, 0), 8)
        east, west = (read(slice(at, at + margin))[:, :packed] for at in (row, row + margin))
        place_sides(refs, early, count, margin, east, west, to)

    def half_step(step, half):
        done = 2 * step + 1 + half
        rows_now = velocity_rows if half else stress_rows
        for first in range(0, margin, GROUP):
            rows_now(refs, step, step // SUB, done + first)
            rows_now(refs, step, step // SUB, bottom - done + first)

    last = SUB * windows - 1
    for step in range(last):
        half_step(step, 0)
        half_step(step, 1)
    half_step(last, 0)
    ends = list(enumerate((0, rows - margin)))
    for number, begin in ends:
        copies += write_rows(refs, out_hbm, stages[number], sems.at[number], margin, begin, margin, 1)
    half_step(last, 1)
    for number, begin in ends:
        copies += write_rows(refs, out_hbm, stages[number], sems.at[number], margin, begin, margin, 0)
    for copy in copies:
        copy.wait()


def params():
    return pltpu.CompilerParams(vmem_limit_bytes=VMEM_LIMIT)


def lon_swaps(first):
    n = lax.axis_size("lon")
    if n % 2:
        raise ValueError("odd ring")
    pairs = [(i, (i + 1) % n) for i in range(first, n, 2)]
    return pairs + [(j, i) for i, j in pairs]


def lat_swaps(first):
    m, n = lax.axis_size("lat"), lax.axis_size("lon")
    partner = {}
    for i in range(m):
        north = i + 1 if (i - first) % 2 == 0 else i - 1
        for k in range(n):
            to = (north, k) if 0 <= north < m else (i, k ^ 1)
            partner[k * m + i] = to[1] * m + to[0]
    return list(partner.items())


def lon_exchange(x, y):
    return lax.ppermute(x, "lon", lon_swaps(0)), lax.ppermute(y, "lon", lon_swaps(1))


def lat_exchange(x, first):
    return lax.ppermute(x, ("lon", "lat"), lat_swaps(first))


def shape(dims, dtype=jnp.float32):
    return jax.ShapeDtypeStruct(dims, dtype)


def local(
    velocity,
    stress,
    thickness,
    concentration,
    land_mask,
    covered,
    ocean_current,
    wind_stress,
    regrid_weights,
    tile_offset,
):
    _, rows, cols = velocity.shape
    windows = wind_stress.shape[0]
    margin = 2 * SUB * windows
    early = STATE + 2 * windows
    count = early + 2 * windows
    tiles = cols // LANES + 1
    packed = -(-count // (LANES // margin)) * LANES
    depths = field_depths(margin, windows)
    early_rows = sum(depths[:early])
    late_rows = sum(depths[early:])
    bf16 = jnp.bfloat16

    tile_x, tile_y = lat_exchange(ocean_current, 0), lat_exchange(ocean_current, 1)

    whole = pl.BlockSpec(memory_space=pltpu.VMEM)
    anywhere = pl.BlockSpec(memory_space=pl.ANY)
    chunks = rows // GROUP
    thick_out, fields, current, side, lon_x, lon_y, lat_x, lat_y = pl.pallas_call(
        functools.partial(local_kernel, margin),
        out_shape=(
            shape(thickness.shape),
            shape((early, rows, cols)),
            shape(wind_stress.shape),
            shape((rows, 2 * rows), bf16),
            shape((rows, packed), bf16),
            shape((rows, packed), bf16),
            shape((early_rows, cols), bf16),
            shape((early_rows, cols), bf16),
        ),
        in_specs=[anywhere] * 10,
        out_specs=(anywhere,) + (whole,) * 7,
        scratch_shapes=[
            pltpu.SMEM(covered.shape, jnp.int32),
            pltpu.VMEM((1, rows), jnp.int32),
            pltpu.VMEM(regrid_weights.shape, bf16),
            pltpu.VMEM(thickness.shape, jnp.float32),
            pltpu.VMEM(thickness.shape, jnp.float32),
            pltpu.VMEM(land_mask.shape, jnp.int32),
            pltpu.VMEM(velocity.shape, jnp.float32),
            pltpu.VMEM(stress.shape, jnp.float32),
            pltpu.VMEM(ocean_current.shape, bf16),
            pltpu.VMEM(wind_stress.shape, bf16),
            pltpu.SemaphoreType.DMA((8,)),
            pltpu.SemaphoreType.DMA((chunks,)),
            pltpu.SemaphoreType.DMA((chunks,)),
            pltpu.SemaphoreType.DMA((chunks,)),
        ],
        compiler_params=params(),
        cost_estimate=pl.CostEstimate(
            flops=100 * thickness.size, bytes_accessed=12 * thickness.size, transcendentals=0
        ),
        name="local",
    )(
        *(
            pltpu.with_memory_space_constraint(x, pltpu.HBM)
            for x in (
                covered,
                tile_offset.reshape(1, rows),
                regrid_weights,
                thickness,
                concentration,
                land_mask,
                velocity,
                stress,
                ocean_current,
                wind_stress,
            )
        )
    )

    early_y = lat_exchange(lat_y, 1)
    current = pl.pallas_call(
        side_kernel,
        out_shape=shape(wind_stress.shape),
        in_specs=[whole] * 3,
        out_specs=whole,
        compiler_params=params(),
        cost_estimate=pl.CostEstimate(flops=1, bytes_accessed=1, transcendentals=0),
        name="side",
    )(side, tile_x, current)
    force, lon_x, lon_y, late_x, late_y, lat_x = pl.pallas_call(
        functools.partial(force_kernel, margin, early),
        out_shape=(
            shape((2 * windows, rows, cols)),
            shape((rows, packed), bf16),
            shape((rows, packed), bf16),
            shape((late_rows, cols), bf16),
            shape((late_rows, cols), bf16),
            shape((early_rows, cols), bf16),
        ),
        in_specs=[whole] * 7,
        out_specs=(whole,) * 6,
        compiler_params=params(),
        cost_estimate=pl.CostEstimate(flops=1, bytes_accessed=1, transcendentals=0),
        name="force",
    )(side, tile_y, current, fields, lon_x, lon_y, lat_x)

    lon_x, lon_y = lon_exchange(lon_x, lon_y)
    early_x = lat_exchange(lat_x, 0)
    message = shape((late_rows + 2 * margin, cols), bf16)
    late_x, late_y = pl.pallas_call(
        functools.partial(corner_kernel, margin, rows),
        out_shape=(message, message),
        in_specs=[whole] * 5,
        out_specs=(whole,) * 2,
        compiler_params=params(),
        cost_estimate=pl.CostEstimate(flops=1, bytes_accessed=1, transcendentals=0),
        name="corner",
    )(late_x, late_y, lon_x, lon_y, early_y)
    late_x, late_y = lat_exchange(late_x, 0), lat_exchange(late_y, 1)

    steps = SUB * windows

    def widened(*lead):
        return shape((*lead, tiles, rows + 2 * margin, LANES))

    domain = (
        widened(steps + 1, 2),
        widened(steps + 1, 3),
        widened(windows),
        widened(windows),
        widened(windows),
        widened(windows, 2),
    )
    outs = (shape(velocity.shape), shape(stress.shape))
    refs = pl.pallas_call(
        functools.partial(interior_kernel, margin, lax.axis_size("lat")),
        out_shape=domain,
        in_specs=[whole] * 6,
        out_specs=(whole,) * 6,
        compiler_params=params(),
        cost_estimate=pl.CostEstimate(
            flops=60 * steps * rows * cols, bytes_accessed=2**22, transcendentals=0
        ),
        name="interior",
    )(fields, force, lon_x, lon_y, early_x, early_y)

    velocity_out, stress_out = pl.pallas_call(
        functools.partial(rim_kernel, margin, early, count, lax.axis_size("lat")),
        out_shape=(shape(velocity.shape), shape(stress.shape)) + domain,
        in_specs=[whole] * 8,
        out_specs=(anywhere,) * 2 + (whole,) * 6,
        input_output_aliases={2 + i: 2 + i for i in range(6)},
        scratch_shapes=[
            pltpu.VMEM((STATE, margin, cols), jnp.float32),
            pltpu.VMEM((STATE, margin, cols), jnp.float32),
            pltpu.VMEM((STATE, rows - 2 * margin, cols), jnp.float32),
            pltpu.SemaphoreType.DMA((3, 2)),
        ],
        compiler_params=params(),
        name="rim",
    )(late_x, late_y, *refs)[:2]
    return (velocity_out, stress_out, thick_out)


def solution(mesh):
    return jax.shard_map(
        local,
        mesh=mesh,
        in_specs=(
            P(None, "lat", "lon"),
            P(None, "lat", "lon"),
            P(None, "lat", "lon"),
            P(None, "lat", "lon"),
            P("lat", "lon"),
            P("lat", None),
            P(None, None, "lat", "lon"),
            P(None, None, "lat", "lon"),
            P("lat", None),
            P("lat"),
        ),
        out_specs=(P(None, "lat", "lon"), P(None, "lat", "lon"), P(None, "lat", "lon")),
        check_vma=False,
    )
```

```python
import functools

import jax
import jax.numpy as jnp
from jax import lax
from jax.experimental import pallas as pl
from jax.experimental.pallas import tpu as pltpu
from jax.sharding import PartitionSpec as P

BLK = 128
SUB = 4
LANES = 128
GROUP = 16
STATE = 5
VMEM_LIMIT = 16 * 1024 * 1024

growth_rate = 0.3
mixing_rate = 0.3


def total(terms):
    result = terms[0]
    for term in terms[1:]:
        result = result + term
    return result


def field_depths(margin, windows):
    depths = [margin] * STATE
    for copies in (2, 2):
        for window in range(windows):
            depths += [margin - 2 * SUB * window] * copies
    return depths


def message_groups(fields, depths):
    groups, held = [], []
    for field in fields:
        held.append(field)
        if sum(depths[f] for f in held) % GROUP == 0:
            groups.append(held)
            held = []
    return groups + ([held] if held else [])


def even(axis):
    return lax.axis_index(axis) % 2 == 0


def pack_rows(message_ref, row, groups, depths, value_of, northward, rows):
    for group in groups:
        parts = []
        for field in group:
            start = jnp.where(northward, rows - depths[field], 0)
            parts.append(value_of(field, pl.ds(pl.multiple_of(start, 8), depths[field])))
        value = parts[0] if len(parts) == 1 else jnp.concatenate(parts, axis=0)
        message_ref[row : row + value.shape[0]] = value.astype(jnp.bfloat16)
        row += value.shape[0]
    return row


def local_kernel(
    margin,
    covered_hbm,
    offset_hbm,
    weights_hbm,
    thick_hbm,
    conc_hbm,
    mask_hbm,
    velocity_hbm,
    stress_hbm,
    ocean_hbm,
    wind_hbm,
    thick_out_hbm,
    fields_ref,
    current_ref,
    side_ref,
    lon_x_ref,
    lon_y_ref,
    lat_x_ref,
    lat_y_ref,
    covered,
    offset,
    weights,
    thick,
    conc,
    mask_in,
    velocity,
    stress,
    ocean,
    wind,
    in_sems,
    thick_sems,
    conc_sems,
    out_sems,
):
    cats, rows, cols = thick.shape
    windows = wind.shape[0]
    step = GROUP
    chunks = rows // step

    def rows_of(chunk):
        return pl.ds(chunk * step, step)

    small = [
        pltpu.make_async_copy(source, target, in_sems.at[i])
        for i, (source, target) in enumerate(
            (
                (covered_hbm, covered),
                (mask_hbm, mask_in),
                (velocity_hbm, velocity),
                (stress_hbm, stress),
                (ocean_hbm, ocean),
                (wind_hbm, wind),
                (weights_hbm, weights),
                (offset_hbm, offset),
            )
        )
    ]
    pairs = [
        [
            pltpu.make_async_copy(hbm.at[:, rows_of(c)], vmem.at[:, rows_of(c)], sems.at[c])
            for hbm, vmem, sems in ((thick_hbm, thick, thick_sems), (conc_hbm, conc, conc_sems))
        ]
        for c in range(chunks)
    ]
    writes = [
        pltpu.make_async_copy(thick.at[:, rows_of(c)], thick_out_hbm.at[:, rows_of(c)], out_sems.at[c])
        for c in range(chunks)
    ]
    for copy in small[:2] + [copy for pair in pairs for copy in pair] + small[2:]:
        copy.start()

    blocks = cols // BLK
    first = lax.axis_index("lon") * blocks
    small[0].wait()
    live = [covered[0, first + block] > 0 for block in range(blocks)]
    small[1].wait()
    for c in range(chunks):
        at = slice(c * step, (c + 1) * step)
        for copy in pairs[c]:
            copy.wait()
        for block in range(blocks):
            lanes = slice(block * BLK, (block + 1) * BLK)
            part = [conc[k, at, lanes] for k in range(cats)]
            height = [thick[k, at, lanes] for k in range(cats)]
            mask = mask_in[at, lanes].astype(jnp.float32)
            area = total(part)
            inverse = 1.0 / area
            factor = jnp.exp(-2.0 * (1.0 - area)) * (mask * (1.0 / 3.0))
            half = 0.5 * mask
            volume = total([a * h for a, h in zip(part, height)])
            for window in range(windows):
                mean = volume * inverse
                grown = [h + growth_rate / (0.5 + h) + mixing_rate * (mean - h) for h in height]
                height = [jnp.where(live[block], g, h) for g, h in zip(grown, height)]
                volume = total([a * h for a, h in zip(part, height)])
                fields_ref[STATE + 2 * window, at, lanes] = volume * factor
                fields_ref[STATE + 2 * window + 1, at, lanes] = half / (volume + 1.0)
            for k in range(cats):
                thick[k, at, lanes] = height[k]
        writes[c].start()

    small[2].wait()
    small[3].wait()
    for row in range(0, rows, step):
        at = slice(row, row + step)
        mask = mask_in[at].astype(jnp.float32)
        fields_ref[0, at] = velocity[0, at]
        fields_ref[1, at] = velocity[1, at]
        fields_ref[2, at] = (stress[0, at] + stress[1, at]) * mask
        fields_ref[3, at] = (stress[0, at] - stress[1, at]) * mask
        fields_ref[4, at] = (stress[2, at] + stress[2, at]) * mask

    count = fields_ref.shape[0]
    per = LANES // margin
    slot_of_lane = lax.broadcasted_iota(jnp.int32, (rows, LANES), 1) // margin
    eastward = even("lon")
    for group in range(lon_x_ref.shape[1] // LANES):
        east = jnp.zeros((rows, LANES), jnp.float32)
        west = jnp.zeros((rows, LANES), jnp.float32)
        for slot in range(min(per, count - group * per)):
            field = group * per + slot
            east, west = add_slot(
                east, west, fields_ref.at[field], slot_of_lane == slot, slot * margin, margin
            )
        store_sides(lon_x_ref, lon_y_ref, group, east, west, eastward)
    depths = field_depths(margin, windows)
    groups = message_groups(range(count), depths)
    northward = even("lat")

    def value_of(field, at):
        return fields_ref[field, at, :]

    pack_rows(lat_x_ref, 0, groups, depths, value_of, northward, rows)
    pack_rows(lat_y_ref, 0, groups, depths, value_of, jnp.logical_not(northward), rows)

    for copy in small[4:]:
        copy.wait()
    own_weights = weights[:, :rows]
    for w in range(windows):
        for k in range(2):
            current_ref[w, k] = wind[w, k].astype(jnp.float32) + jnp.dot(
                own_weights, ocean[w, k], preferred_element_type=jnp.float32
            )
    square = (rows, rows)
    diagonal = lax.broadcasted_iota(jnp.int32, square, 0) == lax.broadcasted_iota(
        jnp.int32, square, 1
    )
    up = offset[...] > 0
    for number, north in enumerate((northward, jnp.logical_not(northward))):
        wanted = jnp.where(north, up.astype(jnp.int32), 1 - up.astype(jnp.int32)) > 0
        pick = jnp.where(diagonal & wanted, 1.0, 0.0).astype(jnp.bfloat16)
        side_ref[:, number * rows : (number + 1) * rows] = jnp.dot(
            pick, weights[:, rows:], preferred_element_type=jnp.float32
        ).astype(jnp.bfloat16)

    for copy in writes:
        copy.wait()


def add_slot(east, west, field_ref, here, shift, margin):
    cols = field_ref.shape[1]
    last = pltpu.roll(field_ref[:, cols - LANES :], (shift + margin) % LANES, 1)
    leading = field_ref[:, :LANES]
    if shift:
        leading = pltpu.roll(leading, shift, 1)
    return jnp.where(here, last, east), jnp.where(here, leading, west)


def store_sides(x_ref, y_ref, group, east, west, eastward):
    lanes = slice(group * LANES, (group + 1) * LANES)
    x_ref[:, lanes] = jnp.where(eastward, east, west).astype(jnp.bfloat16)
    y_ref[:, lanes] = jnp.where(eastward, west, east).astype(jnp.bfloat16)


def side_kernel(side_ref, tile_ref, current_ref, sum_ref):
    windows, parts, rows, _ = current_ref.shape
    weights = side_ref[:, :rows]
    for w in range(windows):
        for k in range(parts):
            sum_ref[w, k] = current_ref[w, k] + jnp.dot(
                weights, tile_ref[w, k], preferred_element_type=jnp.float32
            )


def force_kernel(
    margin,
    early,
    side_ref,
    tile_ref,
    current_ref,
    fields_ref,
    lon_x_in,
    lon_y_in,
    early_x_in,
    force_ref,
    lon_x_ref,
    lon_y_ref,
    lat_x_ref,
    lat_y_ref,
    early_x_ref,
):
    windows, _, rows, cols = current_ref.shape
    weights = side_ref[:, rows:]
    for w in range(windows):
        b = fields_ref[STATE + 2 * w + 1]
        for k in range(2):
            current = jnp.dot(weights, tile_ref[w, k], preferred_element_type=jnp.float32)
            force_ref[2 * w + k] = b * (current_ref[w, k] + current)

    per = LANES // margin
    count = early + force_ref.shape[0]
    slot_of_lane = lax.broadcasted_iota(jnp.int32, (rows, LANES), 1) // margin
    eastward = even("lon")
    for group in range(lon_x_ref.shape[1] // LANES):
        lanes = slice(group * LANES, (group + 1) * LANES)
        x = lon_x_in[:, lanes].astype(jnp.float32)
        y = lon_y_in[:, lanes].astype(jnp.float32)
        east, west = jnp.where(eastward, x, y), jnp.where(eastward, y, x)
        for field in range(max(early, group * per), min(count, (group + 1) * per)):
            slot = field - group * per
            east, west = add_slot(
                east, west, force_ref.at[field - early], slot_of_lane == slot, slot * margin, margin
            )
        store_sides(lon_x_ref, lon_y_ref, group, east, west, eastward)

    depths = field_depths(margin, windows)
    groups = message_groups(range(early, count), depths)
    northward = even("lat")

    def value_of(field, at):
        return force_ref[field - early, at, :]

    for ref, north in ((lat_x_ref, northward), (lat_y_ref, jnp.logical_not(northward))):
        pack_rows(ref, 0, groups, depths, value_of, north, rows)
    early_x_ref[...] = early_x_in[...]


def corner_kernel(
    margin, rows, lat_x_in, lat_y_in, lon_x_ref, lon_y_ref, early_y_ref, lat_x_ref, lat_y_ref
):
    for old_ref, ref, north in (
        (lat_x_in, lat_x_ref, even("lat")),
        (lat_y_in, lat_y_ref, jnp.logical_not(even("lat"))),
    ):
        row, cols = old_ref.shape
        ref[:row] = old_ref[...]
        start = pl.multiple_of(jnp.where(north, rows - margin, 0), GROUP)
        for lon_ref in (lon_x_ref, lon_y_ref):
            packed = lon_ref.shape[1]
            ref[row : row + margin, :packed] = lon_ref[pl.ds(start, margin), :]
            if packed < cols:
                ref[row : row + margin, packed:] = jnp.zeros((margin, cols - packed), ref.dtype)
            row += margin


def place(refs, early, field, tile, row, value):
    velocity, stress, strength, keep, push, force = refs
    at = pl.ds(row, value.shape[0])
    if field < 2:
        velocity[0, field, tile, at, :] = value
    elif field < STATE:
        stress[0, field - 2, tile, at, :] = value
    elif field >= early:
        window, kind = divmod(field - early, 2)
        force[window, kind, tile, at, :] = value
    else:
        window, kind = divmod(field - STATE, 2)
        if kind == 0:
            strength[window, tile, at, :] = value
        else:
            push[window, tile, at, :] = value * 0.25
            keep[window, tile, at, :] = jnp.where(value > 0.0, 1.0 - value, 0.0)


def place_sides(refs, early, count, margin, x, y, row):
    last = refs[0].shape[2] - 1
    per = LANES // margin
    wide = lax.broadcasted_iota(jnp.int32, (x.shape[0], LANES), 1)
    from_x_is_east = even("lon")
    for group in range(x.shape[1] // LANES):
        lanes = slice(group * LANES, (group + 1) * LANES)
        x_now, y_now = x[:, lanes], y[:, lanes]
        east = jnp.where(from_x_is_east, x_now, y_now)
        west = jnp.where(from_x_is_east, y_now, x_now)
        for slot in range(min(per, count - group * per)):
            shift = slot * margin
            back = (LANES - margin - shift) % LANES
            e = pltpu.roll(east, LANES - shift, 1) if shift else east
            w = pltpu.roll(west, back, 1) if back else west
            value = jnp.where(wide < margin, e, jnp.where(wide >= LANES - margin, w, 0.0))
            place(refs, early, group * per + slot, last, row, value)


def across(values):
    tiles = len(values)
    lane = lax.broadcasted_iota(jnp.int32, values[0].shape, 1)
    ahead = [pltpu.roll(x, LANES - 1, 1) for x in values]
    behind = [pltpu.roll(x, 1, 1) for x in values]
    return [
        jnp.where(lane == LANES - 1, ahead[(j + 1) % tiles], ahead[j])
        - jnp.where(lane == 0, behind[j - 1], behind[j])
        for j in range(tiles)
    ]


def stress_rows(refs, step, window, row, height=GROUP):
    velocity, stress, strength, _, _, _ = refs
    every = range(velocity.shape[2])
    at, north, south = (pl.ds(row + shift, height) for shift in (0, 1, -1))
    u_x = across([velocity[step, 0, j, at, :] for j in every])
    v_x = across([velocity[step, 1, j, at, :] for j in every])
    for j in every:
        u_y = velocity[step, 0, j, north, :] - velocity[step, 0, j, south, :]
        v_y = velocity[step, 1, j, north, :] - velocity[step, 1, j, south, :]
        shear = u_y + v_x[j]
        spread = u_x[j] + v_y
        tension = u_x[j] - v_y
        tension4 = tension * 0.25
        shear4 = shear * 0.25
        squares = spread * spread + tension * tension4 + (shear * shear4 + 1.0)
        k = strength[window, j, at, :]
        kr = k * lax.rsqrt(squares)
        old = [stress[step, i, j, at, :] * (2.0 / 3.0) for i in range(3)]
        stress[step + 1, 0, j, at, :] = old[0] + (kr * (spread + tension4) - k)
        stress[step + 1, 1, j, at, :] = old[1] + (kr * (spread - tension4) - k)
        stress[step + 1, 2, j, at, :] = old[2] + kr * shear4


def velocity_rows(refs, step, window, row, height=GROUP):
    velocity, stress, _, keep, push, force = refs
    every = range(velocity.shape[2])
    at, north, south = (pl.ds(row + shift, height) for shift in (0, 1, -1))
    now = step + 1
    p_x = across([stress[now, 0, j, at, :] for j in every])
    t_x = across([stress[now, 2, j, at, :] for j in every])
    for j in every:
        q_y = stress[now, 1, j, north, :] - stress[now, 1, j, south, :]
        t_y = stress[now, 2, j, north, :] - stress[now, 2, j, south, :]
        a = keep[window, j, at, :]
        b = push[window, j, at, :]
        velocity[now, 0, j, at, :] = (
            a * velocity[step, 0, j, at, :] + b * (p_x[j] + t_y) + force[window, 0, j, at, :]
        )
        velocity[now, 1, j, at, :] = (
            a * velocity[step, 1, j, at, :] + b * (t_x[j] + q_y) + force[window, 1, j, at, :]
        )


def write_rows(refs, out_hbm, stage, sem, margin, begin, height, which):
    values = refs[which]
    last = values.shape[0] - 1
    first = 2 * which
    for tile in range(stage.shape[2] // LANES):
        lanes = slice(tile * LANES, (tile + 1) * LANES)
        for row in range(0, height, 8):
            to = slice(row, row + 8)
            at = slice(margin + begin + row, margin + begin + row + 8)
            now = [values[last, i, tile, at, :] for i in range(values.shape[1])]
            if which:
                now = [(now[0] + now[1]) * 0.5, (now[0] - now[1]) * 0.5, now[2] * 0.5]
            for i, value in enumerate(now):
                stage[first + i, to, lanes] = value
    copy = pltpu.make_async_copy(
        stage.at[first : first + values.shape[1]],
        out_hbm[which].at[:, pl.ds(begin, height)],
        sem.at[which],
    )
    copy.start()
    return [copy]


def place_rows(refs, early, fields, margin, rows, lat_count, x_ref, y_ref):
    depths = field_depths(margin, refs[2].shape[0])
    me = lax.axis_index("lat")
    sides = []
    for ref, north in ((x_ref, even("lat")), (y_ref, jnp.logical_not(even("lat")))):
        exists = jnp.where(north, me < lat_count - 1, me > 0)

        def read(at, ref=ref, exists=exists):
            return jnp.where(exists, ref[at].astype(jnp.float32), 0.0)

        row = 0
        for group in message_groups(fields, depths):
            height = sum(depths[f] for f in group)
            value = read(slice(row, row + height))
            begin = 0
            for field in group:
                depth = depths[field]
                to = pl.multiple_of(jnp.where(north, margin + rows, margin - depth), 8)
                for tile in range(refs[0].shape[2] - 1):
                    lanes = slice(tile * LANES, (tile + 1) * LANES)
                    place(refs, early, field, tile, to, value[begin : begin + depth, lanes])
                begin += depth
            row += height
        sides.append((north, read, row))
    return sides


def interior_kernel(
    margin, lat_count, fields_ref, force_ref, lon_x_ref, lon_y_ref, early_x_ref, early_y_ref, *refs
):
    early, rows, cols = fields_ref.shape
    count = early + force_ref.shape[0]
    windows = refs[2].shape[0]
    for field in range(count):
        for tile in range(cols // LANES):
            lanes = slice(tile * LANES, (tile + 1) * LANES)
            own = fields_ref[field, :, lanes] if field < early else force_ref[field - early, :, lanes]
            place(refs, early, field, tile, margin, own)
    lon_x, lon_y = lon_x_ref[...].astype(jnp.float32), lon_y_ref[...].astype(jnp.float32)
    place_sides(refs, early, count, margin, lon_x, lon_y, margin)
    place_rows(refs, early, range(early), margin, rows, lat_count, early_x_ref, early_y_ref)
    for window in range(windows):
        lost = 2 * SUB * window
        row_list = range(margin + lost, margin + rows - lost, 8)

        def subcycle(number, carry):
            step = window * SUB + number
            for row in row_list:
                stress_rows(refs, step, window, row, 8)
            for row in row_list:
                velocity_rows(refs, step, window, row, 8)
            return carry

        lax.fori_loop(0, SUB, subcycle, 0)


def rim_kernel(margin, early, count, lat_count, *args):
    lat_x_ref, lat_y_ref = args[:2]
    refs = args[2:8]
    out_hbm = args[8:10]
    stages, sems = args[16:19], args[19]
    windows = refs[2].shape[0]
    _, rows, cols = out_hbm[0].shape
    inner = rows - 2 * margin
    copies = []
    for which in range(2):
        copies += write_rows(refs, out_hbm, stages[2], sems.at[2], margin, margin, inner, which)
    bottom = margin + rows
    packed = -(-count // (LANES // margin)) * LANES
    late = range(early, count)
    for north, read, row in place_rows(
        refs, early, late, margin, rows, lat_count, lat_x_ref, lat_y_ref
    ):
        to = pl.multiple_of(jnp.where(north, bottom, 0), 8)
        east, west = (read(slice(at, at + margin))[:, :packed] for at in (row, row + margin))
        place_sides(refs, early, count, margin, east, west, to)

    def half_step(step, half):
        done = 2 * step + 1 + half
        rows_now = velocity_rows if half else stress_rows
        for first in range(0, margin, GROUP):
            rows_now(refs, step, step // SUB, done + first)
            rows_now(refs, step, step // SUB, bottom - done + first)

    last = SUB * windows - 1
    for step in range(last):
        half_step(step, 0)
        half_step(step, 1)
    half_step(last, 0)
    ends = list(enumerate((0, rows - margin)))
    for number, begin in ends:
        copies += write_rows(refs, out_hbm, stages[number], sems.at[number], margin, begin, margin, 1)
    half_step(last, 1)
    for number, begin in ends:
        copies += write_rows(refs, out_hbm, stages[number], sems.at[number], margin, begin, margin, 0)
    for copy in copies:
        copy.wait()


def params():
    return pltpu.CompilerParams(vmem_limit_bytes=VMEM_LIMIT)


def lon_swaps(first):
    n = lax.axis_size("lon")
    if n % 2:
        raise ValueError("odd ring")
    pairs = [(i, (i + 1) % n) for i in range(first, n, 2)]
    return pairs + [(j, i) for i, j in pairs]


def lat_swaps(first):
    m, n = lax.axis_size("lat"), lax.axis_size("lon")
    partner = {}
    for i in range(m):
        north = i + 1 if (i - first) % 2 == 0 else i - 1
        for k in range(n):
            to = (north, k) if 0 <= north < m else (i, k ^ 1)
            partner[k * m + i] = to[1] * m + to[0]
    return list(partner.items())


def lon_exchange(x, y):
    return lax.ppermute(x, "lon", lon_swaps(0)), lax.ppermute(y, "lon", lon_swaps(1))


def lat_exchange(x, first):
    return lax.ppermute(x, ("lon", "lat"), lat_swaps(first))


def shape(dims, dtype=jnp.float32):
    return jax.ShapeDtypeStruct(dims, dtype)


def local(
    velocity,
    stress,
    thickness,
    concentration,
    land_mask,
    covered,
    ocean_current,
    wind_stress,
    regrid_weights,
    tile_offset,
):
    _, rows, cols = velocity.shape
    windows = wind_stress.shape[0]
    margin = 2 * SUB * windows
    early = STATE + 2 * windows
    count = early + 2 * windows
    tiles = cols // LANES + 1
    packed = -(-count // (LANES // margin)) * LANES
    depths = field_depths(margin, windows)
    early_rows = sum(depths[:early])
    late_rows = sum(depths[early:])
    bf16 = jnp.bfloat16

    tile_x, tile_y = lat_exchange(ocean_current, 0), lat_exchange(ocean_current, 1)

    whole = pl.BlockSpec(memory_space=pltpu.VMEM)
    anywhere = pl.BlockSpec(memory_space=pl.ANY)
    chunks = rows // GROUP
    thick_out, fields, current, side, lon_x, lon_y, lat_x, lat_y = pl.pallas_call(
        functools.partial(local_kernel, margin),
        out_shape=(
            shape(thickness.shape),
            shape((early, rows, cols)),
            shape(wind_stress.shape),
            shape((rows, 2 * rows), bf16),
            shape((rows, packed), bf16),
            shape((rows, packed), bf16),
            shape((early_rows, cols), bf16),
            shape((early_rows, cols), bf16),
        ),
        in_specs=[anywhere] * 10,
        out_specs=(anywhere,) + (whole,) * 7,
        scratch_shapes=[
            pltpu.SMEM(covered.shape, jnp.int32),
            pltpu.VMEM((1, rows), jnp.int32),
            pltpu.VMEM(regrid_weights.shape, bf16),
            pltpu.VMEM(thickness.shape, jnp.float32),
            pltpu.VMEM(thickness.shape, jnp.float32),
            pltpu.VMEM(land_mask.shape, jnp.int32),
            pltpu.VMEM(velocity.shape, jnp.float32),
            pltpu.VMEM(stress.shape, jnp.float32),
            pltpu.VMEM(ocean_current.shape, bf16),
            pltpu.VMEM(wind_stress.shape, bf16),
            pltpu.SemaphoreType.DMA((8,)),
            pltpu.SemaphoreType.DMA((chunks,)),
            pltpu.SemaphoreType.DMA((chunks,)),
            pltpu.SemaphoreType.DMA((chunks,)),
        ],
        compiler_params=params(),
        cost_estimate=pl.CostEstimate(
            flops=100 * thickness.size, bytes_accessed=12 * thickness.size, transcendentals=0
        ),
        name="local",
    )(
        *(
            pltpu.with_memory_space_constraint(x, pltpu.HBM)
            for x in (
                covered,
                tile_offset.reshape(1, rows),
                regrid_weights,
                thickness,
                concentration,
                land_mask,
                velocity,
                stress,
                ocean_current,
                wind_stress,
            )
        )
    )

    early_y = lat_exchange(lat_y, 1)
    current = pl.pallas_call(
        side_kernel,
        out_shape=shape(wind_stress.shape),
        in_specs=[whole] * 3,
        out_specs=whole,
        compiler_params=params(),
        cost_estimate=pl.CostEstimate(flops=1, bytes_accessed=1, transcendentals=0),
        name="side",
    )(side, tile_x, current)
    force, lon_x, lon_y, late_x, late_y, lat_x = pl.pallas_call(
        functools.partial(force_kernel, margin, early),
        out_shape=(
            shape((2 * windows, rows, cols)),
            shape((rows, packed), bf16),
            shape((rows, packed), bf16),
            shape((late_rows, cols), bf16),
            shape((late_rows, cols), bf16),
            shape((early_rows, cols), bf16),
        ),
        in_specs=[whole] * 7,
        out_specs=(whole,) * 6,
        compiler_params=params(),
        cost_estimate=pl.CostEstimate(flops=1, bytes_accessed=1, transcendentals=0),
        name="force",
    )(side, tile_y, current, fields, lon_x, lon_y, lat_x)

    lon_x, lon_y = lon_exchange(lon_x, lon_y)
    early_x = lat_exchange(lat_x, 0)
    message = shape((late_rows + 2 * margin, cols), bf16)
    late_x, late_y = pl.pallas_call(
        functools.partial(corner_kernel, margin, rows),
        out_shape=(message, message),
        in_specs=[whole] * 5,
        out_specs=(whole,) * 2,
        compiler_params=params(),
        cost_estimate=pl.CostEstimate(flops=1, bytes_accessed=1, transcendentals=0),
        name="corner",
    )(late_x, late_y, lon_x, lon_y, early_y)
    late_x, late_y = lat_exchange(late_x, 0), lat_exchange(late_y, 1)

    steps = SUB * windows

    def widened(*lead):
        return shape((*lead, tiles, rows + 2 * margin, LANES))

    domain = (
        widened(steps + 1, 2),
        widened(steps + 1, 3),
        widened(windows),
        widened(windows),
        widened(windows),
        widened(windows, 2),
    )
    outs = (shape(velocity.shape), shape(stress.shape))
    refs = pl.pallas_call(
        functools.partial(interior_kernel, margin, lax.axis_size("lat")),
        out_shape=domain,
        in_specs=[whole] * 6,
        out_specs=(whole,) * 6,
        compiler_params=params(),
        cost_estimate=pl.CostEstimate(
            flops=60 * steps * rows * cols, bytes_accessed=2**22, transcendentals=0
        ),
        name="interior",
    )(fields, force, lon_x, lon_y, early_x, early_y)

    velocity_out, stress_out = pl.pallas_call(
        functools.partial(rim_kernel, margin, early, count, lax.axis_size("lat")),
        out_shape=(shape(velocity.shape), shape(stress.shape)) + domain,
        in_specs=[whole] * 8,
        out_specs=(anywhere,) * 2 + (whole,) * 6,
        input_output_aliases={2 + i: 2 + i for i in range(6)},
        scratch_shapes=[
            pltpu.VMEM((STATE, margin, cols), jnp.float32),
            pltpu.VMEM((STATE, margin, cols), jnp.float32),
            pltpu.VMEM((STATE, rows - 2 * margin, cols), jnp.float32),
            pltpu.SemaphoreType.DMA((3, 2)),
        ],
        compiler_params=params(),
        name="rim",
    )(late_x, late_y, *refs)[:2]
    return (velocity_out, stress_out, thick_out)


def solution(mesh):
    return jax.shard_map(
        local,
        mesh=mesh,
        in_specs=(
            P(None, "lat", "lon"),
            P(None, "lat", "lon"),
            P(None, "lat", "lon"),
            P(None, "lat", "lon"),
            P("lat", "lon"),
            P("lat", None),
            P(None, None, "lat", "lon"),
            P(None, None, "lat", "lon"),
            P("lat", None),
            P("lat"),
        ),
        out_specs=(P(None, "lat", "lon"), P(None, "lat", "lon"), P(None, "lat", "lon")),
        check_vma=False,
    )
```
